512 devices in a mesh: tm: 16 (over z_lo, core), space: 32 (over x, y, z_hi).
Axes of the slice: x: 4, y: 4, z: 16 (z_hi: 2, z_lo: 8; z = z_hi * 8 + z_lo), core: 2. Of those that a mesh axis runs over, the one named last changes fastest.
Arguments:
- slab_queue: bfloat16 [2, 16, 512, 3072], P(None, 'tm', 'space'), may hold values from -6 to 6
- levels: int32 [2, 16], replicated, may hold values from 0 to 47, as said below
- mod_table: bfloat16 [48, 3, 3072], replicated, may hold values from -3 to 3
- w_qkv: bfloat16 [3072, 16, 384], P(None, 'tm'), may hold values from -0.109375 to 0.109375
- q_gain: float32 [16, 128], P('tm'), may hold values from 0.5 to 12
- k_gain: float32 [16, 128], P('tm'), may hold values from 0.5 to 12
- w_out: bfloat16 [2048, 3072], P('tm'), may hold values from -0.125 to 0.125
Outputs:
- advanced: bfloat16 [2, 16, 512, 3072], P(None, 'tm', 'space')
The draws below stay inside these ranges and needn't reach their ends.
Inputs may be any that keep to these rules, and one draw needn't show every extreme that they name: `levels`: the level of slab s lies from s * 3 up to, not including, (s + 1) * 3.
All inputs are finite; a program needn't handle non-finite values.
Results may differ from the reference program's by a relative error of at most 0.015.
Values may be sent and summed in bfloat16 or wider, within the bound.
A program may use at most 64 MiB of HBM per device.

```python
import math
import jax
import jax.numpy as jnp
from jax import lax

D = 3072
HEADS = 16
HEAD_DIM = 128
LEVELS = 48
BATCH = 2
SLABS = 16
SLAB_TOK = 512
N_TM = 16


def spread_gains(key, head_low, head_high, chan_low, chan_high):
    head_key, chan_key = jax.random.split(key)
    head_factor = jnp.exp(jax.random.uniform(head_key, (HEADS, 1), jnp.float32, math.log(head_low), math.log(head_high)))
    chan_factor = jnp.exp(jax.random.uniform(chan_key, (HEADS, HEAD_DIM), jnp.float32, math.log(chan_low), math.log(chan_high)))
    return head_factor * chan_factor


def sampled_gain(key):
    return spread_gains(key, 1.0, 3.0, 0.5, 2.0)


def draw_q_gain(key, part):
    key = jax.random.fold_in(key, 11)
    return sampled_gain(key)


def draw_k_gain(key, part):
    key = jax.random.fold_in(key, 23)
    return sampled_gain(key)


def draw_levels(key, part):
    key = jax.random.fold_in(key, 5)
    position = jnp.arange(SLABS, dtype=jnp.int32)[None, :]
    lowest = position * LEVELS // SLABS
    highest = (position + 1) * LEVELS // SLABS
    offsets = jax.random.randint(key, (BATCH, SLABS), 0, highest - lowest, jnp.int32)
    return (lowest + offsets).astype(jnp.int32)


def level_of(own_key, shape, cuts, smallest, high):
    factor_of = 1.0
    for axis_at, blocks in cuts:
        steps = jax.random.uniform(jax.random.fold_in(jax.random.fold_in(own_key, 6), axis_at), (blocks,), jnp.float32, smallest / len(cuts), high / len(cuts))
        factor_of = factor_of * jnp.repeat(jnp.exp(steps), shape[axis_at] // blocks).reshape((-1,) + (1,) * (len(shape) - 1 - axis_at))
    return factor_of


def scatter_about(own_key, extent, deviation, most, shards=(), kind=jnp.bfloat16):
    gain = level_of(own_key, extent, shards, -0.22, 0.18) if shards else 1.0
    result = jax.random.normal(own_key, extent, jnp.float32) * deviation * gain
    return jnp.minimum(jnp.maximum(result, -most), most).astype(kind)


def setup_inputs(seed: int = 0) -> dict:
    key_of = jax.random.split(jax.random.key(seed), 8)
    slab_queue = scatter_about(key_of[0], (BATCH, SLABS, SLAB_TOK, D), 1.0, 6.0, ((1, 16), (2, 32)))
    levels = draw_levels(jax.random.fold_in(key_of[7], 71), 0)
    mod_table = scatter_about(key_of[2], (LEVELS, 3, D), 0.5, 3.0)
    w_qkv = scatter_about(key_of[3], (D, HEADS, 3 * HEAD_DIM), D ** -0.5, 0.109375, ((1, 16),))
    q_gain = draw_q_gain(jax.random.fold_in(key_of[7], 71), 0)
    k_gain = draw_k_gain(jax.random.fold_in(key_of[7], 71), 0)
    w_out = scatter_about(key_of[6], (HEADS * HEAD_DIM, D), (HEADS * HEAD_DIM) ** -0.5, 0.125, ((0, 16),))
    return {"slab_queue": slab_queue, "levels": levels, "mod_table": mod_table, "w_qkv": w_qkv, "q_gain": q_gain, "k_gain": k_gain, "w_out": w_out}


def layer_modulate(slab_queue, shift_rows, scale_rows):
    values = slab_queue.astype(jnp.float32)
    centre = lax.optimization_barrier(jnp.mean(values, axis=-1, keepdims=True))
    spread = lax.optimization_barrier(jnp.mean(jnp.square(values - centre), axis=-1, keepdims=True))
    normed = (values - centre) * lax.rsqrt(spread + 1e-06)
    return (normed * (1.0 + scale_rows) + shift_rows).astype(jnp.bfloat16)

def head_norm(values, gain_per_row):
    float_values = values.astype(jnp.float32)
    factor = lax.rsqrt(lax.optimization_barrier(jnp.mean(jnp.square(float_values), axis=-1, keepdims=True)) + 1e-06)
    return (float_values * factor * gain_per_row[:, None, :]).astype(jnp.bfloat16)

def spatial_head(operands):
    query_head, key_head, value_head = operands
    scores = jnp.einsum('bsnc,bsmc->bsnm', query_head.astype(jnp.float32), key_head.astype(jnp.float32)) * HEAD_DIM ** (-0.5)
    row_max = lax.optimization_barrier(jnp.max(scores, axis=-1, keepdims=True))
    weights = jnp.exp(scores - row_max)
    row_total = lax.optimization_barrier(jnp.sum(weights, axis=-1, keepdims=True))
    rounded = lax.optimization_barrier(weights.astype(jnp.bfloat16)).astype(jnp.float32)
    return jnp.einsum('bsnm,bsmc->bsnc', rounded, value_head.astype(jnp.float32)) / row_total

def reference(slab_queue, levels, mod_table, w_qkv, q_gain, k_gain, w_out):
    level_rows = mod_table.astype(jnp.float32)[levels]
    shift_rows = level_rows[:, :, 0][:, :, None, :]
    scale_rows = level_rows[:, :, 1][:, :, None, :]
    gate_per_row = level_rows[:, :, 2][:, :, None, :]
    modulated = layer_modulate(slab_queue, shift_rows, scale_rows)
    flat_rows = modulated.reshape(-1, D).astype(jnp.float32)
    projected = jnp.dot(flat_rows, w_qkv.reshape(D, HEADS * 3 * HEAD_DIM).astype(jnp.float32))
    projected = projected.reshape(BATCH, SLABS, SLAB_TOK, HEADS, 3 * HEAD_DIM)
    projected = jnp.transpose(projected, (0, 1, 3, 2, 4)).astype(jnp.bfloat16)
    queries = head_norm(projected[..., :HEAD_DIM], q_gain)
    key_rows = head_norm(projected[..., HEAD_DIM:2 * HEAD_DIM], k_gain)
    value_rows = projected[..., 2 * HEAD_DIM:]
    spatial = lax.map(spatial_head, (jnp.moveaxis(queries, 2, 0), jnp.moveaxis(key_rows, 2, 0), jnp.moveaxis(value_rows, 2, 0)))
    spatial = jnp.moveaxis(spatial, 0, 2)
    scores = jnp.einsum('bshnc,bthnc->bhnst', queries.astype(jnp.float32), key_rows.astype(jnp.float32)) * HEAD_DIM ** (-0.5)
    row_max = lax.optimization_barrier(jnp.max(scores, axis=-1, keepdims=True))
    weights = jnp.exp(scores - row_max)
    row_total = lax.optimization_barrier(jnp.sum(weights, axis=-1))
    rounded = lax.optimization_barrier(weights.astype(jnp.bfloat16)).astype(jnp.float32)
    temporal = jnp.einsum('bhnst,bthnc->bshnc', rounded, value_rows.astype(jnp.float32))
    temporal = temporal / jnp.transpose(row_total, (0, 3, 1, 2))[..., None]
    combined = (spatial + temporal).astype(jnp.bfloat16)
    per_group = HEADS // N_TM
    grouped = combined.reshape(BATCH, SLABS, N_TM, per_group, SLAB_TOK, HEAD_DIM)
    grouped = jnp.moveaxis(grouped, 2, 0)
    w_groups = w_out.reshape(N_TM, per_group, HEAD_DIM, D)

    def add_group(running, operands):
        block_rows, weight_rows = operands
        term = jnp.einsum('bshnc,hcd->bsnd', block_rows.astype(jnp.float32), weight_rows.astype(jnp.float32))
        term_bf = lax.optimization_barrier(term.astype(jnp.bfloat16))
        return (running + term_bf.astype(jnp.float32), None)
    start_sum = jnp.zeros((BATCH, SLABS, SLAB_TOK, D), jnp.float32)
    projection, _ = lax.scan(add_group, start_sum, (grouped, w_groups))
    attended = (slab_queue.astype(jnp.float32) + gate_per_row * projection).astype(jnp.bfloat16)
    return jnp.roll(attended, 1, axis=1)
```

```python
import math

import jax
import jax.numpy as jnp
from jax import lax
from jax.sharding import PartitionSpec as P

HEAD_DIM = 128


def from_behind(value, axis, steps):
    count = lax.axis_size(axis)
    pairs = [(source, (source + steps) % count) for source in range(count)]
    return lax.ppermute(value, axis, pairs)


def head_norm(values, gain_per_row):
    float_values = values.astype(jnp.float32)
    factor = lax.rsqrt(jnp.mean(jnp.square(float_values), axis=-1, keepdims=True) + 1e-06)
    return (float_values * factor * gain_per_row[:, None, :]).astype(jnp.bfloat16)


def body(slab_queue, levels, mod_table, w_qkv, q_gain, k_gain, w_out):
    batch_count, _, tok_rows, model_width = slab_queue.shape
    slab_count = lax.axis_size("tm")
    tm_index = lax.axis_index("tm")
    heads_here = w_qkv.shape[1]
    inv_root = 1.0 / math.sqrt(HEAD_DIM)
    noise_level_lookup = mod_table.astype(jnp.float32)
    column = tm_index % slab_count
    picked = lax.broadcasted_iota(jnp.int32, levels.shape, 1) == column
    level_now = jnp.sum(jnp.where(picked, levels, 0), axis=1)
    level_ids = lax.broadcasted_iota(jnp.int32, (batch_count, noise_level_lookup.shape[0]), 1)
    one_hot_levels = (level_now[:, None] == level_ids).astype(jnp.float32)
    local_modulation = jnp.einsum(
        "aw,wgs->ags", one_hot_levels, noise_level_lookup, precision=lax.Precision.HIGHEST
    )
    values = slab_queue.astype(jnp.float32)
    centre = jnp.mean(values, axis=-1, keepdims=True)
    spread = jnp.mean(jnp.square(values - centre), axis=-1, keepdims=True)
    normed = (values - centre) * lax.rsqrt(spread + 1e-06)
    modulated = (
        normed * (1.0 + local_modulation[:, 1][:, None, None, :])
        + local_modulation[:, 0][:, None, None, :]
    ).astype(jnp.bfloat16)
    gate_per_row = local_modulation[:, 2]
    projected = jnp.einsum(
        "bknd,dhc->bkhnc",
        lax.all_gather(modulated, "tm", axis=1, tiled=True),
        w_qkv,
        preferred_element_type=jnp.float32,
    ).astype(jnp.bfloat16)
    queries = head_norm(projected[..., :HEAD_DIM], q_gain)
    key_rows = head_norm(projected[..., HEAD_DIM : 2 * HEAD_DIM], k_gain)
    value_rows = projected[..., 2 * HEAD_DIM :]
    scores = (
        jnp.einsum("bshnc,bthnc->bhnst", queries, key_rows, preferred_element_type=jnp.float32)
        * inv_root
    )
    row_max = jnp.max(scores, axis=-1, keepdims=True)
    weights = jnp.exp(scores - row_max)
    row_total = jnp.sum(weights, axis=-1)
    temporal = jnp.einsum(
        "bhnst,bthnc->bshnc",
        weights.astype(jnp.bfloat16),
        value_rows,
        preferred_element_type=jnp.float32,
    )
    temporal = temporal / jnp.transpose(row_total, (0, 3, 1, 2))[..., None]
    group = batch_count * slab_count
    packed = jnp.concatenate([queries, key_rows, value_rows], axis=-1)
    packed = packed.reshape(group, heads_here, tok_rows, 3 * HEAD_DIM)
    whole = lax.all_to_all(packed, "space", split_axis=0, concat_axis=2, tiled=True)
    query_all = whole[..., :HEAD_DIM]
    key_all = whole[..., HEAD_DIM : 2 * HEAD_DIM]
    value_all = whole[..., 2 * HEAD_DIM :]
    block_scores = (
        jnp.einsum("ghnc,ghmc->ghnm", query_all, key_all, preferred_element_type=jnp.float32)
        * inv_root
    )
    block_weights = jnp.exp(block_scores - jnp.max(block_scores, axis=-1, keepdims=True))
    block_total = jnp.sum(block_weights, axis=-1)
    added = jnp.einsum(
        "ghnm,ghmc->ghnc",
        block_weights.astype(jnp.bfloat16),
        value_all,
        preferred_element_type=jnp.float32,
    )
    spatial = (added / block_total[..., None]).astype(jnp.bfloat16)
    spatial = lax.all_to_all(spatial, "space", split_axis=2, concat_axis=0, tiled=True)
    spatial = spatial.astype(jnp.float32)
    combined = (spatial.reshape(queries.shape) + temporal).astype(jnp.bfloat16)
    w_heads = w_out.reshape(heads_here, HEAD_DIM, model_width)
    projection = lax.psum_scatter(
        jnp.einsum("bshnc,hcd->sbnd", combined, w_heads, preferred_element_type=jnp.float32).astype(
            jnp.bfloat16
        ),
        "tm",
        scatter_dimension=0,
        tiled=True,
    ).astype(jnp.float32)
    projection = jnp.swapaxes(projection, 0, 1)
    attended = (
        slab_queue.astype(jnp.float32) + gate_per_row[:, None, None, :] * projection
    ).astype(jnp.bfloat16)
    return from_behind(attended, "tm", 1)


def solution(mesh):
    placed = (
        P(None, "tm", "space", None),
        P(),
        P(),
        P(None, "tm", None),
        P("tm", None),
        P("tm", None),
        P("tm", None),
    )
    return jax.shard_map(
        body, mesh=mesh, in_specs=placed, out_specs=P(None, "tm", "space", None), check_vma=False
    )
```

```python
import functools
import math

import jax
import jax.numpy as jnp
from jax import lax
from jax.experimental import pallas as pl
from jax.experimental.pallas import tpu as pltpu
from jax.sharding import PartitionSpec as P

HEAD_DIM = 128
MESH = pl.DeviceIdType.MESH
F32 = jnp.float32
BF16 = jnp.bfloat16


def dot_t(left, right):
    return lax.dot_general(left, right, (((1,), (1,)), ((), ())), preferred_element_type=F32)


def head_norm(values, gain):
    values = values.astype(F32)
    factor = lax.rsqrt(jnp.mean(jnp.square(values), axis=-1, keepdims=True) + 1e-06)
    return (values * factor * gain).astype(BF16)


def kernel(
    ring, cols,
    slab, levels, mod, w_qkv, q_gain, k_gain, w_out,
    out,
    mod_send, tokens, w_buf, gq, gk, wo, qkv, sp_in, sp_out, sp_back, tmp_out, comb,
    x_own, x_send, x_recv, part, r_send, r_recv, l_send, l_recv, prev, fin_send, fin_recv,
    loc_sem, pair_send, pair_recv, ag_send, ag_recv, aa_send, aa_recv, rt_send, rt_recv,
    x_sems, rs_send, rs_recv, misc_send, misc_recv,
):
    half = ring // 2
    slabs = ring
    tok, width = slab.shape[1], slab.shape[2]
    tm, space = lax.axis_index("tm"), lax.axis_index("space")
    core, z_lo = lax.rem(tm, 2), lax.div(tm, 2)
    me, z_hi = lax.div(space, 2), lax.rem(space, 2)
    z = z_hi * half + z_lo
    other = 1 - core
    inv_root = 1.0 / math.sqrt(HEAD_DIM)

    def mod_ring(value):
        return lax.rem(value + ring, ring)

    def device(plane, of_core, column):
        return (lax.rem(plane, half) * 2 + of_core, column * 2 + lax.div(plane, half))

    right = device(mod_ring(z + 1), core, me)
    left = device(mod_ring(z - 1), core, me)
    partner = device(z, other, me)
    across = device(mod_ring(z + half), core, me)
    tm_next = (lax.rem(tm + 1, slabs), space)
    tm_far = (lax.rem(tm + jnp.where(core == 1, 1, slabs - 1), slabs), space)

    def remote(src, dst, send_sem, recv_sem, target):
        return pltpu.make_async_remote_copy(
            src_ref=src, dst_ref=dst, send_sem=send_sem, recv_sem=recv_sem,
            device_id=target, device_id_type=MESH,
        )

    barrier = pltpu.get_barrier_semaphore()
    for target in (right, left, partner, across, tm_far):
        pl.semaphore_signal(barrier, inc=1, device_id=target, device_id_type=MESH)

    def greet(step, carry):
        column = lax.rem(me + step, cols)
        pl.semaphore_signal(barrier, inc=1, device_id=device(z, core, column), device_id_type=MESH)
        return carry

    lax.fori_loop(1, cols, greet, 0)

    own_head = core == z_hi
    local_w = pltpu.make_async_copy(w_qkv, w_buf, loc_sem.at[0])
    local_wo = pltpu.make_async_copy(w_out, wo.at[core], loc_sem.at[1])
    local_wo.start()

    @pl.when(own_head)
    def _():
        local_w.start()
        gq[...] = q_gain[...]
        gk[...] = k_gain[...]

    def modulate(batch):
        row = mod[levels[batch, tm]].astype(F32)
        values = slab[batch].astype(F32)
        centre = jnp.mean(values, axis=-1, keepdims=True)
        moved = values - centre
        spread = jnp.mean(jnp.square(moved), axis=-1, keepdims=True)
        return (moved * lax.rsqrt(spread + 1e-06) * (1.0 + row[1:2]) + row[0:1]).astype(BF16)

    mod_send[...] = modulate(other)
    tokens[z * 2 + core] = modulate(core)
    pl.semaphore_wait(barrier, 5 + cols - 1)

    def gather_copy(way, step, t, origin):
        slot = origin * 2 + t
        return remote(
            tokens.at[slot], tokens.at[slot], ag_send.at[way, step, t], ag_recv.at[way, step, t],
            (right, left)[way],
        )

    to_pair = remote(mod_send, tokens.at[z * 2 + core], pair_send.at[0], pair_recv.at[0], partner)
    to_pair.start()
    for way in (0, 1):
        gather_copy(way, 1, core, z).start()
    from_pair = remote(mod_send, tokens.at[z * 2 + other], pair_send.at[0], pair_recv.at[0], partner)
    from_pair.wait_recv()
    for way in (0, 1):
        gather_copy(way, 1, other, z).start()

    give_w = remote(w_qkv, w_buf, pair_send.at[1], pair_recv.at[1], partner)
    give_gq = remote(q_gain, gq, pair_send.at[2], pair_recv.at[2], partner)
    give_gk = remote(k_gain, gk, pair_send.at[3], pair_recv.at[3], partner)
    give_wo = remote(w_out, wo.at[core], pair_send.at[4], pair_recv.at[4], partner)
    take_wo = remote(w_out, wo.at[other], pair_send.at[4], pair_recv.at[4], partner)
    pass_slab = remote(slab, prev, misc_send.at[0], misc_recv.at[0], tm_next)

    @pl.when(own_head)
    def _():
        give_w.start()
        give_gq.start()
        give_gk.start()

    give_wo.start()
    pass_slab.start()

    def slab_copy(column, source):
        return remote(
            qkv.at[:, column], sp_in.at[source], aa_send.at[column], aa_recv.at[source],
            device(z, core, column),
        )

    def send_pair(q_lo):
        for t in (0, 1):
            column = q_lo * 2 + t

            @pl.when(column != me)
            def _():
                slab_copy(column, me).start()

    def gather_step(step, carry):
        plane_a = mod_ring(z - step)
        plane_b = mod_ring(z + step)
        for turn in (0, 1):
            t = core if turn == 0 else other
            for way, origin in ((0, plane_a), (1, plane_b)):

                @pl.when((step < half) | (t == way))
                def _():
                    gather_copy(way, step, t, origin).wait_recv()

                @pl.when((step < half - 1) | ((step == half - 1) & (t == way)))
                def _():
                    gather_copy(way, step + 1, t, origin).start()

        @pl.when(step == 1)
        def _():
            @pl.when(own_head)
            def _():
                local_w.wait()

            @pl.when(jnp.logical_not(own_head))
            def _():
                give_w.wait_recv()
                give_gq.wait_recv()
                give_gk.wait_recv()

        second = jnp.where(step == half, z, plane_b)
        rows_a = tokens[pl.ds(plane_a * 2, 2)].reshape(2 * tok, width)
        rows_b = tokens[pl.ds(second * 2, 2)].reshape(2 * tok, width)
        rows = jnp.concatenate([rows_a, rows_b], axis=0)
        projected = jnp.dot(rows, w_buf[...], preferred_element_type=F32).astype(BF16)
        queries = head_norm(projected[:, :HEAD_DIM], gq[...])
        keys = head_norm(projected[:, HEAD_DIM : 2 * HEAD_DIM], gk[...])
        values = projected[:, 2 * HEAD_DIM :]
        for at, plane in ((0, plane_a), (1, second)):
            hi, lo = lax.div(plane, half), lax.rem(plane, half)
            for t in (0, 1):
                cut = slice((at * 2 + t) * tok, (at * 2 + t + 1) * tok)
                qkv[hi, lo * 2 + t, :, 0:HEAD_DIM] = queries[cut]
                qkv[hi, lo * 2 + t, :, HEAD_DIM : 2 * HEAD_DIM] = keys[cut]
                qkv[hi, lo * 2 + t, :, 2 * HEAD_DIM :] = values[cut]

        @pl.when(step >= half // 2)
        def _():
            send_pair(lax.rem(plane_a, half))

        @pl.when((step > half // 2) & (step < half))
        def _():
            send_pair(lax.rem(plane_b, half))

        return carry

    lax.fori_loop(1, half + 1, gather_step, 0)
    sp_in[me] = qkv[:, me]

    rows_t = slabs * tok
    at_row = lax.rem(lax.broadcasted_iota(jnp.int32, (rows_t, rows_t), 0), tok)
    at_col = lax.rem(lax.broadcasted_iota(jnp.int32, (rows_t, rows_t), 1), tok)
    same = at_row == at_col
    for hi in (0, 1):
        queries = qkv[hi, :, :, 0:HEAD_DIM].reshape(rows_t, HEAD_DIM)
        keys = qkv[hi, :, :, HEAD_DIM : 2 * HEAD_DIM].reshape(rows_t, HEAD_DIM)
        values = qkv[hi, :, :, 2 * HEAD_DIM :].reshape(rows_t, HEAD_DIM)
        scores = jnp.where(same, dot_t(queries, keys) * inv_root, -jnp.inf)
        weights = jnp.exp(scores - jnp.max(scores, axis=-1, keepdims=True))
        total = jnp.sum(weights, axis=-1, keepdims=True)
        mixed = jnp.dot(weights.astype(BF16), values, preferred_element_type=F32) / total
        tmp_out[hi] = mixed.reshape(slabs, tok, HEAD_DIM)

    def await_slab(step, carry):
        slab_copy(me, lax.rem(me + step, cols)).wait_recv()
        return carry

    lax.fori_loop(1, cols, await_slab, 0)

    def back_copy(column, of_slab):
        return remote(
            sp_out.at[column], sp_back.at[:, of_slab], rt_send.at[column], rt_recv.at[of_slab],
            device(z, core, column),
        )

    group = 4
    rows_s = group * 2 * tok

    def spatial_step(step, carry):
        keys = sp_in[:, :, :, HEAD_DIM : 2 * HEAD_DIM].reshape(cols * 2 * tok, HEAD_DIM)
        values = sp_in[:, :, :, 2 * HEAD_DIM :].reshape(cols * 2 * tok, HEAD_DIM)
        queries = sp_in[pl.ds(step * group, group), :, :, 0:HEAD_DIM].reshape(rows_s, HEAD_DIM)
        scores = dot_t(queries, keys) * inv_root
        weights = jnp.exp(scores - jnp.max(scores, axis=-1, keepdims=True))
        total = jnp.sum(weights, axis=-1, keepdims=True)
        mixed = jnp.dot(weights.astype(BF16), values, preferred_element_type=F32) / total
        sp_out[pl.ds(step * group, group)] = mixed.astype(BF16).reshape(group, 2, tok, HEAD_DIM)
        for at in range(group):
            column = step * group + at

            @pl.when(column != me)
            def _():
                back_copy(column, me).start()

        return carry

    lax.fori_loop(0, cols // group, spatial_step, 0)
    sp_back[:, me] = sp_out[me]
    local_wo.wait()
    take_wo.wait_recv()

    def await_back(step, carry):
        back_copy(me, lax.rem(me + step, cols)).wait_recv()
        return carry

    lax.fori_loop(1, cols, await_back, 0)
    comb[...] = (sp_back[...].astype(F32) + tmp_out[...]).astype(BF16)

    def fill(dst, plane):
        def one(at, carry):
            place = lax.rem(2 * plane + 2 * ring - (half - 1) + at, 2 * ring)
            from_slab = lax.rem(lax.rem(place, slabs) + slabs - 1, slabs)
            dst[at] = comb[lax.div(place, slabs), from_slab]
            return carry

        lax.fori_loop(0, ring, one, 0)

    fill(x_send, mod_ring(z + half))
    swap = remote(x_send, x_recv, x_sems.at[0], x_sems.at[1], across)
    swap.start()
    fill(x_own, z)
    chunk = min(768, width)
    rows_p = ring * tok
    for at in range(0, width, chunk):
        product = jnp.dot(
            x_own[...].reshape(rows_p, HEAD_DIM), wo[z_hi, :, at : at + chunk],
            preferred_element_type=F32,
        )
        part[:, :, at : at + chunk] = product.reshape(ring, tok, chunk)
    swap.wait_recv()
    for at in range(0, width, chunk):
        product = jnp.dot(
            x_recv[...].reshape(rows_p, HEAD_DIM), wo[1 - z_hi, :, at : at + chunk],
            preferred_element_type=F32,
        )
        part[:, :, at : at + chunk] += product.reshape(ring, tok, chunk)

    def sum_copy(way, step):
        mine, theirs, target = ((r_send, r_recv, right), (l_send, l_recv, left))[way]
        return remote(
            mine.at[step], theirs.at[step], rs_send.at[way, step], rs_recv.at[way, step], target
        )

    def sum_step(step, carry):
        for way, mine, theirs, block in (
            (0, r_send, r_recv, ring - 1 - step), (1, l_send, l_recv, step),
        ):

            @pl.when(step < 2)
            def _():
                mine[step] = part[block].astype(BF16)

            @pl.when(step >= 2)
            def _():
                sum_copy(way, step - 2).wait_recv()
                mine[step] = (part[block] + theirs[step - 2].astype(F32)).astype(BF16)

            sum_copy(way, step).start()
        return carry

    lax.fori_loop(0, half - 1, sum_step, 0)
    if half > 2:
        for way in (0, 1):
            sum_copy(way, half - 3).wait_recv()
    for way in (0, 1):
        sum_copy(way, half - 2).wait_recv()

    def total_of(t):
        if half > 2:
            return (
                part[half - 1 + t]
                + r_recv[half - 2 - t].astype(F32)
                + l_recv[half - 3 + t].astype(F32)
            )
        from_side = jnp.where(t == 0, r_recv[0].astype(F32), l_recv[0].astype(F32))
        return part[half - 1 + t] + from_side

    fin_send[...] = total_of(other).astype(BF16)
    give_fin = remote(fin_send, fin_recv, misc_send.at[1], misc_recv.at[1], partner)
    give_fin.start()
    pass_slab.wait_recv()
    tm_before = lax.rem(tm + slabs - 1, slabs)

    def attend(batch, projection):
        gate = mod[levels[batch, tm_before]].astype(F32)[2:3]
        out[batch] = (prev[batch].astype(F32) + gate * projection).astype(BF16)

    attend(core, total_of(core))
    give_fin.wait_recv()
    attend(other, fin_recv[...].astype(F32))

    to_pair.wait_send()

    @pl.when(own_head)
    def _():
        give_w.wait_send()
        give_gq.wait_send()
        give_gk.wait_send()

    give_wo.wait_send()
    pass_slab.wait_send()
    give_fin.wait_send()
    swap.wait_send()

    def drain_gather(step, carry):
        for way in (0, 1):
            for t in (0, 1):

                @pl.when((step < half) | (t == way))
                def _():
                    gather_copy(way, step, t, z).wait_send()

        return carry

    lax.fori_loop(1, half + 1, drain_gather, 0)

    def drain_plane(step, carry):
        column = lax.rem(me + step, cols)
        slab_copy(column, me).wait_send()
        back_copy(column, me).wait_send()
        return carry

    lax.fori_loop(1, cols, drain_plane, 0)

    def drain_sum(step, carry):
        for way in (0, 1):
            sum_copy(way, step).wait_send()
        return carry

    lax.fori_loop(0, half - 1, drain_sum, 0)


def body(slab_queue, levels, mod_table, w_qkv, q_gain, k_gain, w_out):
    batch, _, tok, width = slab_queue.shape
    ring = lax.axis_size("tm")
    cols = lax.axis_size("space") // 2
    half = ring // 2
    vmem = pl.BlockSpec(memory_space=pltpu.VMEM)
    hbm = pl.BlockSpec(memory_space=pl.ANY)
    dma = pltpu.SemaphoreType.DMA
    block = (tok, width)
    return pl.pallas_call(
        functools.partial(kernel, ring, cols),
        out_shape=jax.ShapeDtypeStruct((batch, tok, width), BF16),
        in_specs=[vmem, pl.BlockSpec(memory_space=pltpu.SMEM), vmem, hbm, vmem, vmem, hbm],
        out_specs=vmem,
        scratch_shapes=[
            pltpu.VMEM(block, BF16),
            pltpu.VMEM((2 * ring,) + block, BF16),
            pltpu.VMEM((width, 3 * HEAD_DIM), BF16),
            pltpu.VMEM((1, HEAD_DIM), F32),
            pltpu.VMEM((1, HEAD_DIM), F32),
            pltpu.VMEM((2, HEAD_DIM, width), BF16),
            pltpu.VMEM((2, ring, tok, 3 * HEAD_DIM), BF16),
            pltpu.VMEM((cols, 2, tok, 3 * HEAD_DIM), BF16),
            pltpu.VMEM((cols, 2, tok, HEAD_DIM), BF16),
            pltpu.VMEM((2, ring, tok, HEAD_DIM), BF16),
            pltpu.VMEM((2, ring, tok, HEAD_DIM), F32),
            pltpu.VMEM((2, ring, tok, HEAD_DIM), BF16),
            pltpu.VMEM((ring, tok, HEAD_DIM), BF16),
            pltpu.VMEM((ring, tok, HEAD_DIM), BF16),
            pltpu.VMEM((ring, tok, HEAD_DIM), BF16),
            pltpu.VMEM((ring,) + block, F32),
            pltpu.VMEM((half - 1,) + block, BF16),
            pltpu.VMEM((half - 1,) + block, BF16),
            pltpu.VMEM((half - 1,) + block, BF16),
            pltpu.VMEM((half - 1,) + block, BF16),
            pltpu.VMEM((batch,) + block, BF16),
            pltpu.VMEM(block, BF16),
            pltpu.VMEM(block, BF16),
            dma((2,)),
            dma((5,)),
            dma((5,)),
            dma((2, half + 1, 2)),
            dma((2, half + 1, 2)),
            dma((cols,)),
            dma((cols,)),
            dma((cols,)),
            dma((cols,)),
            dma((2,)),
            dma((2, half - 1)),
            dma((2, half - 1)),
            dma((2,)),
            dma((2,)),
        ],
        compiler_params=pltpu.CompilerParams(
            collective_id=0, has_side_effects=True, vmem_limit_bytes=48 * 1024 * 1024
        ),
        cost_estimate=pl.CostEstimate(
            flops=4 * 10**9, bytes_accessed=8 * 10**6, transcendentals=4 * 10**5
        ),
    )(
        slab_queue.reshape(batch, tok, width), levels, mod_table,
        w_qkv.reshape(width, 3 * HEAD_DIM), q_gain, k_gain, w_out,
    ).reshape(batch, 1, tok, width)


def solution(mesh):
    placed = (
        P(None, "tm", "space", None),
        P(),
        P(),
        P(None, "tm", None),
        P("tm", None),
        P("tm", None),
        P("tm", None),
    )
    return jax.shard_map(
        body, mesh=mesh, in_specs=placed, out_specs=P(None, "tm", "space", None), check_vma=False
    )
```

```python
import functools
import math

import jax
import jax.numpy as jnp
from jax import lax
from jax.experimental import pallas as pl
from jax.experimental.pallas import tpu as pltpu
from jax.sharding import PartitionSpec as P

HEAD_DIM = 128
W_PIECES = 12
VMEM_BYTES = 64 * 1024 * 1024 - 192 * 1024
MESH = pl.DeviceIdType.MESH
F32 = jnp.float32
BF16 = jnp.bfloat16


def dot_t(left, right):
    return lax.dot_general(left, right, (((1,), (1,)), ((), ())), preferred_element_type=F32)


def head_norm(values, gain):
    values = values.astype(F32)
    factor = lax.rsqrt(jnp.mean(jnp.square(values), axis=-1, keepdims=True) + 1e-06)
    return (values * factor * gain).astype(BF16)


def kernel(
    ring, cols,
    slab_in, levels_in, mod_in, w_qkv, q_gain, k_gain, w_out,
    out,
    slab, levels, mod, rows_of, mod_send, tokens, w_buf, gq, gk, wo, qkv, sp_in, sp_out, sp_back, tmp_out, comb,
    x_own, x_send, x_recv, part, r_send, r_recv, l_send, l_recv, prev, fin_send, fin_recv,
    loc_sem, pair_send, pair_recv, ag_send, ag_recv, aa_send, aa_recv, rt_send, rt_recv,
    x_sems, rs_send, rs_recv, misc_send, misc_recv, w_send, w_recv,
):
    half = ring // 2
    slabs = ring
    tok, width = slab.shape[1], slab.shape[2]
    piece = width // W_PIECES
    tm, space = lax.axis_index("tm"), lax.axis_index("space")
    core, z_lo = lax.rem(tm, 2), lax.div(tm, 2)
    me, z_hi = lax.div(space, 2), lax.rem(space, 2)
    z = z_hi * half + z_lo
    other = 1 - core
    inv_root = 1.0 / math.sqrt(HEAD_DIM)

    def mod_ring(value):
        return lax.rem(value + ring, ring)

    def device(plane, of_core, column):
        return (lax.rem(plane, half) * 2 + of_core, column * 2 + lax.div(plane, half))

    right = device(mod_ring(z + 1), core, me)
    left = device(mod_ring(z - 1), core, me)
    partner = device(z, other, me)
    across = device(mod_ring(z + half), core, me)
    tm_next = (lax.rem(tm + 1, slabs), space)
    tm_far = (lax.rem(tm + jnp.where(core == 1, 1, slabs - 1), slabs), space)

    def remote(src, dst, send_sem, recv_sem, target):
        return pltpu.make_async_remote_copy(
            src_ref=src, dst_ref=dst, send_sem=send_sem, recv_sem=recv_sem,
            device_id=target, device_id_type=MESH,
        )

    barrier = pltpu.get_barrier_semaphore()
    for target in (right, left, partner, across, tm_far):
        pl.semaphore_signal(barrier, inc=1, device_id=target, device_id_type=MESH)

    def greet(step, carry):
        column = lax.rem(me + step, cols)
        pl.semaphore_signal(barrier, inc=1, device_id=device(z, core, column), device_id_type=MESH)
        return carry

    lax.fori_loop(1, cols, greet, 0)

    own_head = core == z_hi
    fetch_levels = pltpu.make_async_copy(levels_in, levels, loc_sem.at[2])
    fetch_mod = pltpu.make_async_copy(mod_in, mod, loc_sem.at[3])
    fetch_slab = pltpu.make_async_copy(slab_in, slab, loc_sem.at[4])
    local_w = pltpu.make_async_copy(w_qkv, w_buf, loc_sem.at[0])
    local_wo = pltpu.make_async_copy(w_out, wo.at[core], loc_sem.at[1])
    local_gq = pltpu.make_async_copy(q_gain, gq, loc_sem.at[5])
    local_gk = pltpu.make_async_copy(k_gain, gk, loc_sem.at[6])
    fetch_levels.start()
    fetch_mod.start()
    fetch_slab.start()

    @pl.when(own_head)
    def _():
        local_gq.start()
        local_gk.start()
        local_w.start()

    local_wo.start()
    fetch_levels.wait()
    fetch_mod.wait()

    tm_before = lax.rem(tm + slabs - 1, slabs)
    pick_row = lax.broadcasted_iota(jnp.int32, (16, mod.shape[1]), 0)
    pick_col = lax.broadcasted_iota(jnp.int32, (16, mod.shape[1]), 1)
    hot = jnp.zeros((16, mod.shape[1]), F32)
    for at, (batch, of_slab) in enumerate(((0, tm), (1, tm), (0, tm_before), (1, tm_before))):
        hot = jnp.where((pick_row == at) & (pick_col == levels[batch, of_slab]), 1.0, hot)
    for kind in range(3):
        picked = jnp.dot(hot.astype(BF16), mod[kind], preferred_element_type=F32)
        for at in range(4):
            rows_of[kind, at] = picked[at : at + 1]

    def modulate(batch):
        values = slab[batch].astype(F32)
        centre = jnp.mean(values, axis=-1, keepdims=True)
        moved = values - centre
        spread = jnp.mean(jnp.square(moved), axis=-1, keepdims=True)
        normed = moved * lax.rsqrt(spread + 1e-06)
        return (normed * (1.0 + rows_of[1, batch]) + rows_of[0, batch]).astype(BF16)

    fetch_slab.wait()
    mod_send[...] = modulate(other)
    tokens[z * 2 + core] = modulate(core)
    pl.semaphore_wait(barrier, 5 + cols - 1)

    def gather_copy(way, step, t, origin):
        slot = origin * 2 + t
        return remote(
            tokens.at[slot], tokens.at[slot], ag_send.at[way, step, t], ag_recv.at[way, step, t],
            (right, left)[way],
        )

    to_pair = remote(mod_send, tokens.at[z * 2 + core], pair_send.at[0], pair_recv.at[0], partner)
    to_pair.start()
    for way in (0, 1):
        gather_copy(way, 1, core, z).start()
    from_pair = remote(mod_send, tokens.at[z * 2 + other], pair_send.at[0], pair_recv.at[0], partner)
    from_pair.wait_recv()
    for way in (0, 1):
        gather_copy(way, 1, other, z).start()

    def give_w(at):
        rows = pl.ds(at * piece, piece)
        return remote(w_qkv.at[rows], w_buf.at[rows], w_send.at[at], w_recv.at[at], partner)

    give_gq = remote(q_gain, gq, pair_send.at[2], pair_recv.at[2], partner)
    give_gk = remote(k_gain, gk, pair_send.at[3], pair_recv.at[3], partner)
    give_wo = remote(w_out, wo.at[core], pair_send.at[4], pair_recv.at[4], partner)
    take_wo = remote(w_out, wo.at[other], pair_send.at[4], pair_recv.at[4], partner)
    pass_slab = remote(slab, prev, misc_send.at[0], misc_recv.at[0], tm_next)

    @pl.when(own_head)
    def _():
        give_gq.start()
        give_gk.start()

    def slab_copy(column, source):
        return remote(
            qkv.at[:, column], sp_in.at[source], aa_send.at[column], aa_recv.at[source],
            device(z, core, column),
        )

    def send_pair(q_lo):
        for t in (0, 1):
            column = q_lo * 2 + t

            @pl.when(column != me)
            def _():
                slab_copy(column, me).start()

    first_dot = max(half // 2, 2)
    per_step = W_PIECES // (first_dot - 1)

    def gather_step(step, carry):
        plane_a = mod_ring(z - step)
        plane_b = mod_ring(z + step)
        for turn in (0, 1):
            t = core if turn == 0 else other
            for way, origin in ((0, plane_a), (1, plane_b)):

                @pl.when((step < half) | (t == way))
                def _():
                    gather_copy(way, step, t, origin).wait_recv()

                @pl.when((step < half - 1) | ((step == half - 1) & (t == way)))
                def _():
                    gather_copy(way, step + 1, t, origin).start()

        @pl.when(own_head & (step < first_dot))
        def _():
            def one(at, inner):
                give_w(at).start()
                return inner

            lax.fori_loop((step - 1) * per_step, step * per_step, one, 0)

        @pl.when(step == first_dot)
        def _():
            give_wo.start()

            @pl.when(own_head)
            def _():
                local_w.wait()
                local_gq.wait()
                local_gk.wait()

            @pl.when(jnp.logical_not(own_head))
            def _():
                def one(at, inner):
                    give_w(at).wait_recv()
                    return inner

                lax.fori_loop(0, W_PIECES, one, 0)
                give_gq.wait_recv()
                give_gk.wait_recv()

        def reach(at):
            return jnp.where(at < first_dot, 0, jnp.minimum(2 * (at - first_dot + 1), at))

        lax.fori_loop(reach(step - 1) + 1, reach(step) + 1, project_step, 0)
        return carry

    def project_step(step, carry):
        plane_a = mod_ring(z - step)
        plane_b = mod_ring(z + step)
        second = jnp.where(step == half, z, plane_b)
        rows_a = tokens[pl.ds(plane_a * 2, 2)].reshape(2 * tok, width)
        rows_b = tokens[pl.ds(second * 2, 2)].reshape(2 * tok, width)
        rows = jnp.concatenate([rows_a, rows_b], axis=0)
        projected = jnp.dot(rows, w_buf[...], preferred_element_type=F32).astype(BF16)
        queries = head_norm(projected[:, :HEAD_DIM], gq[...])
        keys = head_norm(projected[:, HEAD_DIM : 2 * HEAD_DIM], gk[...])
        values = projected[:, 2 * HEAD_DIM :]
        for at, plane in ((0, plane_a), (1, second)):
            hi, lo = lax.div(plane, half), lax.rem(plane, half)
            for t in (0, 1):
                cut = slice((at * 2 + t) * tok, (at * 2 + t + 1) * tok)
                qkv[hi, lo * 2 + t, :, 0:HEAD_DIM] = queries[cut]
                qkv[hi, lo * 2 + t, :, HEAD_DIM : 2 * HEAD_DIM] = keys[cut]
                qkv[hi, lo * 2 + t, :, 2 * HEAD_DIM :] = values[cut]

        @pl.when(step >= half // 2)
        def _():
            send_pair(lax.rem(plane_a, half))

        @pl.when((step > half // 2) & (step < half))
        def _():
            send_pair(lax.rem(plane_b, half))

        return carry

    lax.fori_loop(1, half + 1, gather_step, 0)
    pass_slab.start()
    sp_in[me] = qkv[:, me]

    rows_t = slabs * tok
    at_row = lax.broadcasted_iota(jnp.int32, (rows_t, rows_t), 0) & (tok - 1)
    at_col = lax.broadcasted_iota(jnp.int32, (rows_t, rows_t), 1) & (tok - 1)
    same = at_row == at_col
    for hi in (0, 1):
        queries = qkv[hi, :, :, 0:HEAD_DIM].reshape(rows_t, HEAD_DIM)
        keys = qkv[hi, :, :, HEAD_DIM : 2 * HEAD_DIM].reshape(rows_t, HEAD_DIM)
        values = qkv[hi, :, :, 2 * HEAD_DIM :].reshape(rows_t, HEAD_DIM)
        scores = jnp.where(same, dot_t(queries, keys) * inv_root, -jnp.inf)
        weights = jnp.exp(scores - jnp.max(scores, axis=-1, keepdims=True))
        total = jnp.sum(weights, axis=-1, keepdims=True)
        mixed = jnp.dot(weights.astype(BF16), values, preferred_element_type=F32) / total
        tmp_out[hi] = mixed.reshape(slabs, tok, HEAD_DIM)

    def await_slab(step, carry):
        slab_copy(me, lax.rem(me + step, cols)).wait_recv()
        return carry

    lax.fori_loop(1, cols, await_slab, 0)

    def back_copy(column, of_slab):
        return remote(
            sp_out.at[column], sp_back.at[:, of_slab], rt_send.at[column], rt_recv.at[of_slab],
            device(z, core, column),
        )

    group = 4
    rows_s = group * 2 * tok

    def spatial_step(step, carry):
        keys = sp_in[:, :, :, HEAD_DIM : 2 * HEAD_DIM].reshape(cols * 2 * tok, HEAD_DIM)
        values = sp_in[:, :, :, 2 * HEAD_DIM :].reshape(cols * 2 * tok, HEAD_DIM)
        queries = sp_in[pl.ds(step * group, group), :, :, 0:HEAD_DIM].reshape(rows_s, HEAD_DIM)
        scores = dot_t(queries, keys) * inv_root
        weights = jnp.exp(scores - jnp.max(scores, axis=-1, keepdims=True))
        total = jnp.sum(weights, axis=-1, keepdims=True)
        mixed = jnp.dot(weights.astype(BF16), values, preferred_element_type=F32) / total
        sp_out[pl.ds(step * group, group)] = mixed.astype(BF16).reshape(group, 2, tok, HEAD_DIM)
        for at in range(group):
            column = step * group + at

            @pl.when(column != me)
            def _():
                back_copy(column, me).start()

        return carry

    lax.fori_loop(0, cols // group, spatial_step, 0)
    sp_back[:, me] = sp_out[me]
    local_wo.wait()
    take_wo.wait_recv()

    def await_back(step, carry):
        back_copy(me, lax.rem(me + step, cols)).wait_recv()
        return carry

    lax.fori_loop(1, cols, await_back, 0)
    comb[...] = (sp_back[...].astype(F32) + tmp_out[...]).astype(BF16)

    def fill(dst, plane):
        def one(at, carry):
            step = lax.div(at, 2)
            block = jnp.where(lax.rem(at, 2) == 0, ring - 1 - step, step)
            place = lax.rem(2 * plane + 2 * ring - (half - 1) + block, 2 * ring)
            from_slab = lax.rem(lax.rem(place, slabs) + slabs - 1, slabs)
            dst[at] = comb[lax.div(place, slabs), from_slab]
            return carry

        lax.fori_loop(0, ring, one, 0)

    def swap(at):
        rows = pl.ds(at * 4, 4)
        return remote(x_send.at[rows], x_recv.at[rows], x_sems.at[0, at], x_sems.at[1, at], across)

    swaps = ring // 4
    fill(x_send, mod_ring(z + half))
    for at in range(swaps):
        swap(at).start()
    fill(x_own, z)
    chunk = min(768, width)
    rows_p = ring * tok
    for at in range(0, width, chunk):
        product = jnp.dot(
            x_own[...].reshape(rows_p, HEAD_DIM), wo[z_hi, :, at : at + chunk],
            preferred_element_type=F32,
        )
        part[:, :, at : at + chunk] = product.reshape(ring, tok, chunk)

    def sum_copy(way, step):
        mine, theirs, target = ((r_send, r_recv, right), (l_send, l_recv, left))[way]
        return remote(
            mine.at[step], theirs.at[step], rs_send.at[way, step], rs_recv.at[way, step], target
        )

    def sum_step(step, carry):
        @pl.when(lax.rem(step, 2) == 0)
        def _():
            swap(lax.div(step, 2)).wait_recv()
            rows = pl.ds(step * 2, 4)
            for at in range(0, width, chunk):
                product = jnp.dot(
                    x_recv[rows].reshape(4 * tok, HEAD_DIM), wo[1 - z_hi, :, at : at + chunk],
                    preferred_element_type=F32,
                )
                part[rows, :, at : at + chunk] += product.reshape(4, tok, chunk)

        for way, mine, theirs in ((0, r_send, r_recv), (1, l_send, l_recv)):
            block = step * 2 + way

            @pl.when(step < 2)
            def _():
                mine[step] = part[block].astype(BF16)

            @pl.when(step >= 2)
            def _():
                sum_copy(way, step - 2).wait_recv()
                mine[step] = (part[block] + theirs[step - 2].astype(F32)).astype(BF16)

            sum_copy(way, step).start()
        return carry

    lax.fori_loop(0, half - 1, sum_step, 0)
    if half > 2:
        for way in (0, 1):
            sum_copy(way, half - 3).wait_recv()
    for way in (0, 1):
        sum_copy(way, half - 2).wait_recv()

    def total_of(t):
        if half > 2:
            return (
                part[ring - 1 - t]
                + r_recv[half - 2 - t].astype(F32)
                + l_recv[half - 3 + t].astype(F32)
            )
        from_side = jnp.where(t == 0, r_recv[0].astype(F32), l_recv[0].astype(F32))
        return part[ring - 1 - t] + from_side

    fin_send[...] = total_of(other).astype(BF16)
    give_fin = remote(fin_send, fin_recv, misc_send.at[1], misc_recv.at[1], partner)
    give_fin.start()
    pass_slab.wait_recv()

    def attend(batch, projection):
        gate = rows_of[2, 2 + batch]
        out[batch] = (prev[batch].astype(F32) + gate * projection).astype(BF16)

    attend(core, total_of(core))
    give_fin.wait_recv()
    attend(other, fin_recv[...].astype(F32))

    to_pair.wait_send()

    @pl.when(own_head)
    def _():
        def one(at, inner):
            give_w(at).wait_send()
            return inner

        lax.fori_loop(0, W_PIECES, one, 0)
        give_gq.wait_send()
        give_gk.wait_send()

    give_wo.wait_send()
    pass_slab.wait_send()
    give_fin.wait_send()
    for at in range(swaps):
        swap(at).wait_send()

    def drain_gather(step, carry):
        for way in (0, 1):
            for t in (0, 1):

                @pl.when((step < half) | (t == way))
                def _():
                    gather_copy(way, step, t, z).wait_send()

        return carry

    lax.fori_loop(1, half + 1, drain_gather, 0)

    def drain_plane(step, carry):
        column = lax.rem(me + step, cols)
        slab_copy(column, me).wait_send()
        back_copy(column, me).wait_send()
        return carry

    lax.fori_loop(1, cols, drain_plane, 0)

    def drain_sum(step, carry):
        for way in (0, 1):
            sum_copy(way, step).wait_send()
        return carry

    lax.fori_loop(0, half - 1, drain_sum, 0)


def body(slab_queue, levels, mod_table, w_qkv, q_gain, k_gain, w_out):
    batch, _, tok, width = slab_queue.shape
    ring = lax.axis_size("tm")
    cols = lax.axis_size("space") // 2
    half = ring // 2
    vmem = pl.BlockSpec(memory_space=pltpu.VMEM)
    hbm = pl.BlockSpec(memory_space=pltpu.HBM)
    dma = pltpu.SemaphoreType.DMA
    block = (tok, width)
    return pl.pallas_call(
        functools.partial(kernel, ring, cols),
        out_shape=jax.ShapeDtypeStruct((batch, tok, width), BF16),
        in_specs=[hbm] * 7,
        out_specs=vmem,
        scratch_shapes=[
            pltpu.VMEM((batch,) + block, BF16),
            pltpu.SMEM(levels.shape, jnp.int32),
            pltpu.VMEM((3, mod_table.shape[0], width), BF16),
            pltpu.VMEM((3, 4, 1, width), F32),
            pltpu.VMEM(block, BF16),
            pltpu.VMEM((2 * ring,) + block, BF16),
            pltpu.VMEM((width, 3 * HEAD_DIM), BF16),
            pltpu.VMEM((1, HEAD_DIM), F32),
            pltpu.VMEM((1, HEAD_DIM), F32),
            pltpu.VMEM((2, HEAD_DIM, width), BF16),
            pltpu.VMEM((2, ring, tok, 3 * HEAD_DIM), BF16),
            pltpu.VMEM((cols, 2, tok, 3 * HEAD_DIM), BF16),
            pltpu.VMEM((cols, 2, tok, HEAD_DIM), BF16),
            pltpu.VMEM((2, ring, tok, HEAD_DIM), BF16),
            pltpu.VMEM((2, ring, tok, HEAD_DIM), F32),
            pltpu.VMEM((2, ring, tok, HEAD_DIM), BF16),
            pltpu.VMEM((ring, tok, HEAD_DIM), BF16),
            pltpu.VMEM((ring, tok, HEAD_DIM), BF16),
            pltpu.VMEM((ring, tok, HEAD_DIM), BF16),
            pltpu.VMEM((ring,) + block, F32),
            pltpu.VMEM((half - 1,) + block, BF16),
            pltpu.VMEM((half - 1,) + block, BF16),
            pltpu.VMEM((half - 1,) + block, BF16),
            pltpu.VMEM((half - 1,) + block, BF16),
            pltpu.VMEM((batch,) + block, BF16),
            pltpu.VMEM(block, BF16),
            pltpu.VMEM(block, BF16),
            dma((7,)),
            dma((5,)),
            dma((5,)),
            dma((2, half + 1, 2)),
            dma((2, half + 1, 2)),
            dma((cols,)),
            dma((cols,)),
            dma((cols,)),
            dma((cols,)),
            dma((2, ring // 4)),
            dma((2, half - 1)),
            dma((2, half - 1)),
            dma((2,)),
            dma((2,)),
            dma((W_PIECES,)),
            dma((W_PIECES,)),
        ],
        compiler_params=pltpu.CompilerParams(
            collective_id=0, has_side_effects=True, vmem_limit_bytes=VMEM_BYTES
        ),
        cost_estimate=pl.CostEstimate(
            flops=4 * 10**9, bytes_accessed=8 * 10**6, transcendentals=4 * 10**5
        ),
    )(
        slab_queue.reshape(batch, tok, width), levels, jnp.swapaxes(mod_table, 0, 1),
        w_qkv.reshape(width, 3 * HEAD_DIM), q_gain, k_gain, w_out,
    ).reshape(batch, 1, tok, width)


def solution(mesh):
    placed = (
        P(None, "tm", "space", None),
        P(),
        P(),
        P(None, "tm", None),
        P("tm", None),
        P("tm", None),
        P("tm", None),
    )
    return jax.shard_map(
        body, mesh=mesh, in_specs=placed, out_specs=P(None, "tm", "space", None), check_vma=False
    )
```

```python
import functools
import math

import jax
import jax.numpy as jnp
from jax import lax
from jax.experimental import pallas as pl
from jax.experimental.pallas import tpu as pltpu
from jax.sharding import PartitionSpec as P

HEAD_DIM = 128
W_PIECES = 8
VMEM_BYTES = 64 * 1024 * 1024 - 192 * 1024
MESH = pl.DeviceIdType.MESH
F32 = jnp.float32
BF16 = jnp.bfloat16


def dot_t(left, right):
    return lax.dot_general(left, right, (((1,), (1,)), ((), ())), preferred_element_type=F32)


def head_norm(values, gain):
    values = values.astype(F32)
    factor = lax.rsqrt(jnp.mean(jnp.square(values), axis=-1, keepdims=True) + 1e-06)
    return (values * factor * gain).astype(BF16)


def kernel(
    ring, cols,
    slab_in, levels_in, mod_in, w_qkv, q_gain, k_gain, w_out,
    out,
    slab, levels, mod, rows_of, acc, mod_send, tokens, w_buf, gq, gk, wo, qkv, sp_in, sp_out, sp_back, tmp_out, comb,
    x_own, x_send, x_recv, part, r_send, r_recv, l_send, l_recv, prev, fin_send, fin_recv,
    loc_sem, pair_send, pair_recv, ag_send, ag_recv, aa_send, aa_recv, rt_send, rt_recv,
    x_sems, rs_send, rs_recv, misc_send, misc_recv, w_send, w_recv,
):
    half = ring // 2
    slabs = ring
    tok, width = slab.shape[1], slab.shape[2]
    piece = width // W_PIECES
    tm, space = lax.axis_index("tm"), lax.axis_index("space")
    core, z_lo = lax.rem(tm, 2), lax.div(tm, 2)
    me, z_hi = lax.div(space, 2), lax.rem(space, 2)
    z = z_hi * half + z_lo
    other = 1 - core
    inv_root = 1.0 / math.sqrt(HEAD_DIM)

    def mod_ring(value):
        return lax.rem(value + ring, ring)

    def device(plane, of_core, column):
        return (lax.rem(plane, half) * 2 + of_core, column * 2 + lax.div(plane, half))

    right = device(mod_ring(z + 1), core, me)
    left = device(mod_ring(z - 1), core, me)
    partner = device(z, other, me)
    across = device(mod_ring(z + half), core, me)
    tm_next = (lax.rem(tm + 1, slabs), space)
    tm_far = (lax.rem(tm + jnp.where(core == 1, 1, slabs - 1), slabs), space)

    def remote(src, dst, send_sem, recv_sem, target):
        return pltpu.make_async_remote_copy(
            src_ref=src, dst_ref=dst, send_sem=send_sem, recv_sem=recv_sem,
            device_id=target, device_id_type=MESH,
        )

    barrier = pltpu.get_barrier_semaphore()
    for target in (right, left, partner, across, tm_far):
        pl.semaphore_signal(barrier, inc=1, device_id=target, device_id_type=MESH)

    def greet(step, carry):
        column = lax.rem(me + step, cols)
        pl.semaphore_signal(barrier, inc=1, device_id=device(z, core, column), device_id_type=MESH)
        return carry

    lax.fori_loop(1, cols, greet, 0)

    own_head = core == z_hi
    fetch_levels = pltpu.make_async_copy(levels_in, levels, loc_sem.at[2])
    fetch_mod = pltpu.make_async_copy(mod_in, mod, loc_sem.at[3])
    fetch_slab = pltpu.make_async_copy(slab_in, slab, loc_sem.at[4])
    local_w = pltpu.make_async_copy(w_qkv, w_buf, loc_sem.at[0])
    local_wo = pltpu.make_async_copy(w_out, wo.at[core], loc_sem.at[1])
    local_gq = pltpu.make_async_copy(q_gain, gq, loc_sem.at[5])
    local_gk = pltpu.make_async_copy(k_gain, gk, loc_sem.at[6])
    fetch_levels.start()
    fetch_mod.start()
    fetch_slab.start()

    @pl.when(own_head)
    def _():
        local_gq.start()
        local_gk.start()
        local_w.start()

    local_wo.start()
    fetch_levels.wait()
    fetch_mod.wait()

    tm_before = lax.rem(tm + slabs - 1, slabs)
    pick_row = lax.broadcasted_iota(jnp.int32, (16, mod.shape[1]), 0)
    pick_col = lax.broadcasted_iota(jnp.int32, (16, mod.shape[1]), 1)
    hot = jnp.zeros((16, mod.shape[1]), F32)
    for at, (batch, of_slab) in enumerate(((0, tm), (1, tm), (0, tm_before), (1, tm_before))):
        hot = jnp.where((pick_row == at) & (pick_col == levels[batch, of_slab]), 1.0, hot)
    for kind in range(3):
        picked = jnp.dot(hot.astype(BF16), mod[kind], preferred_element_type=F32)
        for at in range(4):
            rows_of[kind, at] = picked[at : at + 1]

    def modulate(batch):
        values = slab[batch].astype(F32)
        centre = jnp.mean(values, axis=-1, keepdims=True)
        moved = values - centre
        spread = jnp.mean(jnp.square(moved), axis=-1, keepdims=True)
        normed = moved * lax.rsqrt(spread + 1e-06)
        return (normed * (1.0 + rows_of[1, batch]) + rows_of[0, batch]).astype(BF16)

    fetch_slab.wait()
    mod_send[...] = modulate(other)
    tokens[z * 2 + core] = modulate(core)
    pl.semaphore_wait(barrier, 5 + cols - 1)

    def gather_copy(way, step, t, origin):
        slot = origin * 2 + t
        return remote(
            tokens.at[slot], tokens.at[slot], ag_send.at[way, step, t], ag_recv.at[way, step, t],
            (right, left)[way],
        )

    to_pair = remote(mod_send, tokens.at[z * 2 + core], pair_send.at[0], pair_recv.at[0], partner)
    to_pair.start()
    for way in (0, 1):
        gather_copy(way, 1, core, z).start()
    from_pair = remote(mod_send, tokens.at[z * 2 + other], pair_send.at[0], pair_recv.at[0], partner)
    from_pair.wait_recv()
    for way in (0, 1):
        gather_copy(way, 1, other, z).start()

    def give_w(at):
        rows = pl.ds(at * piece, piece)
        return remote(w_qkv.at[rows], w_buf.at[rows], w_send.at[at], w_recv.at[at], partner)

    give_gq = remote(q_gain, gq, pair_send.at[2], pair_recv.at[2], partner)
    give_gk = remote(k_gain, gk, pair_send.at[3], pair_recv.at[3], partner)
    give_wo = remote(w_out, wo.at[core], pair_send.at[4], pair_recv.at[4], partner)
    take_wo = remote(w_out, wo.at[other], pair_send.at[4], pair_recv.at[4], partner)
    pass_slab = remote(slab, prev, misc_send.at[0], misc_recv.at[0], tm_next)

    @pl.when(own_head)
    def _():
        give_gq.start()
        give_gk.start()

    def slab_copy(column, source):
        return remote(
            qkv.at[:, column], sp_in.at[source], aa_send.at[column], aa_recv.at[source],
            device(z, core, column),
        )

    def send_pair(q_lo):
        for t in (0, 1):
            column = q_lo * 2 + t

            @pl.when(column != me)
            def _():
                slab_copy(column, me).start()

    def planes_of(step):
        return mod_ring(z - step), jnp.where(step == half, z, mod_ring(z + step))

    def project_piece(pair, at):
        @pl.when(pair == 0)
        def _():
            @pl.when(own_head)
            def _():
                @pl.when(at == 0)
                def _():
                    local_w.wait()
                    local_gq.wait()
                    local_gk.wait()

            @pl.when(jnp.logical_not(own_head))
            def _():
                give_w(at).wait_recv()

                @pl.when(at == 0)
                def _():
                    give_gq.wait_recv()
                    give_gk.wait_recv()

        span = pl.ds(pl.multiple_of(at * piece, piece), piece)
        blocks = []
        for ahead in (1, 2):
            for plane in planes_of(2 * pair + ahead):
                blocks.append(tokens[pl.ds(plane * 2, 2), :, span].reshape(2 * tok, piece))
        product = jnp.dot(
            jnp.concatenate(blocks, axis=0), w_buf[span, :], preferred_element_type=F32
        )

        @pl.when(at == 0)
        def _():
            acc[...] = product

        @pl.when(at > 0)
        def _():
            acc[...] += product

    def finish_pair(pair):
        projected = acc[...].astype(BF16)
        queries = head_norm(projected[:, :HEAD_DIM], gq[...])
        keys = head_norm(projected[:, HEAD_DIM : 2 * HEAD_DIM], gk[...])
        values = projected[:, 2 * HEAD_DIM :]
        at = 0
        for ahead in (1, 2):
            for plane in planes_of(2 * pair + ahead):
                hi, lo = lax.div(plane, half), lax.rem(plane, half)
                for t in (0, 1):
                    cut = slice(at, at + tok)
                    qkv[hi, lo * 2 + t, :, 0:HEAD_DIM] = queries[cut]
                    qkv[hi, lo * 2 + t, :, HEAD_DIM : 2 * HEAD_DIM] = keys[cut]
                    qkv[hi, lo * 2 + t, :, 2 * HEAD_DIM :] = values[cut]
                    at += tok
        for ahead in (1, 2):
            step = 2 * pair + ahead
            plane_a, plane_b = planes_of(step)

            @pl.when(step >= half // 2)
            def _():
                send_pair(lax.rem(plane_a, half))

            @pl.when((step > half // 2) & (step < half))
            def _():
                send_pair(lax.rem(plane_b, half))

    def gather_step(step, carry):
        plane_a = mod_ring(z - step)
        plane_b = mod_ring(z + step)
        pair = lax.div(step - 1, 2) - 1
        at = lax.rem(step - 1, 2) * 4
        for turn in (0, 1):
            t = core if turn == 0 else other
            for way, origin in ((0, plane_a), (1, plane_b)):

                @pl.when((step < half) | (t == way))
                def _():
                    gather_copy(way, step, t, origin).wait_recv()

                @pl.when((step < half - 1) | ((step == half - 1) & (t == way)))
                def _():
                    gather_copy(way, step + 1, t, origin).start()

                @pl.when(own_head & (step < 3))
                def _():
                    give_w(at + turn * 2 + way).start()

                @pl.when(step >= 3)
                def _():
                    project_piece(pair, at + turn * 2 + way)

        @pl.when((step >= 3) & (lax.rem(step, 2) == 0))
        def _():
            finish_pair(pair)

        @pl.when(step == 3)
        def _():
            give_wo.start()

        return carry

    lax.fori_loop(1, half + 1, gather_step, 0)
    if half < 3:
        give_wo.start()

    def last_piece(at, carry):
        project_piece(half // 2 - 1, at)
        return carry

    lax.fori_loop(0, W_PIECES, last_piece, 0)
    finish_pair(half // 2 - 1)
    pass_slab.start()
    sp_in[me] = qkv[:, me]

    rows_t = slabs * tok
    at_row = lax.broadcasted_iota(jnp.int32, (rows_t, rows_t), 0) & (tok - 1)
    at_col = lax.broadcasted_iota(jnp.int32, (rows_t, rows_t), 1) & (tok - 1)
    same = at_row == at_col
    for hi in (0, 1):
        queries = qkv[hi, :, :, 0:HEAD_DIM].reshape(rows_t, HEAD_DIM)
        keys = qkv[hi, :, :, HEAD_DIM : 2 * HEAD_DIM].reshape(rows_t, HEAD_DIM)
        values = qkv[hi, :, :, 2 * HEAD_DIM :].reshape(rows_t, HEAD_DIM)
        scores = jnp.where(same, dot_t(queries, keys) * inv_root, -jnp.inf)
        weights = jnp.exp(scores - jnp.max(scores, axis=-1, keepdims=True))
        total = jnp.sum(weights, axis=-1, keepdims=True)
        mixed = jnp.dot(weights.astype(BF16), values, preferred_element_type=F32) / total
        tmp_out[hi] = mixed.reshape(slabs, tok, HEAD_DIM)

    def await_slab(step, carry):
        slab_copy(me, lax.rem(me + step, cols)).wait_recv()
        return carry

    lax.fori_loop(1, cols, await_slab, 0)

    def back_copy(column, of_slab):
        return remote(
            sp_out.at[column], sp_back.at[:, of_slab], rt_send.at[column], rt_recv.at[of_slab],
            device(z, core, column),
        )

    group = 4
    rows_s = group * 2 * tok

    def spatial_step(step, carry):
        keys = sp_in[:, :, :, HEAD_DIM : 2 * HEAD_DIM].reshape(cols * 2 * tok, HEAD_DIM)
        values = sp_in[:, :, :, 2 * HEAD_DIM :].reshape(cols * 2 * tok, HEAD_DIM)
        queries = sp_in[pl.ds(step * group, group), :, :, 0:HEAD_DIM].reshape(rows_s, HEAD_DIM)
        scores = dot_t(queries, keys) * inv_root
        weights = jnp.exp(scores - jnp.max(scores, axis=-1, keepdims=True))
        total = jnp.sum(weights, axis=-1, keepdims=True)
        mixed = jnp.dot(weights.astype(BF16), values, preferred_element_type=F32) / total
        sp_out[pl.ds(step * group, group)] = mixed.astype(BF16).reshape(group, 2, tok, HEAD_DIM)
        for at in range(group):
            column = step * group + at

            @pl.when(column != me)
            def _():
                back_copy(column, me).start()

        return carry

    lax.fori_loop(0, cols // group, spatial_step, 0)
    sp_back[:, me] = sp_out[me]
    local_wo.wait()
    take_wo.wait_recv()

    def await_back(step, carry):
        back_copy(me, lax.rem(me + step, cols)).wait_recv()
        return carry

    lax.fori_loop(1, cols, await_back, 0)
    comb[...] = (sp_back[...].astype(F32) + tmp_out[...]).astype(BF16)

    def fill(dst, plane):
        def one(at, carry):
            step = lax.div(at, 2)
            block = jnp.where(lax.rem(at, 2) == 0, ring - 1 - step, step)
            place = lax.rem(2 * plane + 2 * ring - (half - 1) + block, 2 * ring)
            from_slab = lax.rem(lax.rem(place, slabs) + slabs - 1, slabs)
            dst[at] = comb[lax.div(place, slabs), from_slab]
            return carry

        lax.fori_loop(0, ring, one, 0)

    def swap(at):
        rows = pl.ds(at * 4, 4)
        return remote(x_send.at[rows], x_recv.at[rows], x_sems.at[0, at], x_sems.at[1, at], across)

    swaps = ring // 4
    fill(x_send, mod_ring(z + half))
    for at in range(swaps):
        swap(at).start()
    fill(x_own, z)
    chunk = width // 4
    rows_p = ring * tok
    for at in range(0, width, chunk):
        product = jnp.dot(
            x_own[...].reshape(rows_p, HEAD_DIM), wo[z_hi, :, at : at + chunk],
            preferred_element_type=F32,
        )
        part[:, :, at : at + chunk] = product.reshape(ring, tok, chunk)

    def sum_copy(way, step):
        mine, theirs, target = ((r_send, r_recv, right), (l_send, l_recv, left))[way]
        return remote(
            mine.at[step], theirs.at[step], rs_send.at[way, step], rs_recv.at[way, step], target
        )

    def sum_step(step, carry):
        @pl.when(lax.rem(step, 2) == 0)
        def _():
            swap(lax.div(step, 2)).wait_recv()
            rows = pl.ds(step * 2, 4)
            for at in range(0, width, chunk):
                product = jnp.dot(
                    x_recv[rows].reshape(4 * tok, HEAD_DIM), wo[1 - z_hi, :, at : at + chunk],
                    preferred_element_type=F32,
                )
                part[rows, :, at : at + chunk] += product.reshape(4, tok, chunk)

        for way, mine, theirs in ((0, r_send, r_recv), (1, l_send, l_recv)):
            block = step * 2 + way

            @pl.when(step < 2)
            def _():
                mine[step] = part[block].astype(BF16)

            @pl.when(step >= 2)
            def _():
                sum_copy(way, step - 2).wait_recv()
                mine[step] = (part[block] + theirs[step - 2].astype(F32)).astype(BF16)

            sum_copy(way, step).start()
        return carry

    lax.fori_loop(0, half - 1, sum_step, 0)
    if half > 2:
        for way in (0, 1):
            sum_copy(way, half - 3).wait_recv()
    for way in (0, 1):
        sum_copy(way, half - 2).wait_recv()

    def total_of(t):
        if half > 2:
            return (
                part[ring - 1 - t]
                + r_recv[half - 2 - t].astype(F32)
                + l_recv[half - 3 + t].astype(F32)
            )
        from_side = jnp.where(t == 0, r_recv[0].astype(F32), l_recv[0].astype(F32))
        return part[ring - 1 - t] + from_side

    fin_send[...] = total_of(other).astype(BF16)
    give_fin = remote(fin_send, fin_recv, misc_send.at[1], misc_recv.at[1], partner)
    give_fin.start()
    pass_slab.wait_recv()

    def attend(batch, projection):
        gate = rows_of[2, 2 + batch]
        out[batch] = (prev[batch].astype(F32) + gate * projection).astype(BF16)

    attend(core, total_of(core))
    give_fin.wait_recv()
    attend(other, fin_recv[...].astype(F32))

    to_pair.wait_send()

    @pl.when(own_head)
    def _():
        def one(at, inner):
            give_w(at).wait_send()
            return inner

        lax.fori_loop(0, W_PIECES, one, 0)
        give_gq.wait_send()
        give_gk.wait_send()

    give_wo.wait_send()
    pass_slab.wait_send()
    give_fin.wait_send()
    for at in range(swaps):
        swap(at).wait_send()

    def drain_gather(step, carry):
        for way in (0, 1):
            for t in (0, 1):

                @pl.when((step < half) | (t == way))
                def _():
                    gather_copy(way, step, t, z).wait_send()

        return carry

    lax.fori_loop(1, half + 1, drain_gather, 0)

    def drain_plane(step, carry):
        column = lax.rem(me + step, cols)
        slab_copy(column, me).wait_send()
        back_copy(column, me).wait_send()
        return carry

    lax.fori_loop(1, cols, drain_plane, 0)

    def drain_sum(step, carry):
        for way in (0, 1):
            sum_copy(way, step).wait_send()
        return carry

    lax.fori_loop(0, half - 1, drain_sum, 0)


def body(slab_queue, levels, mod_table, w_qkv, q_gain, k_gain, w_out):
    batch, _, tok, width = slab_queue.shape
    ring = lax.axis_size("tm")
    cols = lax.axis_size("space") // 2
    half = ring // 2
    vmem = pl.BlockSpec(memory_space=pltpu.VMEM)
    hbm = pl.BlockSpec(memory_space=pltpu.HBM)
    dma = pltpu.SemaphoreType.DMA
    block = (tok, width)
    return pl.pallas_call(
        functools.partial(kernel, ring, cols),
        out_shape=jax.ShapeDtypeStruct((batch, tok, width), BF16),
        in_specs=[hbm] * 7,
        out_specs=vmem,
        scratch_shapes=[
            pltpu.VMEM((batch,) + block, BF16),
            pltpu.SMEM(levels.shape, jnp.int32),
            pltpu.VMEM((3, mod_table.shape[0], width), BF16),
            pltpu.VMEM((3, 4, 1, width), F32),
            pltpu.VMEM((8 * tok, 3 * HEAD_DIM), F32),
            pltpu.VMEM(block, BF16),
            pltpu.VMEM((2 * ring,) + block, BF16),
            pltpu.VMEM((width, 3 * HEAD_DIM), BF16),
            pltpu.VMEM((1, HEAD_DIM), F32),
            pltpu.VMEM((1, HEAD_DIM), F32),
            pltpu.VMEM((2, HEAD_DIM, width), BF16),
            pltpu.VMEM((2, ring, tok, 3 * HEAD_DIM), BF16),
            pltpu.VMEM((cols, 2, tok, 3 * HEAD_DIM), BF16),
            pltpu.VMEM((cols, 2, tok, HEAD_DIM), BF16),
            pltpu.VMEM((2, ring, tok, HEAD_DIM), BF16),
            pltpu.VMEM((2, ring, tok, HEAD_DIM), F32),
            pltpu.VMEM((2, ring, tok, HEAD_DIM), BF16),
            pltpu.VMEM((ring, tok, HEAD_DIM), BF16),
            pltpu.VMEM((ring, tok, HEAD_DIM), BF16),
            pltpu.VMEM((ring, tok, HEAD_DIM), BF16),
            pltpu.VMEM((ring,) + block, F32),
            pltpu.VMEM((half - 1,) + block, BF16),
            pltpu.VMEM((half - 1,) + block, BF16),
            pltpu.VMEM((half - 1,) + block, BF16),
            pltpu.VMEM((half - 1,) + block, BF16),
            pltpu.VMEM((batch,) + block, BF16),
            pltpu.VMEM(block, BF16),
            pltpu.VMEM(block, BF16),
            dma((7,)),
            dma((5,)),
            dma((5,)),
            dma((2, half + 1, 2)),
            dma((2, half + 1, 2)),
            dma((cols,)),
            dma((cols,)),
            dma((cols,)),
            dma((cols,)),
            dma((2, ring // 4)),
            dma((2, half - 1)),
            dma((2, half - 1)),
            dma((2,)),
            dma((2,)),
            dma((W_PIECES,)),
            dma((W_PIECES,)),
        ],
        compiler_params=pltpu.CompilerParams(
            collective_id=0, has_side_effects=True, vmem_limit_bytes=VMEM_BYTES
        ),
        cost_estimate=pl.CostEstimate(
            flops=4 * 10**9, bytes_accessed=8 * 10**6, transcendentals=4 * 10**5
        ),
    )(
        slab_queue.reshape(batch, tok, width), levels, jnp.swapaxes(mod_table, 0, 1),
        w_qkv.reshape(width, 3 * HEAD_DIM), q_gain, k_gain, w_out,
    ).reshape(batch, 1, tok, width)


def solution(mesh):
    placed = (
        P(None, "tm", "space", None),
        P(),
        P(),
        P(None, "tm", None),
        P("tm", None),
        P("tm", None),
        P("tm", None),
    )
    return jax.shard_map(
        body, mesh=mesh, in_specs=placed, out_specs=P(None, "tm", "space", None), check_vma=False
    )
```

```python
import functools
import math

import jax
import jax.numpy as jnp
from jax import lax
from jax.experimental import pallas as pl
from jax.experimental.pallas import tpu as pltpu
from jax.sharding import PartitionSpec as P

HEAD_DIM = 128
W_PIECES = 12
SUM_PIECES = 4
VMEM_BYTES = 64 * 1024 * 1024 - 192 * 1024
MESH = pl.DeviceIdType.MESH
F32 = jnp.float32
BF16 = jnp.bfloat16


def dot_t(left, right):
    return lax.dot_general(left, right, (((1,), (1,)), ((), ())), preferred_element_type=F32)


def head_norm(values, gain):
    values = values.astype(F32)
    factor = lax.rsqrt(jnp.mean(jnp.square(values), axis=-1, keepdims=True) + 1e-06)
    return (values * factor * gain).astype(BF16)


def kernel(
    ring, cols,
    slab_in, levels_in, mod_in, w_qkv, q_gain, k_gain, w_out,
    out,
    slab, levels, mod, rows_of, mod_send, tokens, w_buf, gq, gk, wo, qkv, sp_in, sp_out, sp_back, tmp_out, comb,
    x_send, x_recv, part, r_send, r_recv, l_send, l_recv, prev, fin_send, fin_recv,
    loc_sem, pair_send, pair_recv, ag_send, ag_recv, aa_send, aa_recv, rt_send, rt_recv,
    xs_send, xs_recv, rs_send, rs_recv, misc_send, misc_recv, w_send, w_recv,
    wz_send, wz_recv, wp_send, wp_recv, wd_sem,
):
    half = ring // 2
    slabs = ring
    tok, width = slab.shape[1], slab.shape[2]
    piece = width // W_PIECES
    tm, space = lax.axis_index("tm"), lax.axis_index("space")
    core, z_lo = lax.rem(tm, 2), lax.div(tm, 2)
    me, z_hi = lax.div(space, 2), lax.rem(space, 2)
    z = z_hi * half + z_lo
    other = 1 - core
    inv_root = 1.0 / math.sqrt(HEAD_DIM)

    def mod_ring(value):
        return lax.rem(value + ring, ring)

    def device(plane, of_core, column):
        return (lax.rem(plane, half) * 2 + of_core, column * 2 + lax.div(plane, half))

    right = device(mod_ring(z + 1), core, me)
    left = device(mod_ring(z - 1), core, me)
    partner = device(z, other, me)
    tm_next = (lax.rem(tm + 1, slabs), space)
    tm_far = (lax.rem(tm + jnp.where(core == 1, 1, slabs - 1), slabs), space)

    def remote(src, dst, send_sem, recv_sem, target):
        return pltpu.make_async_remote_copy(
            src_ref=src, dst_ref=dst, send_sem=send_sem, recv_sem=recv_sem,
            device_id=target, device_id_type=MESH,
        )

    barrier = pltpu.get_barrier_semaphore()
    for target in (right, left, partner, tm_far):
        pl.semaphore_signal(barrier, inc=1, device_id=target, device_id_type=MESH)

    def greet(step, carry):
        column = lax.rem(me + step, cols)
        pl.semaphore_signal(barrier, inc=1, device_id=device(z, core, column), device_id_type=MESH)
        return carry

    lax.fori_loop(1, cols, greet, 0)

    def greet_class(step, carry):
        target = device(mod_ring(z + 2 * step), core, me)
        pl.semaphore_signal(barrier, inc=1, device_id=target, device_id_type=MESH)
        return carry

    lax.fori_loop(1, half, greet_class, 0)

    own_head = core == z_hi
    fetch_levels = pltpu.make_async_copy(levels_in, levels, loc_sem.at[2])
    fetch_mod = pltpu.make_async_copy(mod_in, mod, loc_sem.at[3])
    fetch_slab = pltpu.make_async_copy(slab_in, slab, loc_sem.at[4])
    local_w = pltpu.make_async_copy(w_qkv, w_buf, loc_sem.at[0])
    local_wo = pltpu.make_async_copy(w_out, wo.at[0, core], loc_sem.at[1])
    local_gq = pltpu.make_async_copy(q_gain, gq, loc_sem.at[5])
    local_gk = pltpu.make_async_copy(k_gain, gk, loc_sem.at[6])
    fetch_levels.start()
    fetch_mod.start()
    fetch_slab.start()

    @pl.when(own_head)
    def _():
        local_gq.start()
        local_gk.start()
        local_w.start()

    local_wo.start()
    fetch_levels.wait()
    fetch_mod.wait()

    tm_before = lax.rem(tm + slabs - 1, slabs)
    pick_row = lax.broadcasted_iota(jnp.int32, (16, mod.shape[1]), 0)
    pick_col = lax.broadcasted_iota(jnp.int32, (16, mod.shape[1]), 1)
    hot = jnp.zeros((16, mod.shape[1]), F32)
    for at, (batch, of_slab) in enumerate(((0, tm), (1, tm), (0, tm_before), (1, tm_before))):
        hot = jnp.where((pick_row == at) & (pick_col == levels[batch, of_slab]), 1.0, hot)
    for kind in range(3):
        picked = jnp.dot(hot.astype(BF16), mod[kind], preferred_element_type=F32)
        for at in range(4):
            rows_of[kind, at] = picked[at : at + 1]

    def modulate(batch):
        values = slab[batch].astype(F32)
        centre = jnp.mean(values, axis=-1, keepdims=True)
        moved = values - centre
        spread = jnp.mean(jnp.square(moved), axis=-1, keepdims=True)
        normed = moved * lax.rsqrt(spread + 1e-06)
        return (normed * (1.0 + rows_of[1, batch]) + rows_of[0, batch]).astype(BF16)

    fetch_slab.wait()
    mod_send[...] = modulate(other)
    tokens[z * 2 + core] = modulate(core)
    pl.semaphore_wait(barrier, 4 + cols - 1 + half - 1)

    def gather_copy(way, step, t, origin):
        slot = origin * 2 + t
        return remote(
            tokens.at[slot], tokens.at[slot], ag_send.at[way, step, t], ag_recv.at[way, step, t],
            (right, left)[way],
        )

    to_pair = remote(mod_send, tokens.at[z * 2 + core], pair_send.at[0], pair_recv.at[0], partner)
    to_pair.start()
    for way in (0, 1):
        gather_copy(way, 1, core, z).start()
    from_pair = remote(mod_send, tokens.at[z * 2 + other], pair_send.at[0], pair_recv.at[0], partner)
    from_pair.wait_recv()
    for way in (0, 1):
        gather_copy(way, 1, other, z).start()

    def give_w(at):
        rows = pl.ds(at * piece, piece)
        return remote(w_qkv.at[rows], w_buf.at[rows], w_send.at[at], w_recv.at[at], partner)

    give_gq = remote(q_gain, gq, pair_send.at[2], pair_recv.at[2], partner)
    give_gk = remote(k_gain, gk, pair_send.at[3], pair_recv.at[3], partner)
    give_wo = remote(w_out, wo.at[0, core], pair_send.at[4], pair_recv.at[4], partner)
    take_wo = remote(w_out, wo.at[0, other], pair_send.at[4], pair_recv.at[4], partner)
    pass_slab = remote(slab, prev, misc_send.at[0], misc_recv.at[0], tm_next)

    @pl.when(own_head)
    def _():
        give_gq.start()
        give_gk.start()

    pairs = half // 2
    rows_w = 2 * HEAD_DIM // cols
    cut_rows = pl.ds(pl.multiple_of(lax.div(me, 2) * rows_w, rows_w), rows_w)
    cut_cols = pl.ds(pl.multiple_of(lax.rem(me, 2) * (width // 2), width // 2), width // 2)

    def plane_piece(at):
        apart = 2 * at if 4 * at < half else 2 * at - half
        if 4 * at == half:
            apart = jnp.where(core == 0, half // 2, -(half // 2))
        return remote(
            w_out.at[cut_rows, cut_cols], wo.at[at, core, cut_rows, cut_cols],
            wz_send.at[at], wz_recv.at[at], device(mod_ring(z - apart), core, me),
        )

    def spread_piece(column, source):
        rows = pl.ds(pl.multiple_of(lax.div(source, 2) * rows_w, rows_w), rows_w)
        span = pl.ds(pl.multiple_of(lax.rem(source, 2) * (width // 2), width // 2), width // 2)
        piece_of = wo.at[1:pairs, core, rows, span]
        return remote(
            piece_of, piece_of, wp_send.at[column], wp_recv.at[source], device(z, core, column)
        )

    def pair_wo(of_core):
        block = wo.at[1:pairs, of_core]
        return remote(block, block, wd_sem.at[0], wd_sem.at[1], partner)

    for at in range(1, pairs):
        plane_piece(at).start()

    def slab_copy(column, source):
        return remote(
            qkv.at[:, column], sp_in.at[source], aa_send.at[column], aa_recv.at[source],
            device(z, core, column),
        )

    def send_pair(q_lo):
        for t in (0, 1):
            column = q_lo * 2 + t

            @pl.when(column != me)
            def _():
                slab_copy(column, me).start()

    first_dot = max(half // 2, 2)
    per_step = W_PIECES // (first_dot - 1)

    def gather_step(step, carry):
        plane_a = mod_ring(z - step)
        plane_b = mod_ring(z + step)
        for turn in (0, 1):
            t = core if turn == 0 else other
            for way, origin in ((0, plane_a), (1, plane_b)):

                @pl.when((step < half) | (t == way))
                def _():
                    gather_copy(way, step, t, origin).wait_recv()

                @pl.when((step < half - 1) | ((step == half - 1) & (t == way)))
                def _():
                    gather_copy(way, step + 1, t, origin).start()

        if pairs > 1:

            @pl.when(step == 2)
            def _():
                for at in range(1, pairs):
                    plane_piece(at).wait_recv()

                def spread(ahead, inner):
                    spread_piece(lax.rem(me + ahead, cols), me).start()
                    return inner

                lax.fori_loop(1, cols, spread, 0)

        @pl.when(own_head & (step < first_dot))
        def _():
            def one(at, inner):
                give_w(at).start()
                return inner

            lax.fori_loop((step - 1) * per_step, step * per_step, one, 0)

        @pl.when(step == first_dot)
        def _():
            give_wo.start()

            @pl.when(own_head)
            def _():
                local_w.wait()
                local_gq.wait()
                local_gk.wait()

            @pl.when(jnp.logical_not(own_head))
            def _():
                def one(at, inner):
                    give_w(at).wait_recv()
                    return inner

                lax.fori_loop(0, W_PIECES, one, 0)
                give_gq.wait_recv()
                give_gk.wait_recv()

        def reach(at):
            return jnp.where(at < first_dot, 0, jnp.minimum(2 * (at - first_dot + 1), at))

        lax.fori_loop(reach(step - 1) + 1, reach(step) + 1, project_step, 0)
        return carry

    def project_step(step, carry):
        plane_a = mod_ring(z - step)
        plane_b = mod_ring(z + step)
        second = jnp.where(step == half, z, plane_b)
        rows_a = tokens[pl.ds(plane_a * 2, 2)].reshape(2 * tok, width)
        rows_b = tokens[pl.ds(second * 2, 2)].reshape(2 * tok, width)
        rows = jnp.concatenate([rows_a, rows_b], axis=0)
        projected = jnp.dot(rows, w_buf[...], preferred_element_type=F32).astype(BF16)
        queries = head_norm(projected[:, :HEAD_DIM], gq[...])
        keys = head_norm(projected[:, HEAD_DIM : 2 * HEAD_DIM], gk[...])
        values = projected[:, 2 * HEAD_DIM :]
        for at, plane in ((0, plane_a), (1, second)):
            hi, lo = lax.div(plane, half), lax.rem(plane, half)
            for t in (0, 1):
                cut = slice((at * 2 + t) * tok, (at * 2 + t + 1) * tok)
                qkv[hi, lo * 2 + t, :, 0:HEAD_DIM] = queries[cut]
                qkv[hi, lo * 2 + t, :, HEAD_DIM : 2 * HEAD_DIM] = keys[cut]
                qkv[hi, lo * 2 + t, :, 2 * HEAD_DIM :] = values[cut]

        @pl.when(step >= half // 2)
        def _():
            send_pair(lax.rem(plane_a, half))

        @pl.when((step > half // 2) & (step < half))
        def _():
            send_pair(lax.rem(plane_b, half))

        return carry

    lax.fori_loop(1, half + 1, gather_step, 0)
    pass_slab.start()
    sp_in[me] = qkv[:, me]
    if pairs > 1:

        def await_spread(ahead, carry):
            spread_piece(me, lax.rem(me + ahead, cols)).wait_recv()
            return carry

        lax.fori_loop(1, cols, await_spread, 0)
        pair_wo(core).start()

    rows_t = slabs * tok
    at_row = lax.broadcasted_iota(jnp.int32, (rows_t, rows_t), 0) & (tok - 1)
    at_col = lax.broadcasted_iota(jnp.int32, (rows_t, rows_t), 1) & (tok - 1)
    same = at_row == at_col
    for hi in (0, 1):
        queries = qkv[hi, :, :, 0:HEAD_DIM].reshape(rows_t, HEAD_DIM)
        keys = qkv[hi, :, :, HEAD_DIM : 2 * HEAD_DIM].reshape(rows_t, HEAD_DIM)
        values = qkv[hi, :, :, 2 * HEAD_DIM :].reshape(rows_t, HEAD_DIM)
        scores = jnp.where(same, dot_t(queries, keys) * inv_root, -jnp.inf)
        weights = jnp.exp(scores - jnp.max(scores, axis=-1, keepdims=True))
        total = jnp.sum(weights, axis=-1, keepdims=True)
        mixed = jnp.dot(weights.astype(BF16), values, preferred_element_type=F32) / total
        tmp_out[hi] = mixed.reshape(slabs, tok, HEAD_DIM)

    def await_slab(step, carry):
        slab_copy(me, lax.rem(me + step, cols)).wait_recv()
        return carry

    lax.fori_loop(1, cols, await_slab, 0)

    def back_copy(column, of_slab):
        return remote(
            sp_out.at[column], sp_back.at[:, of_slab], rt_send.at[column], rt_recv.at[of_slab],
            device(z, core, column),
        )

    group = 4
    rows_s = group * 2 * tok

    def spatial_step(step, carry):
        keys = sp_in[:, :, :, HEAD_DIM : 2 * HEAD_DIM].reshape(cols * 2 * tok, HEAD_DIM)
        values = sp_in[:, :, :, 2 * HEAD_DIM :].reshape(cols * 2 * tok, HEAD_DIM)
        queries = sp_in[pl.ds(step * group, group), :, :, 0:HEAD_DIM].reshape(rows_s, HEAD_DIM)
        scores = dot_t(queries, keys) * inv_root
        weights = jnp.exp(scores - jnp.max(scores, axis=-1, keepdims=True))
        total = jnp.sum(weights, axis=-1, keepdims=True)
        mixed = jnp.dot(weights.astype(BF16), values, preferred_element_type=F32) / total
        sp_out[pl.ds(step * group, group)] = mixed.astype(BF16).reshape(group, 2, tok, HEAD_DIM)
        for at in range(group):
            column = step * group + at

            @pl.when(column != me)
            def _():
                back_copy(column, me).start()

        return carry

    lax.fori_loop(0, cols // group, spatial_step, 0)
    sp_back[:, me] = sp_out[me]
    local_wo.wait()
    take_wo.wait_recv()

    def await_back(step, carry):
        back_copy(me, lax.rem(me + step, cols)).wait_recv()
        return carry

    lax.fori_loop(1, cols, await_back, 0)
    comb[...] = (sp_back[...].astype(F32) + tmp_out[...]).astype(BF16)

    def fill(dst, plane):
        for at, block in enumerate((3, 0, 1, 2)):
            place = lax.rem(2 * plane + 2 * ring - 1 + block, 2 * ring)
            from_slab = lax.rem(lax.rem(place, slabs) + slabs - 1, slabs)
            dst[at] = comb[lax.div(place, slabs), from_slab]

    def head_copy(step):
        plane = mod_ring(z + 2 * step)
        slot = lax.div(lax.rem(z_lo - lax.rem(plane, half) + half, half), 2)
        return remote(
            x_send.at[step], x_recv.at[slot, z_hi], xs_send.at[step], xs_recv.at[slot, z_hi],
            device(plane, core, me),
        )

    def send_heads(step, carry):
        fill(x_send.at[step], mod_ring(z + 2 * step))
        head_copy(step).start()
        return carry

    lax.fori_loop(1, half, send_heads, 0)
    fill(x_recv.at[0, z_hi], z)
    if pairs > 1:
        pair_wo(other).wait_recv()

    def await_heads(step, carry):
        plane = mod_ring(z + 2 * step)
        slot = lax.div(lax.rem(lax.rem(plane, half) - z_lo + half, half), 2)
        hi = lax.div(plane, half)
        remote(
            x_send.at[step], x_recv.at[slot, hi], xs_send.at[step], xs_recv.at[slot, hi],
            device(plane, core, me),
        ).wait_recv()
        return carry

    lax.fori_loop(1, half, await_heads, 0)

    def sum_copy(way, at):
        mine, theirs, target = ((r_send, r_recv, right), (l_send, l_recv, left))[way]
        span = slice(at * chunk, (at + 1) * chunk)
        return remote(
            mine.at[:, span], theirs.at[:, span], rs_send.at[way, at], rs_recv.at[way, at], target
        )

    chunk = width // SUM_PIECES
    rows_x = 4 * tok
    heads = jnp.concatenate(
        [x_recv[at // 2, at % 2].reshape(rows_x, HEAD_DIM) for at in range(half)], axis=1
    )
    for at in range(SUM_PIECES):
        span = slice(at * chunk, (at + 1) * chunk)
        weights = wo[:, :, :, span].reshape(half * HEAD_DIM, chunk)
        product = jnp.dot(heads, weights, preferred_element_type=F32)
        r_send[:, span] = product[0:tok].astype(BF16)
        sum_copy(0, at).start()
        l_send[:, span] = product[tok : 2 * tok].astype(BF16)
        sum_copy(1, at).start()
        part[0, :, span] = product[2 * tok : 3 * tok]
        part[1, :, span] = product[3 * tok :]
    for at in range(SUM_PIECES):
        for way in (0, 1):
            sum_copy(way, at).wait_recv()

    def total_of(t):
        from_side = jnp.where(t == 0, r_recv[...].astype(F32), l_recv[...].astype(F32))
        return part[t] + from_side

    fin_send[...] = total_of(other).astype(BF16)
    give_fin = remote(fin_send, fin_recv, misc_send.at[1], misc_recv.at[1], partner)
    give_fin.start()
    pass_slab.wait_recv()

    def attend(batch, projection):
        gate = rows_of[2, 2 + batch]
        out[batch] = (prev[batch].astype(F32) + gate * projection).astype(BF16)

    attend(core, total_of(core))
    give_fin.wait_recv()
    attend(other, fin_recv[...].astype(F32))

    to_pair.wait_send()

    @pl.when(own_head)
    def _():
        def one(at, inner):
            give_w(at).wait_send()
            return inner

        lax.fori_loop(0, W_PIECES, one, 0)
        give_gq.wait_send()
        give_gk.wait_send()

    give_wo.wait_send()
    pass_slab.wait_send()
    give_fin.wait_send()
    for at in range(1, pairs):
        plane_piece(at).wait_send()
    if pairs > 1:
        pair_wo(core).wait_send()

    def drain_gather(step, carry):
        for way in (0, 1):
            for t in (0, 1):

                @pl.when((step < half) | (t == way))
                def _():
                    gather_copy(way, step, t, z).wait_send()

        return carry

    lax.fori_loop(1, half + 1, drain_gather, 0)

    def drain_plane(step, carry):
        column = lax.rem(me + step, cols)
        slab_copy(column, me).wait_send()
        back_copy(column, me).wait_send()
        if pairs > 1:
            spread_piece(column, me).wait_send()
        return carry

    lax.fori_loop(1, cols, drain_plane, 0)

    def drain_heads(step, carry):
        head_copy(step).wait_send()
        return carry

    lax.fori_loop(1, half, drain_heads, 0)
    for at in range(SUM_PIECES):
        for way in (0, 1):
            sum_copy(way, at).wait_send()


def body(slab_queue, levels, mod_table, w_qkv, q_gain, k_gain, w_out):
    batch, _, tok, width = slab_queue.shape
    ring = lax.axis_size("tm")
    cols = lax.axis_size("space") // 2
    half = ring // 2
    vmem = pl.BlockSpec(memory_space=pltpu.VMEM)
    hbm = pl.BlockSpec(memory_space=pltpu.HBM)
    dma = pltpu.SemaphoreType.DMA
    block = (tok, width)
    return pl.pallas_call(
        functools.partial(kernel, ring, cols),
        out_shape=jax.ShapeDtypeStruct((batch, tok, width), BF16),
        in_specs=[hbm] * 7,
        out_specs=vmem,
        scratch_shapes=[
            pltpu.VMEM((batch,) + block, BF16),
            pltpu.SMEM(levels.shape, jnp.int32),
            pltpu.VMEM((3, mod_table.shape[0], width), BF16),
            pltpu.VMEM((3, 4, 1, width), F32),
            pltpu.VMEM(block, BF16),
            pltpu.VMEM((2 * ring,) + block, BF16),
            pltpu.VMEM((width, 3 * HEAD_DIM), BF16),
            pltpu.VMEM((1, HEAD_DIM), F32),
            pltpu.VMEM((1, HEAD_DIM), F32),
            pltpu.VMEM((half // 2, 2, HEAD_DIM, width), BF16),
            pltpu.VMEM((2, ring, tok, 3 * HEAD_DIM), BF16),
            pltpu.VMEM((cols, 2, tok, 3 * HEAD_DIM), BF16),
            pltpu.VMEM((cols, 2, tok, HEAD_DIM), BF16),
            pltpu.VMEM((2, ring, tok, HEAD_DIM), BF16),
            pltpu.VMEM((2, ring, tok, HEAD_DIM), F32),
            pltpu.VMEM((2, ring, tok, HEAD_DIM), BF16),
            pltpu.VMEM((half, 4, tok, HEAD_DIM), BF16),
            pltpu.VMEM((half // 2, 2, 4, tok, HEAD_DIM), BF16),
            pltpu.VMEM((2,) + block, F32),
            pltpu.VMEM(block, BF16),
            pltpu.VMEM(block, BF16),
            pltpu.VMEM(block, BF16),
            pltpu.VMEM(block, BF16),
            pltpu.VMEM((batch,) + block, BF16),
            pltpu.VMEM(block, BF16),
            pltpu.VMEM(block, BF16),
            dma((7,)),
            dma((5,)),
            dma((5,)),
            dma((2, half + 1, 2)),
            dma((2, half + 1, 2)),
            dma((cols,)),
            dma((cols,)),
            dma((cols,)),
            dma((cols,)),
            dma((half,)),
            dma((half // 2, 2)),
            dma((2, SUM_PIECES)),
            dma((2, SUM_PIECES)),
            dma((2,)),
            dma((2,)),
            dma((W_PIECES,)),
            dma((W_PIECES,)),
            dma((half // 2,)),
            dma((half // 2,)),
            dma((cols,)),
            dma((cols,)),
            dma((2,)),
        ],
        compiler_params=pltpu.CompilerParams(
            collective_id=0, has_side_effects=True, vmem_limit_bytes=VMEM_BYTES
        ),
        cost_estimate=pl.CostEstimate(
            flops=4 * 10**9, bytes_accessed=8 * 10**6, transcendentals=4 * 10**5
        ),
    )(
        slab_queue.reshape(batch, tok, width), levels, jnp.swapaxes(mod_table, 0, 1),
        w_qkv.reshape(width, 3 * HEAD_DIM), q_gain, k_gain, w_out,
    ).reshape(batch, 1, tok, width)


def solution(mesh):
    placed = (
        P(None, "tm", "space", None),
        P(),
        P(),
        P(None, "tm", None),
        P("tm", None),
        P("tm", None),
        P("tm", None),
    )
    return jax.shard_map(
        body, mesh=mesh, in_specs=placed, out_specs=P(None, "tm", "space", None), check_vma=False
    )
```

```python
import functools
import math

import jax
import jax.numpy as jnp
from jax import lax
from jax.experimental import pallas as pl
from jax.experimental.pallas import tpu as pltpu
from jax.sharding import PartitionSpec as P

HEAD_DIM = 128
W_PIECES = 12
SUM_PIECES = 4
VMEM_BYTES = 64 * 1024 * 1024 - 192 * 1024
MESH = pl.DeviceIdType.MESH
F32 = jnp.float32
BF16 = jnp.bfloat16


def dot_t(left, right):
    return lax.dot_general(left, right, (((1,), (1,)), ((), ())), preferred_element_type=F32)


def head_norm(values, gain):
    values = values.astype(F32)
    factor = lax.rsqrt(jnp.mean(jnp.square(values), axis=-1, keepdims=True) + 1e-06)
    return (values * factor * gain).astype(BF16)


def kernel(
    ring, cols,
    slab_in, levels_in, mod_in, w_qkv, q_gain, k_gain, w_out,
    out,
    slab, levels, mod, rows_of, mod_send, tokens, w_buf, gq, gk, wo, qkv, sp_in, sp_out, sp_back, tmp_out, comb,
    x_send, x_recv, part, r_send, r_recv, l_send, l_recv, prev, fin_send, fin_recv,
    loc_sem, pair_send, pair_recv, ag_send, ag_recv, aa_send, aa_recv, rt_send, rt_recv,
    xs_send, xs_recv, rs_send, rs_recv, misc_send, misc_recv, w_send, w_recv,
    wz_send, wz_recv, wp_send, wp_recv, wd_sem,
):
    half = ring // 2
    group = 2 if ring > 4 else 1
    stride = half // group
    peers = ring // stride
    pieces = stride // 2
    slabs = ring
    tok, width = slab.shape[1], slab.shape[2]
    piece = width // W_PIECES
    tm, space = lax.axis_index("tm"), lax.axis_index("space")
    core, z_lo = lax.rem(tm, 2), lax.div(tm, 2)
    me, z_hi = lax.div(space, 2), lax.rem(space, 2)
    z = z_hi * half + z_lo
    other = 1 - core
    inv_root = 1.0 / math.sqrt(HEAD_DIM)

    def mod_ring(value):
        return lax.rem(value + ring, ring)

    def device(plane, of_core, column):
        return (lax.rem(plane, half) * 2 + of_core, column * 2 + lax.div(plane, half))

    right = device(mod_ring(z + 1), core, me)
    left = device(mod_ring(z - 1), core, me)
    partner = device(z, other, me)
    tm_next = (lax.rem(tm + 1, slabs), space)
    tm_far = (lax.rem(tm + jnp.where(core == 1, 1, slabs - 1), slabs), space)

    def remote(src, dst, send_sem, recv_sem, target):
        return pltpu.make_async_remote_copy(
            src_ref=src, dst_ref=dst, send_sem=send_sem, recv_sem=recv_sem,
            device_id=target, device_id_type=MESH,
        )

    barrier = pltpu.get_barrier_semaphore()
    for target in (right, left, partner, tm_far):
        pl.semaphore_signal(barrier, inc=1, device_id=target, device_id_type=MESH)

    def greet(step, carry):
        column = lax.rem(me + step, cols)
        pl.semaphore_signal(barrier, inc=1, device_id=device(z, core, column), device_id_type=MESH)
        return carry

    lax.fori_loop(1, cols, greet, 0)

    def greet_class(step, carry):
        target = device(mod_ring(z + stride * step), core, me)
        pl.semaphore_signal(barrier, inc=1, device_id=target, device_id_type=MESH)
        return carry

    lax.fori_loop(1, peers, greet_class, 0)

    own_head = core == z_hi
    fetch_levels = pltpu.make_async_copy(levels_in, levels, loc_sem.at[2])
    fetch_mod = pltpu.make_async_copy(mod_in, mod, loc_sem.at[3])
    fetch_slab = pltpu.make_async_copy(slab_in, slab, loc_sem.at[4])
    local_w = pltpu.make_async_copy(w_qkv, w_buf, loc_sem.at[0])
    local_wo = pltpu.make_async_copy(w_out, wo.at[0, core], loc_sem.at[1])
    local_gq = pltpu.make_async_copy(q_gain, gq, loc_sem.at[5])
    local_gk = pltpu.make_async_copy(k_gain, gk, loc_sem.at[6])
    fetch_levels.start()
    fetch_mod.start()
    fetch_slab.start()

    @pl.when(own_head)
    def _():
        local_gq.start()
        local_gk.start()
        local_w.start()

    local_wo.start()
    fetch_levels.wait()
    fetch_mod.wait()

    tm_before = lax.rem(tm + slabs - 1, slabs)
    pick_row = lax.broadcasted_iota(jnp.int32, (16, mod.shape[1]), 0)
    pick_col = lax.broadcasted_iota(jnp.int32, (16, mod.shape[1]), 1)
    hot = jnp.zeros((16, mod.shape[1]), F32)
    for at, (batch, of_slab) in enumerate(((0, tm), (1, tm), (0, tm_before), (1, tm_before))):
        hot = jnp.where((pick_row == at) & (pick_col == levels[batch, of_slab]), 1.0, hot)
    for kind in range(3):
        picked = jnp.dot(hot.astype(BF16), mod[kind], preferred_element_type=F32)
        for at in range(4):
            rows_of[kind, at] = picked[at : at + 1]

    def modulate(batch):
        values = slab[batch].astype(F32)
        centre = jnp.mean(values, axis=-1, keepdims=True)
        moved = values - centre
        spread = jnp.mean(jnp.square(moved), axis=-1, keepdims=True)
        normed = moved * lax.rsqrt(spread + 1e-06)
        return (normed * (1.0 + rows_of[1, batch]) + rows_of[0, batch]).astype(BF16)

    fetch_slab.wait()
    mod_send[...] = modulate(other)
    tokens[z * 2 + core] = modulate(core)
    pl.semaphore_wait(barrier, 4 + cols - 1 + peers - 1)

    def gather_copy(way, step, t, origin):
        slot = origin * 2 + t
        return remote(
            tokens.at[slot], tokens.at[slot], ag_send.at[way, step, t], ag_recv.at[way, step, t],
            (right, left)[way],
        )

    to_pair = remote(mod_send, tokens.at[z * 2 + core], pair_send.at[0], pair_recv.at[0], partner)
    to_pair.start()
    for way in (0, 1):
        gather_copy(way, 1, core, z).start()
    from_pair = remote(mod_send, tokens.at[z * 2 + other], pair_send.at[0], pair_recv.at[0], partner)
    from_pair.wait_recv()
    for way in (0, 1):
        gather_copy(way, 1, other, z).start()

    def give_w(at):
        rows = pl.ds(at * piece, piece)
        return remote(w_qkv.at[rows], w_buf.at[rows], w_send.at[at], w_recv.at[at], partner)

    give_gq = remote(q_gain, gq, pair_send.at[2], pair_recv.at[2], partner)
    give_gk = remote(k_gain, gk, pair_send.at[3], pair_recv.at[3], partner)
    give_wo = remote(w_out, wo.at[0, core], pair_send.at[4], pair_recv.at[4], partner)
    take_wo = remote(w_out, wo.at[0, other], pair_send.at[4], pair_recv.at[4], partner)
    pass_slab = remote(slab, prev, misc_send.at[0], misc_recv.at[0], tm_next)

    @pl.when(own_head)
    def _():
        give_gq.start()
        give_gk.start()

    pairs = group
    rows_w = 2 * HEAD_DIM // cols
    cut_rows = pl.ds(pl.multiple_of(lax.div(me, 2) * rows_w, rows_w), rows_w)
    cut_cols = pl.ds(pl.multiple_of(lax.rem(me, 2) * (width // 2), width // 2), width // 2)

    def plane_piece(at):
        apart = stride * at if 2 * stride * at < half else stride * at - half
        if 2 * stride * at == half:
            apart = jnp.where(core == 0, half // 2, -(half // 2))
        return remote(
            w_out.at[cut_rows, cut_cols], wo.at[at, core, cut_rows, cut_cols],
            wz_send.at[at], wz_recv.at[at], device(mod_ring(z - apart), core, me),
        )

    def spread_piece(column, source):
        rows = pl.ds(pl.multiple_of(lax.div(source, 2) * rows_w, rows_w), rows_w)
        span = pl.ds(pl.multiple_of(lax.rem(source, 2) * (width // 2), width // 2), width // 2)
        piece_of = wo.at[1:pairs, core, rows, span]
        return remote(
            piece_of, piece_of, wp_send.at[column], wp_recv.at[source], device(z, core, column)
        )

    def pair_wo(of_core):
        block = wo.at[1:pairs, of_core]
        return remote(block, block, wd_sem.at[0], wd_sem.at[1], partner)

    for at in range(1, pairs):
        plane_piece(at).start()

    def slab_copy(hi, column, source):
        return remote(
            qkv.at[hi, column], sp_in.at[source, hi], aa_send.at[hi, column], aa_recv.at[hi, source],
            device(z, core, column),
        )

    first_dot = max(half // 2, 2)
    per_step = W_PIECES // (first_dot - 1)

    def gather_step(step, carry):
        plane_a = mod_ring(z - step)
        plane_b = mod_ring(z + step)
        for turn in (0, 1):
            t = core if turn == 0 else other
            for way, origin in ((0, plane_a), (1, plane_b)):

                @pl.when((step < half) | (t == way))
                def _():
                    gather_copy(way, step, t, origin).wait_recv()

                @pl.when((step < half - 1) | ((step == half - 1) & (t == way)))
                def _():
                    gather_copy(way, step + 1, t, origin).start()

        if pairs > 1:

            @pl.when(step == 2)
            def _():
                for at in range(1, pairs):
                    plane_piece(at).wait_recv()

                def spread(ahead, inner):
                    spread_piece(lax.rem(me + ahead, cols), me).start()
                    return inner

                lax.fori_loop(1, cols, spread, 0)

        @pl.when(own_head & (step < first_dot))
        def _():
            def one(at, inner):
                give_w(at).start()
                return inner

            lax.fori_loop((step - 1) * per_step, step * per_step, one, 0)

        @pl.when(step == first_dot)
        def _():
            give_wo.start()

            @pl.when(own_head)
            def _():
                local_w.wait()
                local_gq.wait()
                local_gk.wait()

            @pl.when(jnp.logical_not(own_head))
            def _():
                def one(at, inner):
                    give_w(at).wait_recv()
                    return inner

                lax.fori_loop(0, W_PIECES, one, 0)
                give_gq.wait_recv()
                give_gk.wait_recv()

        def reach(at):
            return jnp.where(at < first_dot, 0, jnp.minimum(2 * (at - first_dot + 1), at))

        lax.fori_loop(reach(step - 1) + 1, reach(step) + 1, project_step, 0)
        return carry

    def project_step(step, carry):
        planes = (mod_ring(z - step), mod_ring(z + step - 1))
        rows = jnp.concatenate(
            [tokens[pl.ds(plane * 2, 2)].reshape(2 * tok, width) for plane in planes], axis=0
        )
        projected = jnp.dot(rows, w_buf[...], preferred_element_type=F32).astype(BF16)
        queries = head_norm(projected[:, :HEAD_DIM], gq[...])
        keys = head_norm(projected[:, HEAD_DIM : 2 * HEAD_DIM], gk[...])
        values = projected[:, 2 * HEAD_DIM :]
        for at, plane in enumerate(planes):
            hi, lo = lax.div(plane, half), lax.rem(plane, half)
            for t in (0, 1):
                cut = slice((at * 2 + t) * tok, (at * 2 + t + 1) * tok)
                column = lo * 2 + t
                qkv[hi, column, :, 0:HEAD_DIM] = queries[cut]
                qkv[hi, column, :, HEAD_DIM : 2 * HEAD_DIM] = keys[cut]
                qkv[hi, column, :, 2 * HEAD_DIM :] = values[cut]

                @pl.when(column != me)
                def _():
                    slab_copy(hi, column, me).start()

        return carry

    lax.fori_loop(1, half + 1, gather_step, 0)
    pass_slab.start()
    sp_in[me] = qkv[:, me]
    if pairs > 1:

        def await_spread(ahead, carry):
            spread_piece(me, lax.rem(me + ahead, cols)).wait_recv()
            return carry

        lax.fori_loop(1, cols, await_spread, 0)
        pair_wo(core).start()

    rows_t = slabs * tok
    at_row = lax.broadcasted_iota(jnp.int32, (rows_t, rows_t), 0) & (tok - 1)
    at_col = lax.broadcasted_iota(jnp.int32, (rows_t, rows_t), 1) & (tok - 1)
    same = at_row == at_col
    for hi in (0, 1):
        queries = qkv[hi, :, :, 0:HEAD_DIM].reshape(rows_t, HEAD_DIM)
        keys = qkv[hi, :, :, HEAD_DIM : 2 * HEAD_DIM].reshape(rows_t, HEAD_DIM)
        values = qkv[hi, :, :, 2 * HEAD_DIM :].reshape(rows_t, HEAD_DIM)
        scores = jnp.where(same, dot_t(queries, keys) * inv_root, -jnp.inf)
        weights = jnp.exp(scores - jnp.max(scores, axis=-1, keepdims=True))
        total = jnp.sum(weights, axis=-1, keepdims=True)
        mixed = jnp.dot(weights.astype(BF16), values, preferred_element_type=F32) / total
        tmp_out[hi] = mixed.reshape(slabs, tok, HEAD_DIM)

    def await_slab(step, carry):
        for hi in (0, 1):
            slab_copy(hi, me, lax.rem(me + step, cols)).wait_recv()
        return carry

    lax.fori_loop(1, cols, await_slab, 0)

    def back_copy(column, of_slab):
        return remote(
            sp_out.at[column], sp_back.at[:, of_slab], rt_send.at[column], rt_recv.at[of_slab],
            device(z, core, column),
        )

    batch_s = 4
    rows_s = batch_s * 2 * tok

    def spatial_step(step, carry):
        keys = sp_in[:, :, :, HEAD_DIM : 2 * HEAD_DIM].reshape(cols * 2 * tok, HEAD_DIM)
        values = sp_in[:, :, :, 2 * HEAD_DIM :].reshape(cols * 2 * tok, HEAD_DIM)
        queries = sp_in[pl.ds(step * batch_s, batch_s), :, :, 0:HEAD_DIM].reshape(rows_s, HEAD_DIM)
        scores = dot_t(queries, keys) * inv_root
        weights = jnp.exp(scores - jnp.max(scores, axis=-1, keepdims=True))
        total = jnp.sum(weights, axis=-1, keepdims=True)
        mixed = jnp.dot(weights.astype(BF16), values, preferred_element_type=F32) / total
        sp_out[pl.ds(step * batch_s, batch_s)] = mixed.astype(BF16).reshape(batch_s, 2, tok, HEAD_DIM)
        for at in range(batch_s):
            column = step * batch_s + at

            @pl.when(column != me)
            def _():
                back_copy(column, me).start()

        return carry

    lax.fori_loop(0, cols // batch_s, spatial_step, 0)
    sp_back[:, me] = sp_out[me]
    local_wo.wait()
    take_wo.wait_recv()

    def await_back(step, carry):
        back_copy(me, lax.rem(me + step, cols)).wait_recv()
        return carry

    lax.fori_loop(1, cols, await_back, 0)
    comb[...] = (sp_back[...].astype(F32) + tmp_out[...]).astype(BF16)

    def fill(dst, plane):
        def one(at, carry):
            step = lax.div(at, 2)
            block = jnp.where(lax.rem(at, 2) == 0, 2 * stride - 1 - step, step)
            place = lax.rem(2 * plane + 2 * ring - (stride - 1) + block, 2 * ring)
            from_slab = lax.rem(lax.rem(place, slabs) + slabs - 1, slabs)
            dst[at] = comb[lax.div(place, slabs), from_slab]
            return carry

        lax.fori_loop(0, 2 * stride, one, 0)

    def head_copy(step, at):
        plane = mod_ring(z + stride * step)
        slot = lax.div(lax.rem(z_lo - lax.rem(plane, half) + half, half), stride)
        rows = pl.ds(4 * at, 4)
        return remote(
            x_send.at[step, rows], x_recv.at[slot, z_hi, rows],
            xs_send.at[step, at], xs_recv.at[slot, z_hi, at], device(plane, core, me),
        )

    for step in range(1, peers):
        fill(x_send.at[step], mod_ring(z + stride * step))
        head_copy(step, 0).start()
    for at in range(1, pieces):
        for step in range(1, peers):
            head_copy(step, at).start()
    fill(x_recv.at[0, z_hi], z)
    if pairs > 1:
        pair_wo(other).wait_recv()

    def await_heads(at):
        for step in range(1, peers):
            plane = mod_ring(z + stride * step)
            slot = lax.div(lax.rem(lax.rem(plane, half) - z_lo + half, half), stride)
            hi = lax.div(plane, half)
            rows = pl.ds(4 * at, 4)
            remote(
                x_send.at[step, rows], x_recv.at[slot, hi, rows],
                xs_send.at[step, at], xs_recv.at[slot, hi, at], device(plane, core, me),
            ).wait_recv()

    def sum_copy(way, step):
        mine, theirs, target = ((r_send, r_recv, right), (l_send, l_recv, left))[way]
        return remote(
            mine.at[step], theirs.at[step], rs_send.at[way, step], rs_recv.at[way, step], target
        )

    chunk = width // SUM_PIECES
    rows_x = 4 * tok
    for step in range(stride - 1):
        if step % 2 == 0:
            await_heads(step // 2)
            rows = slice(2 * step, 2 * step + 4)
            heads = jnp.concatenate(
                [x_recv[at // 2, at % 2, rows].reshape(rows_x, HEAD_DIM) for at in range(2 * pairs)],
                axis=1,
            )
            for at in range(0, width, chunk):
                weights = wo[:, :, :, at : at + chunk].reshape(2 * pairs * HEAD_DIM, chunk)
                product = jnp.dot(heads, weights, preferred_element_type=F32)
                part[rows, :, at : at + chunk] = product.reshape(4, tok, chunk)
        for way, mine, theirs in ((0, r_send, r_recv), (1, l_send, l_recv)):
            share = part[step * 2 + way]
            if step >= 2:
                sum_copy(way, step - 2).wait_recv()
                share = share + theirs[step - 2].astype(F32)
            mine[step] = share.astype(BF16)
            sum_copy(way, step).start()
    for step in range(max(stride - 3, 0), stride - 1):
        for way in (0, 1):
            sum_copy(way, step).wait_recv()

    def total_of(t):
        if stride > 2:
            return (
                part[2 * stride - 1 - t]
                + r_recv[stride - 2 - t].astype(F32)
                + l_recv[stride - 3 + t].astype(F32)
            )
        from_side = jnp.where(t == 0, r_recv[0].astype(F32), l_recv[0].astype(F32))
        return part[2 * stride - 1 - t] + from_side

    fin_send[...] = total_of(other).astype(BF16)
    give_fin = remote(fin_send, fin_recv, misc_send.at[1], misc_recv.at[1], partner)
    give_fin.start()
    pass_slab.wait_recv()

    def attend(batch, projection):
        gate = rows_of[2, 2 + batch]
        out[batch] = (prev[batch].astype(F32) + gate * projection).astype(BF16)

    attend(core, total_of(core))
    give_fin.wait_recv()
    attend(other, fin_recv[...].astype(F32))

    to_pair.wait_send()

    @pl.when(own_head)
    def _():
        def one(at, inner):
            give_w(at).wait_send()
            return inner

        lax.fori_loop(0, W_PIECES, one, 0)
        give_gq.wait_send()
        give_gk.wait_send()

    give_wo.wait_send()
    pass_slab.wait_send()
    give_fin.wait_send()
    for at in range(1, pairs):
        plane_piece(at).wait_send()
    if pairs > 1:
        pair_wo(core).wait_send()

    def drain_gather(step, carry):
        for way in (0, 1):
            for t in (0, 1):

                @pl.when((step < half) | (t == way))
                def _():
                    gather_copy(way, step, t, z).wait_send()

        return carry

    lax.fori_loop(1, half + 1, drain_gather, 0)

    def drain_plane(step, carry):
        column = lax.rem(me + step, cols)
        for hi in (0, 1):
            slab_copy(hi, column, me).wait_send()
        back_copy(column, me).wait_send()
        if pairs > 1:
            spread_piece(column, me).wait_send()
        return carry

    lax.fori_loop(1, cols, drain_plane, 0)

    for step in range(1, peers):
        for at in range(pieces):
            head_copy(step, at).wait_send()
    for step in range(stride - 1):
        for way in (0, 1):
            sum_copy(way, step).wait_send()


def body(slab_queue, levels, mod_table, w_qkv, q_gain, k_gain, w_out):
    batch, _, tok, width = slab_queue.shape
    ring = lax.axis_size("tm")
    cols = lax.axis_size("space") // 2
    half = ring // 2
    group = 2 if ring > 4 else 1
    stride = half // group
    vmem = pl.BlockSpec(memory_space=pltpu.VMEM)
    hbm = pl.BlockSpec(memory_space=pltpu.HBM)
    dma = pltpu.SemaphoreType.DMA
    block = (tok, width)
    return pl.pallas_call(
        functools.partial(kernel, ring, cols),
        out_shape=jax.ShapeDtypeStruct((batch, tok, width), BF16),
        in_specs=[hbm] * 7,
        out_specs=vmem,
        scratch_shapes=[
            pltpu.VMEM((batch,) + block, BF16),
            pltpu.SMEM(levels.shape, jnp.int32),
            pltpu.VMEM((3, mod_table.shape[0], width), BF16),
            pltpu.VMEM((3, 4, 1, width), F32),
            pltpu.VMEM(block, BF16),
            pltpu.VMEM((2 * ring,) + block, BF16),
            pltpu.VMEM((width, 3 * HEAD_DIM), BF16),
            pltpu.VMEM((1, HEAD_DIM), F32),
            pltpu.VMEM((1, HEAD_DIM), F32),
            pltpu.VMEM((group, 2, HEAD_DIM, width), BF16),
            pltpu.VMEM((2, ring, tok, 3 * HEAD_DIM), BF16),
            pltpu.VMEM((cols, 2, tok, 3 * HEAD_DIM), BF16),
            pltpu.VMEM((cols, 2, tok, HEAD_DIM), BF16),
            pltpu.VMEM((2, ring, tok, HEAD_DIM), BF16),
            pltpu.VMEM((2, ring, tok, HEAD_DIM), F32),
            pltpu.VMEM((2, ring, tok, HEAD_DIM), BF16),
            pltpu.VMEM((ring // stride, 2 * stride, tok, HEAD_DIM), BF16),
            pltpu.VMEM((group, 2, 2 * stride, tok, HEAD_DIM), BF16),
            pltpu.VMEM((2 * stride,) + block, F32),
            pltpu.VMEM((stride - 1,) + block, BF16),
            pltpu.VMEM((stride - 1,) + block, BF16),
            pltpu.VMEM((stride - 1,) + block, BF16),
            pltpu.VMEM((stride - 1,) + block, BF16),
            pltpu.VMEM((batch,) + block, BF16),
            pltpu.VMEM(block, BF16),
            pltpu.VMEM(block, BF16),
            dma((7,)),
            dma((5,)),
            dma((5,)),
            dma((2, half + 1, 2)),
            dma((2, half + 1, 2)),
            dma((2, cols)),
            dma((2, cols)),
            dma((cols,)),
            dma((cols,)),
            dma((ring // stride, stride // 2)),
            dma((group, 2, stride // 2)),
            dma((2, stride - 1)),
            dma((2, stride - 1)),
            dma((2,)),
            dma((2,)),
            dma((W_PIECES,)),
            dma((W_PIECES,)),
            dma((group,)),
            dma((group,)),
            dma((cols,)),
            dma((cols,)),
            dma((2,)),
        ],
        compiler_params=pltpu.CompilerParams(
            collective_id=0, has_side_effects=True, vmem_limit_bytes=VMEM_BYTES
        ),
        cost_estimate=pl.CostEstimate(
            flops=4 * 10**9, bytes_accessed=8 * 10**6, transcendentals=4 * 10**5
        ),
    )(
        slab_queue.reshape(batch, tok, width), levels, jnp.swapaxes(mod_table, 0, 1),
        w_qkv.reshape(width, 3 * HEAD_DIM), q_gain, k_gain, w_out,
    ).reshape(batch, 1, tok, width)


def solution(mesh):
    placed = (
        P(None, "tm", "space", None),
        P(),
        P(),
        P(None, "tm", None),
        P("tm", None),
        P("tm", None),
        P("tm", None),
    )
    return jax.shard_map(
        body, mesh=mesh, in_specs=placed, out_specs=P(None, "tm", "space", None), check_vma=False
    )
```

```python
import functools
import math

import jax
import jax.numpy as jnp
from jax import lax
from jax.experimental import pallas as pl
from jax.experimental.pallas import tpu as pltpu
from jax.sharding import PartitionSpec as P

HEAD_DIM = 128
W_PIECES = 12
SUM_PIECES = 4
VMEM_BYTES = 64 * 1024 * 1024 - 192 * 1024
MESH = pl.DeviceIdType.MESH
F32 = jnp.float32
BF16 = jnp.bfloat16


def dot_t(left, right):
    return lax.dot_general(left, right, (((1,), (1,)), ((), ())), preferred_element_type=F32)


def head_norm(values, gain):
    values = values.astype(F32)
    factor = lax.rsqrt(jnp.mean(jnp.square(values), axis=-1, keepdims=True) + 1e-06)
    return (values * factor * gain).astype(BF16)


def kernel(
    ring, cols,
    slab_in, levels_in, mod_in, w_qkv, q_gain, k_gain, w_out,
    out,
    slab, levels, mod, rows_of, mod_send, tokens, w_buf, gq, gk, wo, qkv, sp_in, sp_out, sp_back, tmp_out, comb,
    x_send, x_recv, part, r_send, r_recv, l_send, l_recv, prev, fin_send, fin_recv,
    loc_sem, pair_send, pair_recv, ag_send, ag_recv, aa_send, aa_recv, rt_send, rt_recv,
    xs_send, xs_recv, rs_send, rs_recv, misc_send, misc_recv, w_send, w_recv,
    wz_send, wz_recv, wp_send, wp_recv, wd_sem,
):
    half = ring // 2
    group = 2 if ring > 4 else 1
    stride = half // group
    peers = ring // stride
    pieces = stride // 2
    slabs = ring
    tok, width = slab.shape[1], slab.shape[2]
    piece = width // W_PIECES
    tm, space = lax.axis_index("tm"), lax.axis_index("space")
    core, z_lo = lax.rem(tm, 2), lax.div(tm, 2)
    me, z_hi = lax.div(space, 2), lax.rem(space, 2)
    z = z_hi * half + z_lo
    other = 1 - core
    inv_root = 1.0 / math.sqrt(HEAD_DIM)

    def mod_ring(value):
        return lax.rem(value + ring, ring)

    def device(plane, of_core, column):
        return (lax.rem(plane, half) * 2 + of_core, column * 2 + lax.div(plane, half))

    right = device(mod_ring(z + 1), core, me)
    left = device(mod_ring(z - 1), core, me)
    partner = device(z, other, me)
    tm_next = (lax.rem(tm + 1, slabs), space)
    tm_far = (lax.rem(tm + jnp.where(core == 1, 1, slabs - 1), slabs), space)

    def remote(src, dst, send_sem, recv_sem, target):
        return pltpu.make_async_remote_copy(
            src_ref=src, dst_ref=dst, send_sem=send_sem, recv_sem=recv_sem,
            device_id=target, device_id_type=MESH,
        )

    barrier = pltpu.get_barrier_semaphore()
    for target in (right, left, partner, tm_far):
        pl.semaphore_signal(barrier, inc=1, device_id=target, device_id_type=MESH)

    def greet(step, carry):
        column = lax.rem(me + step, cols)
        pl.semaphore_signal(barrier, inc=1, device_id=device(z, core, column), device_id_type=MESH)
        return carry

    lax.fori_loop(1, cols, greet, 0)

    def greet_class(step, carry):
        target = device(mod_ring(z + stride * step), core, me)
        pl.semaphore_signal(barrier, inc=1, device_id=target, device_id_type=MESH)
        return carry

    lax.fori_loop(1, peers, greet_class, 0)

    own_head = core == z_hi
    fetch_levels = pltpu.make_async_copy(levels_in, levels, loc_sem.at[2])
    fetch_mod = pltpu.make_async_copy(mod_in, mod, loc_sem.at[3])
    fetch_slab = pltpu.make_async_copy(slab_in, slab, loc_sem.at[4])
    local_w = pltpu.make_async_copy(w_qkv, w_buf, loc_sem.at[0])
    local_wo = pltpu.make_async_copy(w_out, wo.at[0, core], loc_sem.at[1])
    local_gq = pltpu.make_async_copy(q_gain, gq, loc_sem.at[5])
    local_gk = pltpu.make_async_copy(k_gain, gk, loc_sem.at[6])
    fetch_levels.start()
    fetch_mod.start()
    fetch_slab.start()

    @pl.when(own_head)
    def _():
        local_gq.start()
        local_gk.start()
        local_w.start()

    local_wo.start()
    fetch_levels.wait()
    fetch_mod.wait()

    tm_before = lax.rem(tm + slabs - 1, slabs)
    pick_row = lax.broadcasted_iota(jnp.int32, (16, mod.shape[1]), 0)
    pick_col = lax.broadcasted_iota(jnp.int32, (16, mod.shape[1]), 1)
    hot = jnp.zeros((16, mod.shape[1]), F32)
    for at, (batch, of_slab) in enumerate(((0, tm), (1, tm), (0, tm_before), (1, tm_before))):
        hot = jnp.where((pick_row == at) & (pick_col == levels[batch, of_slab]), 1.0, hot)
    for kind in range(3):
        picked = jnp.dot(hot.astype(BF16), mod[kind], preferred_element_type=F32)
        for at in range(4):
            rows_of[kind, at] = picked[at : at + 1]

    def modulate(batch):
        values = slab[batch].astype(F32)
        centre = jnp.mean(values, axis=-1, keepdims=True)
        moved = values - centre
        spread = jnp.mean(jnp.square(moved), axis=-1, keepdims=True)
        normed = moved * lax.rsqrt(spread + 1e-06)
        return (normed * (1.0 + rows_of[1, batch]) + rows_of[0, batch]).astype(BF16)

    fetch_slab.wait()
    mod_send[...] = modulate(other)
    tokens[z * 2 + core] = modulate(core)
    pl.semaphore_wait(barrier, 4 + cols - 1 + peers - 1)

    def gather_copy(way, step, t, origin):
        slot = origin * 2 + t
        return remote(
            tokens.at[slot], tokens.at[slot], ag_send.at[0], ag_recv.at[way, step, t],
            (right, left)[way],
        )

    to_pair = remote(mod_send, tokens.at[z * 2 + core], pair_send.at[0], pair_recv.at[0], partner)
    to_pair.start()
    for way in (0, 1):
        gather_copy(way, 1, core, z).start()
    from_pair = remote(mod_send, tokens.at[z * 2 + other], pair_send.at[0], pair_recv.at[0], partner)
    from_pair.wait_recv()
    for way in (0, 1):
        gather_copy(way, 1, other, z).start()

    def give_w(at):
        rows = pl.ds(at * piece, piece)
        return remote(w_qkv.at[rows], w_buf.at[rows], w_send.at[0], w_recv.at[0], partner)

    whole_w = remote(w_qkv, w_buf, w_send.at[0], w_recv.at[0], partner)
    give_gq = remote(q_gain, gq, pair_send.at[2], pair_recv.at[2], partner)
    give_gk = remote(k_gain, gk, pair_send.at[3], pair_recv.at[3], partner)
    give_wo = remote(w_out, wo.at[0, core], pair_send.at[4], pair_recv.at[4], partner)
    take_wo = remote(w_out, wo.at[0, other], pair_send.at[4], pair_recv.at[4], partner)
    pass_slab = remote(slab, prev, misc_send.at[0], misc_recv.at[0], tm_next)

    @pl.when(own_head)
    def _():
        give_gq.start()
        give_gk.start()

    pairs = group
    rows_w = 2 * HEAD_DIM // cols
    cut_rows = pl.ds(pl.multiple_of(lax.div(me, 2) * rows_w, rows_w), rows_w)
    cut_cols = pl.ds(pl.multiple_of(lax.rem(me, 2) * (width // 2), width // 2), width // 2)

    def plane_piece(at):
        apart = stride * at if 2 * stride * at < half else stride * at - half
        if 2 * stride * at == half:
            apart = jnp.where(core == 0, half // 2, -(half // 2))
        return remote(
            w_out.at[cut_rows, cut_cols], wo.at[at, core, cut_rows, cut_cols],
            wz_send.at[at], wz_recv.at[at], device(mod_ring(z - apart), core, me),
        )

    def spread_piece(column, source):
        rows = pl.ds(pl.multiple_of(lax.div(source, 2) * rows_w, rows_w), rows_w)
        span = pl.ds(pl.multiple_of(lax.rem(source, 2) * (width // 2), width // 2), width // 2)
        piece_of = wo.at[1:pairs, core, rows, span]
        return remote(
            piece_of, piece_of, wp_send.at[column], wp_recv.at[source], device(z, core, column)
        )

    def pair_wo(of_core):
        block = wo.at[1:pairs, of_core]
        return remote(block, block, wd_sem.at[0], wd_sem.at[1], partner)

    for at in range(1, pairs):
        plane_piece(at).start()

    def slab_copy(hi, column, source):
        return remote(
            qkv.at[hi, column], sp_in.at[source, hi], aa_send.at[0], aa_recv.at[0],
            device(z, core, column),
        )

    first_dot = max(half // 2, 2)
    per_step = W_PIECES // (first_dot - 1)

    def gather_step(step, carry):
        plane_a = mod_ring(z - step)
        plane_b = mod_ring(z + step)
        for turn in (0, 1):
            t = core if turn == 0 else other
            for way, origin in ((0, plane_a), (1, plane_b)):

                @pl.when((step < half) | (t == way))
                def _():
                    gather_copy(way, step, t, origin).wait_recv()

                @pl.when((step < half - 1) | ((step == half - 1) & (t == way)))
                def _():
                    gather_copy(way, step + 1, t, origin).start()

        if pairs > 1:

            @pl.when(step == 2)
            def _():
                for at in range(1, pairs):
                    plane_piece(at).wait_recv()

                def spread(ahead, inner):
                    spread_piece(lax.rem(me + ahead, cols), me).start()
                    return inner

                lax.fori_loop(1, cols, spread, 0)

        @pl.when(own_head & (step < first_dot))
        def _():
            def one(at, inner):
                give_w(at).start()
                return inner

            lax.fori_loop((step - 1) * per_step, step * per_step, one, 0)

        @pl.when(step == first_dot)
        def _():
            give_wo.start()

            @pl.when(own_head)
            def _():
                local_w.wait()
                local_gq.wait()
                local_gk.wait()

            @pl.when(jnp.logical_not(own_head))
            def _():
                whole_w.wait_recv()
                give_gq.wait_recv()
                give_gk.wait_recv()

        def reach(at):
            done = jnp.minimum(2 * (at - first_dot + 1), half)
            return jnp.where(at < first_dot, 0, jnp.where(at == half, half + 1, done))

        lax.fori_loop(reach(step - 1), reach(step), project_step, 0)
        return carry

    def project_step(step, carry):
        planes = (mod_ring(z - step), mod_ring(z + step))
        rows = jnp.concatenate(
            [tokens[pl.ds(plane * 2, 2)].reshape(2 * tok, width) for plane in planes], axis=0
        )
        projected = jnp.dot(rows, w_buf[...], preferred_element_type=F32).astype(BF16)
        queries = head_norm(projected[:, :HEAD_DIM], gq[...])
        keys = head_norm(projected[:, HEAD_DIM : 2 * HEAD_DIM], gk[...])
        values = projected[:, 2 * HEAD_DIM :]
        def place(at):
            hi, lo = lax.div(planes[at], half), lax.rem(planes[at], half)
            for t in (0, 1):
                cut = slice((at * 2 + t) * tok, (at * 2 + t + 1) * tok)
                column = lo * 2 + t
                qkv[hi, column, :, 0:HEAD_DIM] = queries[cut]
                qkv[hi, column, :, HEAD_DIM : 2 * HEAD_DIM] = keys[cut]
                qkv[hi, column, :, 2 * HEAD_DIM :] = values[cut]

                @pl.when(column != me)
                def _():
                    slab_copy(hi, column, me).start()

        place(0)

        @pl.when(lax.rem(step, half) != 0)
        def _():
            place(1)

        return carry

    lax.fori_loop(1, half + 1, gather_step, 0)
    pass_slab.start()
    sp_in[me] = qkv[:, me]

    rows_t = slabs * tok
    at_row = lax.broadcasted_iota(jnp.int32, (rows_t, rows_t), 0) & (tok - 1)
    at_col = lax.broadcasted_iota(jnp.int32, (rows_t, rows_t), 1) & (tok - 1)
    same = at_row == at_col
    for hi in (0, 1):
        queries = qkv[hi, :, :, 0:HEAD_DIM].reshape(rows_t, HEAD_DIM)
        keys = qkv[hi, :, :, HEAD_DIM : 2 * HEAD_DIM].reshape(rows_t, HEAD_DIM)
        values = qkv[hi, :, :, 2 * HEAD_DIM :].reshape(rows_t, HEAD_DIM)
        scores = jnp.where(same, dot_t(queries, keys) * inv_root, -jnp.inf)
        weights = jnp.exp(scores - jnp.max(scores, axis=-1, keepdims=True))
        total = jnp.sum(weights, axis=-1, keepdims=True)
        mixed = jnp.dot(weights.astype(BF16), values, preferred_element_type=F32) / total
        tmp_out[hi] = mixed.reshape(slabs, tok, HEAD_DIM)

    if pairs > 1:

        def await_spread(ahead, carry):
            spread_piece(me, lax.rem(me + ahead, cols)).wait_recv()
            return carry

        lax.fori_loop(1, cols, await_spread, 0)
        pair_wo(core).start()

    part_in = sp_in.at[0 : cols - 1]
    remote(part_in, part_in, aa_send.at[0], aa_recv.at[0], partner).wait_recv()

    mine_late = lax.div(me, 2) == z_lo
    is_late = jnp.where(mine_late, 1, 0)

    def back_copy(column, of_slab):
        return remote(
            sp_out.at[column], sp_back.at[:, of_slab], rt_send.at[0], rt_recv.at[is_late],
            device(z, core, column),
        )

    batch_s = 4
    rows_s = batch_s * 2 * tok

    def spatial_step(step, carry):
        keys = sp_in[:, :, :, HEAD_DIM : 2 * HEAD_DIM].reshape(cols * 2 * tok, HEAD_DIM)
        values = sp_in[:, :, :, 2 * HEAD_DIM :].reshape(cols * 2 * tok, HEAD_DIM)
        queries = sp_in[pl.ds(step * batch_s, batch_s), :, :, 0:HEAD_DIM].reshape(rows_s, HEAD_DIM)
        scores = dot_t(queries, keys) * inv_root
        weights = jnp.exp(scores - jnp.max(scores, axis=-1, keepdims=True))
        total = jnp.sum(weights, axis=-1, keepdims=True)
        mixed = jnp.dot(weights.astype(BF16), values, preferred_element_type=F32) / total
        sp_out[pl.ds(step * batch_s, batch_s)] = mixed.astype(BF16).reshape(batch_s, 2, tok, HEAD_DIM)
        for at in range(batch_s):
            column = step * batch_s + at

            @pl.when(column != me)
            def _():
                back_copy(column, me).start()

        return carry

    lax.fori_loop(0, cols // batch_s, spatial_step, 0)
    sp_back[:, me] = sp_out[me]
    local_wo.wait()
    take_wo.wait_recv()

    def await_back(late, count):
        block = sp_back.at[:, 0:count]
        remote(block, block, rt_send.at[0], rt_recv.at[late], partner).wait_recv()

    @pl.when(mine_late)
    def _():
        await_back(0, slabs - 2)
        await_back(1, 1)

    @pl.when(jnp.logical_not(mine_late))
    def _():
        await_back(0, slabs - 3)
        await_back(1, 2)

    comb[...] = (sp_back[...].astype(F32) + tmp_out[...]).astype(BF16)

    def fill(dst, plane):
        def one(at, carry):
            step = lax.div(at, 2)
            block = jnp.where(lax.rem(at, 2) == 0, 2 * stride - 1 - step, step)
            place = lax.rem(2 * plane + 2 * ring - (stride - 1) + block, 2 * ring)
            from_slab = lax.rem(lax.rem(place, slabs) + slabs - 1, slabs)
            dst[at] = comb[lax.div(place, slabs), from_slab]
            return carry

        lax.fori_loop(0, 2 * stride, one, 0)

    def head_copy(step, at):
        plane = mod_ring(z + stride * step)
        slot = lax.div(lax.rem(z_lo - lax.rem(plane, half) + half, half), stride)
        rows = pl.ds(4 * at, 4)
        return remote(
            x_send.at[step, rows], x_recv.at[slot, z_hi, rows],
            xs_send.at[step, at], xs_recv.at[slot, z_hi, at], device(plane, core, me),
        )

    for step in range(1, peers):
        fill(x_send.at[step], mod_ring(z + stride * step))
        head_copy(step, 0).start()
    for at in range(1, pieces):
        for step in range(1, peers):
            head_copy(step, at).start()
    fill(x_recv.at[0, z_hi], z)
    if pairs > 1:
        pair_wo(other).wait_recv()

    to_pair.wait_send()

    @pl.when(own_head)
    def _():
        whole_w.wait_send()
        give_gq.wait_send()
        give_gk.wait_send()

    give_wo.wait_send()
    pass_slab.wait_send()
    pass_slab.wait_recv()
    for at in range(1, pairs):
        plane_piece(at).wait_send()
    if pairs > 1:
        pair_wo(core).wait_send()

        def drain_spread(ahead, carry):
            spread_piece(lax.rem(me + ahead, cols), me).wait_send()
            return carry

        lax.fori_loop(1, cols, drain_spread, 0)
    sent = tokens.at[0 : 2 * ring - 2]
    remote(sent, sent, ag_send.at[0], ag_recv.at[0, 0, 0], partner).wait_send()
    sent = qkv.at[:, 0 : cols - 1]
    remote(sent, sent, aa_send.at[0], aa_recv.at[0], partner).wait_send()
    sent = sp_out.at[0 : cols - 1]
    remote(sent, sent, rt_send.at[0], rt_recv.at[0], partner).wait_send()

    def await_heads(at):
        for step in range(1, peers):
            plane = mod_ring(z + stride * step)
            slot = lax.div(lax.rem(lax.rem(plane, half) - z_lo + half, half), stride)
            hi = lax.div(plane, half)
            rows = pl.ds(4 * at, 4)
            remote(
                x_send.at[step, rows], x_recv.at[slot, hi, rows],
                xs_send.at[step, at], xs_recv.at[slot, hi, at], device(plane, core, me),
            ).wait_recv()

    def sum_copy(way, step):
        mine, theirs, target = ((r_send, r_recv, right), (l_send, l_recv, left))[way]
        return remote(
            mine.at[step], theirs.at[step], rs_send.at[way, step], rs_recv.at[way, step], target
        )

    chunk = width // SUM_PIECES
    rows_x = 4 * tok
    for step in range(stride - 1):
        if step % 2 == 0:
            await_heads(step // 2)
            rows = slice(2 * step, 2 * step + 4)
            heads = jnp.concatenate(
                [x_recv[at // 2, at % 2, rows].reshape(rows_x, HEAD_DIM) for at in range(2 * pairs)],
                axis=1,
            )
            for at in range(0, width, chunk):
                weights = wo[:, :, :, at : at + chunk].reshape(2 * pairs * HEAD_DIM, chunk)
                product = jnp.dot(heads, weights, preferred_element_type=F32)
                part[rows, :, at : at + chunk] = product.reshape(4, tok, chunk)
        for way, mine, theirs in ((0, r_send, r_recv), (1, l_send, l_recv)):
            share = part[step * 2 + way]
            if step >= 2:
                sum_copy(way, step - 2).wait_recv()
                share = share + theirs[step - 2].astype(F32)
            mine[step] = share.astype(BF16)
            sum_copy(way, step).start()
    for step in range(max(stride - 3, 0), stride - 1):
        for way in (0, 1):
            sum_copy(way, step).wait_recv()

    def total_of(t):
        if stride > 2:
            return (
                part[2 * stride - 1 - t]
                + r_recv[stride - 2 - t].astype(F32)
                + l_recv[stride - 3 + t].astype(F32)
            )
        from_side = jnp.where(t == 0, r_recv[0].astype(F32), l_recv[0].astype(F32))
        return part[2 * stride - 1 - t] + from_side

    fin_send[...] = total_of(other).astype(BF16)
    give_fin = remote(fin_send, fin_recv, misc_send.at[1], misc_recv.at[1], partner)
    give_fin.start()

    def attend(batch, projection):
        gate = rows_of[2, 2 + batch]
        out[batch] = (prev[batch].astype(F32) + gate * projection).astype(BF16)

    attend(core, total_of(core))
    give_fin.wait_recv()
    attend(other, fin_recv[...].astype(F32))

    give_fin.wait_send()
    for step in range(1, peers):
        for at in range(pieces):
            head_copy(step, at).wait_send()
    for step in range(stride - 1):
        for way in (0, 1):
            sum_copy(way, step).wait_send()


def body(slab_queue, levels, mod_table, w_qkv, q_gain, k_gain, w_out):
    batch, _, tok, width = slab_queue.shape
    ring = lax.axis_size("tm")
    cols = lax.axis_size("space") // 2
    half = ring // 2
    group = 2 if ring > 4 else 1
    stride = half // group
    vmem = pl.BlockSpec(memory_space=pltpu.VMEM)
    hbm = pl.BlockSpec(memory_space=pltpu.HBM)
    dma = pltpu.SemaphoreType.DMA
    block = (tok, width)
    return pl.pallas_call(
        functools.partial(kernel, ring, cols),
        out_shape=jax.ShapeDtypeStruct((batch, tok, width), BF16),
        in_specs=[hbm] * 7,
        out_specs=vmem,
        scratch_shapes=[
            pltpu.VMEM((batch,) + block, BF16),
            pltpu.SMEM(levels.shape, jnp.int32),
            pltpu.VMEM((3, mod_table.shape[0], width), BF16),
            pltpu.VMEM((3, 4, 1, width), F32),
            pltpu.VMEM(block, BF16),
            pltpu.VMEM((2 * ring,) + block, BF16),
            pltpu.VMEM((width, 3 * HEAD_DIM), BF16),
            pltpu.VMEM((1, HEAD_DIM), F32),
            pltpu.VMEM((1, HEAD_DIM), F32),
            pltpu.VMEM((group, 2, HEAD_DIM, width), BF16),
            pltpu.VMEM((2, ring, tok, 3 * HEAD_DIM), BF16),
            pltpu.VMEM((cols, 2, tok, 3 * HEAD_DIM), BF16),
            pltpu.VMEM((cols, 2, tok, HEAD_DIM), BF16),
            pltpu.VMEM((2, ring, tok, HEAD_DIM), BF16),
            pltpu.VMEM((2, ring, tok, HEAD_DIM), F32),
            pltpu.VMEM((2, ring, tok, HEAD_DIM), BF16),
            pltpu.VMEM((ring // stride, 2 * stride, tok, HEAD_DIM), BF16),
            pltpu.VMEM((group, 2, 2 * stride, tok, HEAD_DIM), BF16),
            pltpu.VMEM((2 * stride,) + block, F32),
            pltpu.VMEM((stride - 1,) + block, BF16),
            pltpu.VMEM((stride - 1,) + block, BF16),
            pltpu.VMEM((stride - 1,) + block, BF16),
            pltpu.VMEM((stride - 1,) + block, BF16),
            pltpu.VMEM((batch,) + block, BF16),
            pltpu.VMEM(block, BF16),
            pltpu.VMEM(block, BF16),
            dma((7,)),
            dma((5,)),
            dma((5,)),
            dma((1,)),
            dma((2, half + 1, 2)),
            dma((1,)),
            dma((1,)),
            dma((1,)),
            dma((2,)),
            dma((ring // stride, stride // 2)),
            dma((group, 2, stride // 2)),
            dma((2, stride - 1)),
            dma((2, stride - 1)),
            dma((2,)),
            dma((2,)),
            dma((1,)),
            dma((1,)),
            dma((group,)),
            dma((group,)),
            dma((cols,)),
            dma((cols,)),
            dma((2,)),
        ],
        compiler_params=pltpu.CompilerParams(
            collective_id=0, has_side_effects=True, vmem_limit_bytes=VMEM_BYTES
        ),
        cost_estimate=pl.CostEstimate(
            flops=4 * 10**9, bytes_accessed=8 * 10**6, transcendentals=4 * 10**5
        ),
    )(
        slab_queue.reshape(batch, tok, width), levels, jnp.swapaxes(mod_table, 0, 1),
        w_qkv.reshape(width, 3 * HEAD_DIM), q_gain, k_gain, w_out,
    ).reshape(batch, 1, tok, width)


def solution(mesh):
    placed = (
        P(None, "tm", "space", None),
        P(),
        P(),
        P(None, "tm", None),
        P("tm", None),
        P("tm", None),
        P("tm", None),
    )
    return jax.shard_map(
        body, mesh=mesh, in_specs=placed, out_specs=P(None, "tm", "space", None), check_vma=False
    )
```

```python
import functools
import math

import jax
import jax.numpy as jnp
from jax import lax
from jax.experimental import pallas as pl
from jax.experimental.pallas import tpu as pltpu
from jax.sharding import PartitionSpec as P

HEAD_DIM = 128
W_PIECES = 12
SUM_PIECES = 4
VMEM_BYTES = 64 * 1024 * 1024 - 192 * 1024
MESH = pl.DeviceIdType.MESH
F32 = jnp.float32
BF16 = jnp.bfloat16


def dot_t(left, right):
    return lax.dot_general(left, right, (((1,), (1,)), ((), ())), preferred_element_type=F32)


def head_norm(values, gain):
    values = values.astype(F32)
    factor = lax.rsqrt(jnp.mean(jnp.square(values), axis=-1, keepdims=True) + 1e-06)
    return (values * factor * gain).astype(BF16)


def kernel(
    ring, cols,
    slab_in, levels_in, mod_in, w_qkv, q_gain, k_gain, w_out,
    out,
    slab, levels, mod, rows_of, mod_send, tokens, w_buf, gq, gk, wo, qkv, sp_in, sp_out, sp_back, tmp_out, comb,
    x_send, x_recv, part, r_send, r_recv, l_send, l_recv, prev, fin_send, fin_recv,
    loc_sem, pair_send, pair_recv, ag_send, ag_recv, aa_send, aa_recv, rt_send, rt_recv,
    xs_send, xs_recv, rs_send, rs_recv, misc_send, misc_recv, w_send, w_recv,
    wz_send, wz_recv, wp_send, wp_recv, wd_sem,
):
    half = ring // 2
    group = 2 if ring > 4 else 1
    stride = half // group
    peers = ring // stride
    pieces = stride // 2
    slabs = ring
    tok, width = slab.shape[1], slab.shape[2]
    piece = width // W_PIECES
    tm, space = lax.axis_index("tm"), lax.axis_index("space")
    core, z_lo = lax.rem(tm, 2), lax.div(tm, 2)
    me, z_hi = lax.div(space, 2), lax.rem(space, 2)
    z = z_hi * half + z_lo
    other = 1 - core
    inv_root = 1.0 / math.sqrt(HEAD_DIM)

    def mod_ring(value):
        return lax.rem(value + ring, ring)

    def device(plane, of_core, column):
        return (lax.rem(plane, half) * 2 + of_core, column * 2 + lax.div(plane, half))

    right = device(mod_ring(z + 1), core, me)
    left = device(mod_ring(z - 1), core, me)
    partner = device(z, other, me)
    tm_next = (lax.rem(tm + 1, slabs), space)
    tm_far = (lax.rem(tm + jnp.where(core == 1, 1, slabs - 1), slabs), space)

    def remote(src, dst, send_sem, recv_sem, target):
        return pltpu.make_async_remote_copy(
            src_ref=src, dst_ref=dst, send_sem=send_sem, recv_sem=recv_sem,
            device_id=target, device_id_type=MESH,
        )

    barrier = pltpu.get_barrier_semaphore()
    for target in (right, left, partner, tm_far):
        pl.semaphore_signal(barrier, inc=1, device_id=target, device_id_type=MESH)

    def greet(step, carry):
        column = lax.rem(me + step, cols)
        pl.semaphore_signal(barrier, inc=1, device_id=device(z, core, column), device_id_type=MESH)
        return carry

    lax.fori_loop(1, cols, greet, 0)

    def greet_class(step, carry):
        target = device(mod_ring(z + stride * step), core, me)
        pl.semaphore_signal(barrier, inc=1, device_id=target, device_id_type=MESH)
        return carry

    lax.fori_loop(1, peers, greet_class, 0)

    own_head = core == z_hi
    fetch_levels = pltpu.make_async_copy(levels_in, levels, loc_sem.at[2])
    fetch_mod = pltpu.make_async_copy(mod_in, mod, loc_sem.at[3])
    fetch_slab = pltpu.make_async_copy(slab_in, slab, loc_sem.at[4])
    local_w = pltpu.make_async_copy(w_qkv, w_buf, loc_sem.at[0])
    local_wo = pltpu.make_async_copy(w_out, wo.at[0, core], loc_sem.at[1])
    local_gq = pltpu.make_async_copy(q_gain, gq, loc_sem.at[5])
    local_gk = pltpu.make_async_copy(k_gain, gk, loc_sem.at[6])
    fetch_levels.start()
    fetch_mod.start()
    fetch_slab.start()

    @pl.when(own_head)
    def _():
        local_gq.start()
        local_gk.start()
        local_w.start()

    local_wo.start()
    fetch_levels.wait()
    fetch_mod.wait()

    tm_before = lax.rem(tm + slabs - 1, slabs)
    pick_row = lax.broadcasted_iota(jnp.int32, (16, mod.shape[1]), 0)
    pick_col = lax.broadcasted_iota(jnp.int32, (16, mod.shape[1]), 1)
    hot = jnp.zeros((16, mod.shape[1]), F32)
    for at, (batch, of_slab) in enumerate(((0, tm), (1, tm), (0, tm_before), (1, tm_before))):
        hot = jnp.where((pick_row == at) & (pick_col == levels[batch, of_slab]), 1.0, hot)
    for kind in range(3):
        picked = jnp.dot(hot.astype(BF16), mod[kind], preferred_element_type=F32)
        for at in range(4):
            rows_of[kind, at] = picked[at : at + 1]

    def modulate(batch):
        values = slab[batch].astype(F32)
        centre = jnp.mean(values, axis=-1, keepdims=True)
        moved = values - centre
        spread = jnp.mean(jnp.square(moved), axis=-1, keepdims=True)
        normed = moved * lax.rsqrt(spread + 1e-06)
        return (normed * (1.0 + rows_of[1, batch]) + rows_of[0, batch]).astype(BF16)

    fetch_slab.wait()
    mod_send[...] = modulate(other)
    tokens[z * 2 + core] = modulate(core)
    pl.semaphore_wait(barrier, 4 + cols - 1 + peers - 1)

    def gather_copy(way, step, t, origin):
        slot = origin * 2 + t
        return remote(
            tokens.at[slot], tokens.at[slot], ag_send.at[0], ag_recv.at[way, step, t],
            (right, left)[way],
        )

    to_pair = remote(mod_send, tokens.at[z * 2 + core], pair_send.at[0], pair_recv.at[0], partner)
    to_pair.start()
    for way in (0, 1):
        gather_copy(way, 1, core, z).start()
    from_pair = remote(mod_send, tokens.at[z * 2 + other], pair_send.at[0], pair_recv.at[0], partner)
    from_pair.wait_recv()
    for way in (0, 1):
        gather_copy(way, 1, other, z).start()

    def give_w(at):
        rows = pl.ds(at * piece, piece)
        return remote(w_qkv.at[rows], w_buf.at[rows], w_send.at[0], w_recv.at[0], partner)

    whole_w = remote(w_qkv, w_buf, w_send.at[0], w_recv.at[0], partner)
    give_gq = remote(q_gain, gq, pair_send.at[2], pair_recv.at[2], partner)
    give_gk = remote(k_gain, gk, pair_send.at[3], pair_recv.at[3], partner)
    give_wo = remote(w_out, wo.at[0, core], pair_send.at[4], pair_recv.at[4], partner)
    take_wo = remote(w_out, wo.at[0, other], pair_send.at[4], pair_recv.at[4], partner)
    pass_slab = remote(slab, prev, misc_send.at[0], misc_recv.at[0], tm_next)

    @pl.when(own_head)
    def _():
        give_gq.start()
        give_gk.start()

    pairs = group
    rows_w = 2 * HEAD_DIM // cols
    cut_rows = pl.ds(pl.multiple_of(lax.div(me, 2) * rows_w, rows_w), rows_w)
    cut_cols = pl.ds(pl.multiple_of(lax.rem(me, 2) * (width // 2), width // 2), width // 2)

    def plane_piece(at):
        apart = stride * at if 2 * stride * at < half else stride * at - half
        if 2 * stride * at == half:
            apart = jnp.where(core == 0, half // 2, -(half // 2))
        return remote(
            w_out.at[cut_rows, cut_cols], wo.at[at, core, cut_rows, cut_cols],
            wz_send.at[at], wz_recv.at[at], device(mod_ring(z - apart), core, me),
        )

    def spread_piece(column, source):
        rows = pl.ds(pl.multiple_of(lax.div(source, 2) * rows_w, rows_w), rows_w)
        span = pl.ds(pl.multiple_of(lax.rem(source, 2) * (width // 2), width // 2), width // 2)
        piece_of = wo.at[1:pairs, core, rows, span]
        return remote(
            piece_of, piece_of, wp_send.at[column], wp_recv.at[source], device(z, core, column)
        )

    def pair_wo(of_core):
        block = wo.at[1:pairs, of_core]
        return remote(block, block, wd_sem.at[0], wd_sem.at[1], partner)

    for at in range(1, pairs):
        plane_piece(at).start()

    def slab_copy(hi, column, source):
        return remote(
            qkv.at[hi, column], sp_in.at[source, hi], aa_send.at[0], aa_recv.at[0],
            device(z, core, column),
        )

    first_dot = max(1, 3 * half // 8)
    give_steps = max(first_dot - 1, 1)
    per_step = W_PIECES // give_steps

    def gather_step(step, carry):
        step = jnp.asarray(step, jnp.int32)
        plane_a = mod_ring(z - step)
        plane_b = mod_ring(z + step)
        for turn in (0, 1):
            t = core if turn == 0 else other
            for way, origin in ((0, plane_a), (1, plane_b)):

                @pl.when((step < half) | (t == way))
                def _():
                    gather_copy(way, step, t, origin).wait_recv()

                @pl.when((step < half - 1) | ((step == half - 1) & (t == way)))
                def _():
                    gather_copy(way, step + 1, t, origin).start()

        if pairs > 1:

            @pl.when(step == 2)
            def _():
                for at in range(1, pairs):
                    plane_piece(at).wait_recv()

                def spread(ahead, inner):
                    spread_piece(lax.rem(me + ahead, cols), me).start()
                    return inner

                lax.fori_loop(1, cols, spread, 0)

        @pl.when(own_head & (step <= give_steps))
        def _():
            def one(at, inner):
                give_w(at).start()
                return inner

            lax.fori_loop((step - 1) * per_step, step * per_step, one, 0)

        @pl.when(step == first_dot)
        def _():
            give_wo.start()

            @pl.when(own_head)
            def _():
                local_w.wait()
                local_gq.wait()
                local_gk.wait()

            @pl.when(jnp.logical_not(own_head))
            def _():
                whole_w.wait_recv()
                give_gq.wait_recv()
                give_gk.wait_recv()

        def reach(at):
            done = jnp.minimum(2 * (at - first_dot + 1), at + 1)
            return jnp.where(at < first_dot, 0, jnp.where(at == half, half + 1, done))

        lax.fori_loop(reach(step - 1), reach(step), project_step, 0)
        return carry

    def project_step(step, carry):
        planes = (mod_ring(z - step), mod_ring(z + step))
        rows = jnp.concatenate(
            [tokens[pl.ds(plane * 2, 2)].reshape(2 * tok, width) for plane in planes], axis=0
        )
        projected = jnp.dot(rows, w_buf[...], preferred_element_type=F32).astype(BF16)
        queries = head_norm(projected[:, :HEAD_DIM], gq[...])
        keys = head_norm(projected[:, HEAD_DIM : 2 * HEAD_DIM], gk[...])
        values = projected[:, 2 * HEAD_DIM :]
        def place(at):
            hi, lo = lax.div(planes[at], half), lax.rem(planes[at], half)
            for t in (0, 1):
                cut = slice((at * 2 + t) * tok, (at * 2 + t + 1) * tok)
                column = lo * 2 + t
                qkv[hi, column, :, 0:HEAD_DIM] = queries[cut]
                qkv[hi, column, :, HEAD_DIM : 2 * HEAD_DIM] = keys[cut]
                qkv[hi, column, :, 2 * HEAD_DIM :] = values[cut]

                @pl.when(column != me)
                def _():
                    slab_copy(hi, column, me).start()

        place(0)

        @pl.when(lax.rem(step, half) != 0)
        def _():
            place(1)

        return carry

    rows_t = slabs * tok
    at_row = lax.broadcasted_iota(jnp.int32, (rows_t, rows_t), 0) & (tok - 1)
    at_col = lax.broadcasted_iota(jnp.int32, (rows_t, rows_t), 1) & (tok - 1)
    same = at_row == at_col

    def temporal(hi):
        queries = qkv[hi, :, :, 0:HEAD_DIM].reshape(rows_t, HEAD_DIM)
        keys = qkv[hi, :, :, HEAD_DIM : 2 * HEAD_DIM].reshape(rows_t, HEAD_DIM)
        values = qkv[hi, :, :, 2 * HEAD_DIM :].reshape(rows_t, HEAD_DIM)
        scores = jnp.where(same, dot_t(queries, keys) * inv_root, -jnp.inf)
        weights = jnp.exp(scores - jnp.max(scores, axis=-1, keepdims=True))
        total = jnp.sum(weights, axis=-1, keepdims=True)
        mixed = jnp.dot(weights.astype(BF16), values, preferred_element_type=F32) / total
        tmp_out[hi] = mixed.reshape(slabs, tok, HEAD_DIM)

    lax.fori_loop(1, half, gather_step, 0)
    temporal(z_hi)
    gather_step(half, 0)
    pass_slab.start()
    sp_in[me] = qkv[:, me]

    if pairs > 1:

        def await_spread(ahead, carry):
            spread_piece(me, lax.rem(me + ahead, cols)).wait_recv()
            return carry

        lax.fori_loop(1, cols, await_spread, 0)
        pair_wo(core).start()

    mine_late = lax.div(me, 2) == z_lo

    @pl.when(mine_late)
    def _():
        temporal(1 - z_hi)

    part_in = sp_in.at[0 : cols - 1]
    remote(part_in, part_in, aa_send.at[0], aa_recv.at[0], partner).wait_recv()

    is_late = jnp.where(mine_late, 1, 0)

    def back_copy(column, of_slab):
        return remote(
            sp_out.at[column], sp_back.at[:, of_slab], rt_send.at[0], rt_recv.at[is_late],
            device(z, core, column),
        )

    batch_s = 4
    rows_s = batch_s * 2 * tok

    def spatial_step(step, carry):
        keys = sp_in[:, :, :, HEAD_DIM : 2 * HEAD_DIM].reshape(cols * 2 * tok, HEAD_DIM)
        values = sp_in[:, :, :, 2 * HEAD_DIM :].reshape(cols * 2 * tok, HEAD_DIM)
        queries = sp_in[pl.ds(step * batch_s, batch_s), :, :, 0:HEAD_DIM].reshape(rows_s, HEAD_DIM)
        scores = dot_t(queries, keys) * inv_root
        weights = jnp.exp(scores - jnp.max(scores, axis=-1, keepdims=True))
        total = jnp.sum(weights, axis=-1, keepdims=True)
        mixed = jnp.dot(weights.astype(BF16), values, preferred_element_type=F32) / total
        sp_out[pl.ds(step * batch_s, batch_s)] = mixed.astype(BF16).reshape(batch_s, 2, tok, HEAD_DIM)
        for at in range(batch_s):
            column = step * batch_s + at

            @pl.when(column != me)
            def _():
                back_copy(column, me).start()

        return carry

    lax.fori_loop(0, cols // batch_s, spatial_step, 0)
    sp_back[:, me] = sp_out[me]

    @pl.when(jnp.logical_not(mine_late))
    def _():
        temporal(1 - z_hi)


    def await_back(late, count):
        block = sp_back.at[:, 0:count]
        remote(block, block, rt_send.at[0], rt_recv.at[late], partner).wait_recv()

    def combine(ahead, carry):
        of_slab = lax.rem(2 * z_lo + ahead, slabs)
        both = sp_back[:, of_slab].astype(F32) + tmp_out[:, of_slab]
        comb[:, of_slab] = both.astype(BF16)
        return carry

    @pl.when(mine_late)
    def _():
        await_back(0, slabs - 2)

    @pl.when(jnp.logical_not(mine_late))
    def _():
        await_back(0, slabs - 3)

    lax.fori_loop(2, slabs, combine, 0)

    def fill(dst, plane, piece_at):
        def one(at, carry):
            step = lax.div(at, 2)
            block = jnp.where(lax.rem(at, 2) == 0, 2 * stride - 1 - step, step)
            place = lax.rem(2 * plane + 2 * ring - (stride - 1) + block, 2 * ring)
            from_slab = lax.rem(lax.rem(place, slabs) + slabs - 1, slabs)
            dst[at] = comb[lax.div(place, slabs), from_slab]
            return carry

        lax.fori_loop(4 * piece_at, 4 * piece_at + 4, one, 0)

    def head_copy(step, at):
        plane = mod_ring(z + stride * step)
        slot = lax.div(lax.rem(z_lo - lax.rem(plane, half) + half, half), stride)
        rows = pl.ds(4 * at, 4)
        return remote(
            x_send.at[step, rows], x_recv.at[slot, z_hi, rows],
            xs_send.at[step, at], xs_recv.at[slot, z_hi, at], device(plane, core, me),
        )

    def send_heads(step, at):
        fill(x_send.at[step], mod_ring(z + stride * step), at)
        head_copy(step, at).start()

    far = peers // 2
    for at in range(pieces):
        for step in range(1, peers):
            if step != far or at < pieces - 1:
                send_heads(step, at)
    for at in range(pieces - 1):
        fill(x_recv.at[0, z_hi], z, at)

    @pl.when(mine_late)
    def _():
        await_back(1, 1)

    @pl.when(jnp.logical_not(mine_late))
    def _():
        await_back(1, 2)

    lax.fori_loop(0, 2, combine, 0)
    send_heads(far, pieces - 1)
    fill(x_recv.at[0, z_hi], z, pieces - 1)
    local_wo.wait()
    take_wo.wait_recv()
    if pairs > 1:
        pair_wo(other).wait_recv()

    to_pair.wait_send()

    @pl.when(own_head)
    def _():
        whole_w.wait_send()
        give_gq.wait_send()
        give_gk.wait_send()

    give_wo.wait_send()
    pass_slab.wait_send()
    pass_slab.wait_recv()
    for at in range(1, pairs):
        plane_piece(at).wait_send()
    if pairs > 1:
        pair_wo(core).wait_send()

        def drain_spread(ahead, carry):
            spread_piece(lax.rem(me + ahead, cols), me).wait_send()
            return carry

        lax.fori_loop(1, cols, drain_spread, 0)
    sent = tokens.at[0 : 2 * ring - 2]
    remote(sent, sent, ag_send.at[0], ag_recv.at[0, 0, 0], partner).wait_send()
    sent = qkv.at[:, 0 : cols - 1]
    remote(sent, sent, aa_send.at[0], aa_recv.at[0], partner).wait_send()
    sent = sp_out.at[0 : cols - 1]
    remote(sent, sent, rt_send.at[0], rt_recv.at[0], partner).wait_send()

    def await_heads(at):
        for step in range(1, peers):
            plane = mod_ring(z + stride * step)
            slot = lax.div(lax.rem(lax.rem(plane, half) - z_lo + half, half), stride)
            hi = lax.div(plane, half)
            rows = pl.ds(4 * at, 4)
            remote(
                x_send.at[step, rows], x_recv.at[slot, hi, rows],
                xs_send.at[step, at], xs_recv.at[slot, hi, at], device(plane, core, me),
            ).wait_recv()

    def sum_copy(way, step):
        mine, theirs, target = ((r_send, r_recv, right), (l_send, l_recv, left))[way]
        return remote(
            mine.at[step], theirs.at[step], rs_send.at[way, step], rs_recv.at[way, step], target
        )

    chunk = width // SUM_PIECES
    rows_x = 4 * tok
    for step in range(stride - 1):
        if step % 2 == 0:
            await_heads(step // 2)
            rows = slice(2 * step, 2 * step + 4)
            heads = jnp.concatenate(
                [x_recv[at // 2, at % 2, rows].reshape(rows_x, HEAD_DIM) for at in range(2 * pairs)],
                axis=1,
            )
            for at in range(0, width, chunk):
                weights = wo[:, :, :, at : at + chunk].reshape(2 * pairs * HEAD_DIM, chunk)
                product = jnp.dot(heads, weights, preferred_element_type=F32)
                part[rows, :, at : at + chunk] = product.reshape(4, tok, chunk)
        for way, mine, theirs in ((0, r_send, r_recv), (1, l_send, l_recv)):
            share = part[step * 2 + way]
            if step >= 2:
                sum_copy(way, step - 2).wait_recv()
                share = share + theirs[step - 2].astype(F32)
            mine[step] = share.astype(BF16)
            sum_copy(way, step).start()
    for step in range(max(stride - 3, 0), stride - 1):
        for way in (0, 1):
            sum_copy(way, step).wait_recv()

    def total_of(t):
        if stride > 2:
            return (
                part[2 * stride - 1 - t]
                + r_recv[stride - 2 - t].astype(F32)
                + l_recv[stride - 3 + t].astype(F32)
            )
        from_side = jnp.where(t == 0, r_recv[0].astype(F32), l_recv[0].astype(F32))
        return part[2 * stride - 1 - t] + from_side

    fin_send[...] = total_of(other).astype(BF16)
    give_fin = remote(fin_send, fin_recv, misc_send.at[1], misc_recv.at[1], partner)
    give_fin.start()

    def attend(batch, projection):
        gate = rows_of[2, 2 + batch]
        out[batch] = (prev[batch].astype(F32) + gate * projection).astype(BF16)

    attend(core, total_of(core))
    give_fin.wait_recv()
    attend(other, fin_recv[...].astype(F32))

    give_fin.wait_send()
    for step in range(1, peers):
        for at in range(pieces):
            head_copy(step, at).wait_send()
    for step in range(stride - 1):
        for way in (0, 1):
            sum_copy(way, step).wait_send()


def body(slab_queue, levels, mod_table, w_qkv, q_gain, k_gain, w_out):
    batch, _, tok, width = slab_queue.shape
    ring = lax.axis_size("tm")
    cols = lax.axis_size("space") // 2
    half = ring // 2
    group = 2 if ring > 4 else 1
    stride = half // group
    vmem = pl.BlockSpec(memory_space=pltpu.VMEM)
    hbm = pl.BlockSpec(memory_space=pltpu.HBM)
    dma = pltpu.SemaphoreType.DMA
    block = (tok, width)
    return pl.pallas_call(
        functools.partial(kernel, ring, cols),
        out_shape=jax.ShapeDtypeStruct((batch, tok, width), BF16),
        in_specs=[hbm] * 7,
        out_specs=vmem,
        scratch_shapes=[
            pltpu.VMEM((batch,) + block, BF16),
            pltpu.SMEM(levels.shape, jnp.int32),
            pltpu.VMEM((3, mod_table.shape[0], width), BF16),
            pltpu.VMEM((3, 4, 1, width), F32),
            pltpu.VMEM(block, BF16),
            pltpu.VMEM((2 * ring,) + block, BF16),
            pltpu.VMEM((width, 3 * HEAD_DIM), BF16),
            pltpu.VMEM((1, HEAD_DIM), F32),
            pltpu.VMEM((1, HEAD_DIM), F32),
            pltpu.VMEM((group, 2, HEAD_DIM, width), BF16),
            pltpu.VMEM((2, ring, tok, 3 * HEAD_DIM), BF16),
            pltpu.VMEM((cols, 2, tok, 3 * HEAD_DIM), BF16),
            pltpu.VMEM((cols, 2, tok, HEAD_DIM), BF16),
            pltpu.VMEM((2, ring, tok, HEAD_DIM), BF16),
            pltpu.VMEM((2, ring, tok, HEAD_DIM), F32),
            pltpu.VMEM((2, ring, tok, HEAD_DIM), BF16),
            pltpu.VMEM((ring // stride, 2 * stride, tok, HEAD_DIM), BF16),
            pltpu.VMEM((group, 2, 2 * stride, tok, HEAD_DIM), BF16),
            pltpu.VMEM((2 * stride,) + block, F32),
            pltpu.VMEM((stride - 1,) + block, BF16),
            pltpu.VMEM((stride - 1,) + block, BF16),
            pltpu.VMEM((stride - 1,) + block, BF16),
            pltpu.VMEM((stride - 1,) + block, BF16),
            pltpu.VMEM((batch,) + block, BF16),
            pltpu.VMEM(block, BF16),
            pltpu.VMEM(block, BF16),
            dma((7,)),
            dma((5,)),
            dma((5,)),
            dma((1,)),
            dma((2, half + 1, 2)),
            dma((1,)),
            dma((1,)),
            dma((1,)),
            dma((2,)),
            dma((ring // stride, stride // 2)),
            dma((group, 2, stride // 2)),
            dma((2, stride - 1)),
            dma((2, stride - 1)),
            dma((2,)),
            dma((2,)),
            dma((1,)),
            dma((1,)),
            dma((group,)),
            dma((group,)),
            dma((cols,)),
            dma((cols,)),
            dma((2,)),
        ],
        compiler_params=pltpu.CompilerParams(
            collective_id=0, has_side_effects=True, vmem_limit_bytes=VMEM_BYTES
        ),
        cost_estimate=pl.CostEstimate(
            flops=4 * 10**9, bytes_accessed=8 * 10**6, transcendentals=4 * 10**5
        ),
    )(
        slab_queue.reshape(batch, tok, width), levels, jnp.swapaxes(mod_table, 0, 1),
        w_qkv.reshape(width, 3 * HEAD_DIM), q_gain, k_gain, w_out,
    ).reshape(batch, 1, tok, width)


def solution(mesh):
    placed = (
        P(None, "tm", "space", None),
        P(),
        P(),
        P(None, "tm", None),
        P("tm", None),
        P("tm", None),
        P("tm", None),
    )
    return jax.shard_map(
        body, mesh=mesh, in_specs=placed, out_specs=P(None, "tm", "space", None), check_vma=False
    )
```

```python
import functools
import math

import jax
import jax.numpy as jnp
from jax import lax
from jax.experimental import pallas as pl
from jax.experimental.pallas import tpu as pltpu
from jax.sharding import PartitionSpec as P

HEAD_DIM = 128
W_PIECES = 12
RING_PARTS = 2
SUM_PIECES = 4
VMEM_BYTES = 63 * 1024 * 1024
MESH = pl.DeviceIdType.MESH
F32 = jnp.float32
BF16 = jnp.bfloat16


def dot_t(left, right):
    return lax.dot_general(left, right, (((1,), (1,)), ((), ())), preferred_element_type=F32)


def head_norm(values, gain):
    values = values.astype(F32)
    factor = lax.rsqrt(jnp.mean(jnp.square(values), axis=-1, keepdims=True) + 1e-06)
    return (values * factor * gain).astype(BF16)


def kernel(
    ring, cols,
    slab_in, levels_in, mod_in, w_qkv, q_gain, k_gain, w_out,
    out,
    slab, levels, mod, rows_of, mod_send, tokens, w_buf, gq, gk, wo, qkv, sp_in, sp_out, sp_back, tmp_out, comb,
    x_send, x_recv, part, r_send, r_recv, l_send, l_recv, prev, fin_send, fin_recv,
    loc_sem, pair_send, pair_recv, ag_send, ag_recv, aa_send, aa_recv, rt_send, rt_recv,
    xs_send, xs_recv, rs_send, rs_recv, misc_send, misc_recv, w_send, w_recv,
    wz_send, wz_recv, wp_send, wp_recv, wd_sem,
):
    half = ring // 2
    group = 2 if ring > 4 else 1
    stride = half // group
    peers = ring // stride
    pieces = stride // 2
    slabs = ring
    tok, width = slab.shape[1], slab.shape[2]
    piece = width // W_PIECES
    tm, space = lax.axis_index("tm"), lax.axis_index("space")
    core, z_lo = lax.rem(tm, 2), lax.div(tm, 2)
    me, z_hi = lax.div(space, 2), lax.rem(space, 2)
    z = z_hi * half + z_lo
    other = 1 - core
    inv_root = 1.0 / math.sqrt(HEAD_DIM)

    def mod_ring(value):
        return lax.rem(value + ring, ring)

    def device(plane, of_core, column):
        return (lax.rem(plane, half) * 2 + of_core, column * 2 + lax.div(plane, half))

    right = device(mod_ring(z + 1), core, me)
    left = device(mod_ring(z - 1), core, me)
    partner = device(z, other, me)
    tm_next = (lax.rem(tm + 1, slabs), space)
    tm_far = (lax.rem(tm + jnp.where(core == 1, 1, slabs - 1), slabs), space)

    def remote(src, dst, send_sem, recv_sem, target):
        return pltpu.make_async_remote_copy(
            src_ref=src, dst_ref=dst, send_sem=send_sem, recv_sem=recv_sem,
            device_id=target, device_id_type=MESH,
        )

    barrier = pltpu.get_barrier_semaphore()
    for target in (right, left, partner, tm_far):
        pl.semaphore_signal(barrier, inc=1, device_id=target, device_id_type=MESH)

    def greet(step, carry):
        column = lax.rem(me + step, cols)
        pl.semaphore_signal(barrier, inc=1, device_id=device(z, core, column), device_id_type=MESH)
        return carry

    lax.fori_loop(1, cols, greet, 0)

    def greet_class(step, carry):
        target = device(mod_ring(z + stride * step), core, me)
        pl.semaphore_signal(barrier, inc=1, device_id=target, device_id_type=MESH)
        return carry

    lax.fori_loop(1, peers, greet_class, 0)

    own_head = core == z_hi
    fetch_levels = pltpu.make_async_copy(levels_in, levels, loc_sem.at[2])
    fetch_mod = pltpu.make_async_copy(mod_in, mod, loc_sem.at[3])
    fetch_slab = pltpu.make_async_copy(slab_in, slab, loc_sem.at[4])
    local_w = pltpu.make_async_copy(w_qkv, w_buf, loc_sem.at[0])
    local_wo = pltpu.make_async_copy(w_out, wo.at[0, core], loc_sem.at[1])
    local_gq = pltpu.make_async_copy(q_gain, gq, loc_sem.at[5])
    local_gk = pltpu.make_async_copy(k_gain, gk, loc_sem.at[6])
    fetch_levels.start()
    fetch_mod.start()
    fetch_slab.start()

    @pl.when(own_head)
    def _():
        local_gq.start()
        local_gk.start()
        local_w.start()

    local_wo.start()
    fetch_levels.wait()
    fetch_mod.wait()

    tm_before = lax.rem(tm + slabs - 1, slabs)
    pick_row = lax.broadcasted_iota(jnp.int32, (16, mod.shape[1]), 0)
    pick_col = lax.broadcasted_iota(jnp.int32, (16, mod.shape[1]), 1)
    hot = jnp.zeros((16, mod.shape[1]), F32)
    for at, (batch, of_slab) in enumerate(((0, tm), (1, tm), (0, tm_before), (1, tm_before))):
        hot = jnp.where((pick_row == at) & (pick_col == levels[batch, of_slab]), 1.0, hot)
    for kind in range(3):
        picked = jnp.dot(hot.astype(BF16), mod[kind], preferred_element_type=F32)
        for at in range(4):
            rows_of[kind, at] = picked[at : at + 1]

    def modulate(batch):
        values = slab[batch].astype(F32)
        centre = jnp.mean(values, axis=-1, keepdims=True)
        moved = values - centre
        spread = jnp.mean(jnp.square(moved), axis=-1, keepdims=True)
        normed = moved * lax.rsqrt(spread + 1e-06)
        return (normed * (1.0 + rows_of[1, batch]) + rows_of[0, batch]).astype(BF16)

    fetch_slab.wait()
    mod_send[...] = modulate(other)
    tokens[z * 2 + core] = modulate(core)
    pl.semaphore_wait(barrier, 4 + cols - 1 + peers - 1)

    span = width // RING_PARTS

    def gather_copy(way, step, t, origin, at):
        block = tokens.at[origin * 2 + t, :, at * span : (at + 1) * span]
        return remote(
            block, block, ag_send.at[0], ag_recv.at[way, step, t, at], (right, left)[way]
        )

    def gather_start(t):
        for at in range(RING_PARTS):
            for way in (0, 1):
                gather_copy(way, 1, t, z, at).start()

    to_pair = remote(mod_send, tokens.at[z * 2 + core], pair_send.at[0], pair_recv.at[0], partner)
    to_pair.start()
    gather_start(core)
    from_pair = remote(mod_send, tokens.at[z * 2 + other], pair_send.at[0], pair_recv.at[0], partner)
    from_pair.wait_recv()
    gather_start(other)

    def give_w(at):
        rows = pl.ds(at * piece, piece)
        return remote(w_qkv.at[rows], w_buf.at[rows], w_send.at[0], w_recv.at[0], partner)

    whole_w = remote(w_qkv, w_buf, w_send.at[0], w_recv.at[0], partner)
    give_gq = remote(q_gain, gq, pair_send.at[2], pair_recv.at[2], partner)
    give_gk = remote(k_gain, gk, pair_send.at[3], pair_recv.at[3], partner)
    give_wo = remote(w_out, wo.at[0, core], pair_send.at[4], pair_recv.at[4], partner)
    take_wo = remote(w_out, wo.at[0, other], pair_send.at[4], pair_recv.at[4], partner)
    pass_slab = remote(slab, prev, misc_send.at[0], misc_recv.at[0], tm_next)

    @pl.when(own_head)
    def _():
        give_gq.start()
        give_gk.start()

    pairs = group
    rows_w = 2 * HEAD_DIM // cols
    cut_rows = pl.ds(pl.multiple_of(lax.div(me, 2) * rows_w, rows_w), rows_w)
    cut_cols = pl.ds(pl.multiple_of(lax.rem(me, 2) * (width // 2), width // 2), width // 2)

    def plane_piece(at):
        apart = stride * at if 2 * stride * at < half else stride * at - half
        if 2 * stride * at == half:
            apart = jnp.where(core == 0, half // 2, -(half // 2))
        return remote(
            w_out.at[cut_rows, cut_cols], wo.at[at, core, cut_rows, cut_cols],
            wz_send.at[at], wz_recv.at[at], device(mod_ring(z - apart), core, me),
        )

    def spread_piece(column, source):
        rows = pl.ds(pl.multiple_of(lax.div(source, 2) * rows_w, rows_w), rows_w)
        span = pl.ds(pl.multiple_of(lax.rem(source, 2) * (width // 2), width // 2), width // 2)
        piece_of = wo.at[1:pairs, core, rows, span]
        return remote(
            piece_of, piece_of, wp_send.at[column], wp_recv.at[source], device(z, core, column)
        )

    def pair_wo(of_core):
        block = wo.at[1:pairs, of_core]
        return remote(block, block, wd_sem.at[0], wd_sem.at[1], partner)

    for at in range(1, pairs):
        plane_piece(at).start()

    def slab_copy(hi, column, source):
        return remote(
            qkv.at[hi, column], sp_in.at[source, hi], aa_send.at[0], aa_recv.at[0],
            device(z, core, column),
        )

    first_dot = max(1, 3 * half // 8)
    give_steps = max(first_dot - 1, 1)
    per_step = W_PIECES // give_steps

    def gather_step(step, carry):
        step = jnp.asarray(step, jnp.int32)
        plane_a = mod_ring(z - step)
        plane_b = mod_ring(z + step)
        for turn in (0, 1):
            t = core if turn == 0 else other
            for at in range(RING_PARTS):
                for way, origin in ((0, plane_a), (1, plane_b)):

                    @pl.when((step < half) | (t == way))
                    def _():
                        gather_copy(way, step, t, origin, at).wait_recv()

                    @pl.when((step < half - 1) | ((step == half - 1) & (t == way)))
                    def _():
                        gather_copy(way, step + 1, t, origin, at).start()

        if pairs > 1:

            @pl.when(step == 2)
            def _():
                for at in range(1, pairs):
                    plane_piece(at).wait_recv()

                def spread(ahead, inner):
                    spread_piece(lax.rem(me + ahead, cols), me).start()
                    return inner

                lax.fori_loop(1, cols, spread, 0)

        @pl.when(own_head & (step <= give_steps))
        def _():
            def one(at, inner):
                give_w(at).start()
                return inner

            lax.fori_loop((step - 1) * per_step, step * per_step, one, 0)

        @pl.when(step == first_dot)
        def _():
            give_wo.start()

            @pl.when(own_head)
            def _():
                local_w.wait()
                local_gq.wait()
                local_gk.wait()

            @pl.when(jnp.logical_not(own_head))
            def _():
                whole_w.wait_recv()
                give_gq.wait_recv()
                give_gk.wait_recv()

        def reach(at):
            done = jnp.minimum(2 * (at - first_dot + 1), at + 1)
            return jnp.where(at < first_dot, 0, jnp.where(at == half, half + 1, done))

        lax.fori_loop(reach(step - 1), reach(step), project_step, 0)
        return carry

    def project_step(step, carry):
        planes = (mod_ring(z - step), mod_ring(z + step))
        rows = jnp.concatenate(
            [tokens[pl.ds(plane * 2, 2)].reshape(2 * tok, width) for plane in planes], axis=0
        )
        projected = jnp.dot(rows, w_buf[...], preferred_element_type=F32).astype(BF16)
        queries = head_norm(projected[:, :HEAD_DIM], gq[...])
        keys = head_norm(projected[:, HEAD_DIM : 2 * HEAD_DIM], gk[...])
        values = projected[:, 2 * HEAD_DIM :]
        def place(at):
            hi, lo = lax.div(planes[at], half), lax.rem(planes[at], half)
            for t in (0, 1):
                cut = slice((at * 2 + t) * tok, (at * 2 + t + 1) * tok)
                column = lo * 2 + t
                qkv[hi, column, :, 0:HEAD_DIM] = queries[cut]
                qkv[hi, column, :, HEAD_DIM : 2 * HEAD_DIM] = keys[cut]
                qkv[hi, column, :, 2 * HEAD_DIM :] = values[cut]

                @pl.when(column != me)
                def _():
                    slab_copy(hi, column, me).start()

        place(0)

        @pl.when(lax.rem(step, half) != 0)
        def _():
            place(1)

        return carry

    rows_t = slabs * tok
    at_row = lax.broadcasted_iota(jnp.int32, (rows_t, rows_t), 0) & (tok - 1)
    at_col = lax.broadcasted_iota(jnp.int32, (rows_t, rows_t), 1) & (tok - 1)
    same = at_row == at_col

    def temporal(hi):
        queries = qkv[hi, :, :, 0:HEAD_DIM].reshape(rows_t, HEAD_DIM)
        keys = qkv[hi, :, :, HEAD_DIM : 2 * HEAD_DIM].reshape(rows_t, HEAD_DIM)
        values = qkv[hi, :, :, 2 * HEAD_DIM :].reshape(rows_t, HEAD_DIM)
        scores = jnp.where(same, dot_t(queries, keys) * inv_root, -jnp.inf)
        weights = jnp.exp(scores - jnp.max(scores, axis=-1, keepdims=True))
        total = jnp.sum(weights, axis=-1, keepdims=True)
        mixed = jnp.dot(weights.astype(BF16), values, preferred_element_type=F32) / total
        tmp_out[hi] = mixed.reshape(slabs, tok, HEAD_DIM)

    lax.fori_loop(1, half, gather_step, 0)
    temporal(z_hi)
    gather_step(half, 0)
    pass_slab.start()
    sp_in[me] = qkv[:, me]

    if pairs > 1:

        def await_spread(ahead, carry):
            spread_piece(me, lax.rem(me + ahead, cols)).wait_recv()
            return carry

        lax.fori_loop(1, cols, await_spread, 0)
        pair_wo(core).start()

    mine_late = lax.div(me, 2) == z_lo

    @pl.when(mine_late)
    def _():
        temporal(1 - z_hi)

    part_in = sp_in.at[0 : cols - 1]
    remote(part_in, part_in, aa_send.at[0], aa_recv.at[0], partner).wait_recv()

    is_late = jnp.where(mine_late, 1, 0)

    def back_copy(column, of_slab):
        return remote(
            sp_out.at[column], sp_back.at[:, of_slab], rt_send.at[0], rt_recv.at[is_late],
            device(z, core, column),
        )

    batch_s = 4
    rows_s = batch_s * 2 * tok

    def spatial_step(step, carry):
        keys = sp_in[:, :, :, HEAD_DIM : 2 * HEAD_DIM].reshape(cols * 2 * tok, HEAD_DIM)
        values = sp_in[:, :, :, 2 * HEAD_DIM :].reshape(cols * 2 * tok, HEAD_DIM)
        queries = sp_in[pl.ds(step * batch_s, batch_s), :, :, 0:HEAD_DIM].reshape(rows_s, HEAD_DIM)
        scores = dot_t(queries, keys) * inv_root
        weights = jnp.exp(scores - jnp.max(scores, axis=-1, keepdims=True))
        total = jnp.sum(weights, axis=-1, keepdims=True)
        mixed = jnp.dot(weights.astype(BF16), values, preferred_element_type=F32) / total
        sp_out[pl.ds(step * batch_s, batch_s)] = mixed.astype(BF16).reshape(batch_s, 2, tok, HEAD_DIM)
        for at in range(batch_s):
            column = step * batch_s + at

            @pl.when(column != me)
            def _():
                back_copy(column, me).start()

        return carry

    lax.fori_loop(0, cols // batch_s, spatial_step, 0)
    sp_back[:, me] = sp_out[me]

    @pl.when(jnp.logical_not(mine_late))
    def _():
        temporal(1 - z_hi)


    def await_back(late, count):
        block = sp_back.at[:, 0:count]
        remote(block, block, rt_send.at[0], rt_recv.at[late], partner).wait_recv()

    def combine(ahead, carry):
        of_slab = lax.rem(2 * z_lo + ahead, slabs)
        both = sp_back[:, of_slab].astype(F32) + tmp_out[:, of_slab]
        comb[:, of_slab] = both.astype(BF16)
        return carry

    @pl.when(mine_late)
    def _():
        await_back(0, slabs - 2)

    @pl.when(jnp.logical_not(mine_late))
    def _():
        await_back(0, slabs - 3)

    lax.fori_loop(2, slabs, combine, 0)

    def fill(dst, plane, piece_at):
        def one(at, carry):
            step = lax.div(at, 2)
            block = jnp.where(lax.rem(at, 2) == 0, 2 * stride - 1 - step, step)
            place = lax.rem(2 * plane + 2 * ring - (stride - 1) + block, 2 * ring)
            from_slab = lax.rem(lax.rem(place, slabs) + slabs - 1, slabs)
            dst[at] = comb[lax.div(place, slabs), from_slab]
            return carry

        lax.fori_loop(4 * piece_at, 4 * piece_at + 4, one, 0)

    def head_copy(step, at):
        plane = mod_ring(z + stride * step)
        slot = lax.div(lax.rem(z_lo - lax.rem(plane, half) + half, half), stride)
        rows = pl.ds(4 * at, 4)
        return remote(
            x_send.at[step, rows], x_recv.at[slot, z_hi, rows],
            xs_send.at[step, at], xs_recv.at[slot, z_hi, at], device(plane, core, me),
        )

    def send_heads(step, at):
        fill(x_send.at[step], mod_ring(z + stride * step), at)
        head_copy(step, at).start()

    far = peers // 2
    for at in range(pieces):
        for step in range(1, peers):
            if step != far or at < pieces - 1:
                send_heads(step, at)
    for at in range(pieces - 1):
        fill(x_recv.at[0, z_hi], z, at)

    @pl.when(mine_late)
    def _():
        await_back(1, 1)

    @pl.when(jnp.logical_not(mine_late))
    def _():
        await_back(1, 2)

    lax.fori_loop(0, 2, combine, 0)
    send_heads(far, pieces - 1)
    fill(x_recv.at[0, z_hi], z, pieces - 1)
    local_wo.wait()
    take_wo.wait_recv()
    if pairs > 1:
        pair_wo(other).wait_recv()

    to_pair.wait_send()

    @pl.when(own_head)
    def _():
        whole_w.wait_send()
        give_gq.wait_send()
        give_gk.wait_send()

    give_wo.wait_send()
    pass_slab.wait_send()
    pass_slab.wait_recv()
    for at in range(1, pairs):
        plane_piece(at).wait_send()
    if pairs > 1:
        pair_wo(core).wait_send()

        def drain_spread(ahead, carry):
            spread_piece(lax.rem(me + ahead, cols), me).wait_send()
            return carry

        lax.fori_loop(1, cols, drain_spread, 0)
    sent = tokens.at[0 : 2 * ring - 2]
    remote(sent, sent, ag_send.at[0], ag_recv.at[0, 0, 0, 0], partner).wait_send()
    sent = qkv.at[:, 0 : cols - 1]
    remote(sent, sent, aa_send.at[0], aa_recv.at[0], partner).wait_send()
    sent = sp_out.at[0 : cols - 1]
    remote(sent, sent, rt_send.at[0], rt_recv.at[0], partner).wait_send()

    def await_heads(at):
        for step in range(1, peers):
            plane = mod_ring(z + stride * step)
            slot = lax.div(lax.rem(lax.rem(plane, half) - z_lo + half, half), stride)
            hi = lax.div(plane, half)
            rows = pl.ds(4 * at, 4)
            remote(
                x_send.at[step, rows], x_recv.at[slot, hi, rows],
                xs_send.at[step, at], xs_recv.at[slot, hi, at], device(plane, core, me),
            ).wait_recv()

    def sum_copy(way, step):
        mine, theirs, target = ((r_send, r_recv, right), (l_send, l_recv, left))[way]
        return remote(
            mine.at[step], theirs.at[step], rs_send.at[way, step], rs_recv.at[way, step], target
        )

    chunk = width // SUM_PIECES
    rows_x = 4 * tok
    for step in range(stride - 1):
        if step % 2 == 0:
            await_heads(step // 2)
            rows = slice(2 * step, 2 * step + 4)
            heads = jnp.concatenate(
                [x_recv[at // 2, at % 2, rows].reshape(rows_x, HEAD_DIM) for at in range(2 * pairs)],
                axis=1,
            )
            for at in range(0, width, chunk):
                weights = wo[:, :, :, at : at + chunk].reshape(2 * pairs * HEAD_DIM, chunk)
                product = jnp.dot(heads, weights, preferred_element_type=F32)
                part[rows, :, at : at + chunk] = product.reshape(4, tok, chunk)
        for way, mine, theirs in ((0, r_send, r_recv), (1, l_send, l_recv)):
            share = part[step * 2 + way]
            if step >= 2:
                sum_copy(way, step - 2).wait_recv()
                share = share + theirs[step - 2].astype(F32)
            mine[step] = share.astype(BF16)
            sum_copy(way, step).start()
    for step in range(max(stride - 3, 0), stride - 1):
        for way in (0, 1):
            sum_copy(way, step).wait_recv()

    def total_of(t):
        if stride > 2:
            return (
                part[2 * stride - 1 - t]
                + r_recv[stride - 2 - t].astype(F32)
                + l_recv[stride - 3 + t].astype(F32)
            )
        from_side = jnp.where(t == 0, r_recv[0].astype(F32), l_recv[0].astype(F32))
        return part[2 * stride - 1 - t] + from_side

    fin_send[...] = total_of(other).astype(BF16)
    give_fin = remote(fin_send, fin_recv, misc_send.at[1], misc_recv.at[1], partner)
    give_fin.start()

    def attend(batch, projection):
        gate = rows_of[2, 2 + batch]
        out[batch] = (prev[batch].astype(F32) + gate * projection).astype(BF16)

    attend(core, total_of(core))
    give_fin.wait_recv()
    attend(other, fin_recv[...].astype(F32))

    give_fin.wait_send()
    for step in range(1, peers):
        for at in range(pieces):
            head_copy(step, at).wait_send()
    for step in range(stride - 1):
        for way in (0, 1):
            sum_copy(way, step).wait_send()


def body(slab_queue, levels, mod_table, w_qkv, q_gain, k_gain, w_out):
    batch, _, tok, width = slab_queue.shape
    ring = lax.axis_size("tm")
    cols = lax.axis_size("space") // 2
    half = ring // 2
    group = 2 if ring > 4 else 1
    stride = half // group
    vmem = pl.BlockSpec(memory_space=pltpu.VMEM)
    hbm = pl.BlockSpec(memory_space=pltpu.HBM)
    dma = pltpu.SemaphoreType.DMA
    block = (tok, width)
    return pl.pallas_call(
        functools.partial(kernel, ring, cols),
        out_shape=pltpu.VMEM((batch, tok, width), BF16),
        in_specs=[hbm] * 7,
        out_specs=vmem,
        scratch_shapes=[
            pltpu.VMEM((batch,) + block, BF16),
            pltpu.SMEM(levels.shape, jnp.int32),
            pltpu.VMEM((3, mod_table.shape[0], width), BF16),
            pltpu.VMEM((3, 4, 1, width), F32),
            pltpu.VMEM(block, BF16),
            pltpu.VMEM((2 * ring,) + block, BF16),
            pltpu.VMEM((width, 3 * HEAD_DIM), BF16),
            pltpu.VMEM((1, HEAD_DIM), F32),
            pltpu.VMEM((1, HEAD_DIM), F32),
            pltpu.VMEM((group, 2, HEAD_DIM, width), BF16),
            pltpu.VMEM((2, ring, tok, 3 * HEAD_DIM), BF16),
            pltpu.VMEM((cols, 2, tok, 3 * HEAD_DIM), BF16),
            pltpu.VMEM((cols, 2, tok, HEAD_DIM), BF16),
            pltpu.VMEM((2, ring, tok, HEAD_DIM), BF16),
            pltpu.VMEM((2, ring, tok, HEAD_DIM), F32),
            pltpu.VMEM((2, ring, tok, HEAD_DIM), BF16),
            pltpu.VMEM((ring // stride, 2 * stride, tok, HEAD_DIM), BF16),
            pltpu.VMEM((group, 2, 2 * stride, tok, HEAD_DIM), BF16),
            pltpu.VMEM((2 * stride,) + block, F32),
            pltpu.VMEM((stride - 1,) + block, BF16),
            pltpu.VMEM((stride - 1,) + block, BF16),
            pltpu.VMEM((stride - 1,) + block, BF16),
            pltpu.VMEM((stride - 1,) + block, BF16),
            pltpu.VMEM((batch,) + block, BF16),
            pltpu.VMEM(block, BF16),
            pltpu.VMEM(block, BF16),
            dma((7,)),
            dma((5,)),
            dma((5,)),
            dma((1,)),
            dma((2, half + 1, 2, RING_PARTS)),
            dma((1,)),
            dma((1,)),
            dma((1,)),
            dma((2,)),
            dma((ring // stride, stride // 2)),
            dma((group, 2, stride // 2)),
            dma((2, stride - 1)),
            dma((2, stride - 1)),
            dma((2,)),
            dma((2,)),
            dma((1,)),
            dma((1,)),
            dma((group,)),
            dma((group,)),
            dma((cols,)),
            dma((cols,)),
            dma((2,)),
        ],
        compiler_params=pltpu.CompilerParams(
            collective_id=0, has_side_effects=True, vmem_limit_bytes=VMEM_BYTES
        ),
        cost_estimate=pl.CostEstimate(
            flops=4 * 10**9, bytes_accessed=8 * 10**6, transcendentals=4 * 10**5
        ),
    )(
        slab_queue.reshape(batch, tok, width), levels, jnp.swapaxes(mod_table, 0, 1),
        w_qkv.reshape(width, 3 * HEAD_DIM), q_gain, k_gain, w_out,
    ).reshape(batch, 1, tok, width)


def solution(mesh):
    placed = (
        P(None, "tm", "space", None),
        P(),
        P(),
        P(None, "tm", None),
        P("tm", None),
        P("tm", None),
        P("tm", None),
    )
    return jax.shard_map(
        body, mesh=mesh, in_specs=placed, out_specs=P(None, "tm", "space", None), check_vma=False
    )
```

```python
import functools
import math

import jax
import jax.numpy as jnp
from jax import lax
from jax.experimental import pallas as pl
from jax.experimental.pallas import tpu as pltpu
from jax.sharding import PartitionSpec as P

HEAD_DIM = 128
W_PIECES = 12
RING_PARTS = 2
SUM_PIECES = 4
SUM_PARTS = 2
VMEM_BYTES = 63 * 1024 * 1024
MESH = pl.DeviceIdType.MESH
F32 = jnp.float32
BF16 = jnp.bfloat16


def dot_t(left, right):
    return lax.dot_general(left, right, (((1,), (1,)), ((), ())), preferred_element_type=F32)


def head_norm(values, gain):
    values = values.astype(F32)
    factor = lax.rsqrt(jnp.mean(jnp.square(values), axis=-1, keepdims=True) + 1e-06)
    return (values * factor * gain).astype(BF16)


def kernel(
    ring, cols,
    slab_in, levels_in, mod_in, w_qkv, q_gain, k_gain, w_out,
    out,
    slab, levels, mod, rows_of, mod_send, tokens, w_buf, gq, gk, wo, qkv, sp_in, sp_out, sp_back, tmp_out, comb,
    x_send, x_recv, part, r_send, r_recv, l_send, l_recv, r_last, l_last, prev, fin_send, fin_recv,
    loc_sem, pair_send, pair_recv, ag_send, ag_recv, aa_send, aa_recv, rt_send, rt_recv,
    xs_send, xs_recv, rs_send, rs_recv, last_recv, misc_send, misc_recv, w_send, w_recv,
    wz_send, wz_recv, wp_send, wp_recv, wd_sem,
):
    half = ring // 2
    group = 2 if ring > 4 else 1
    stride = half // group
    peers = ring // stride
    pieces = stride // 2
    slabs = ring
    tok, width = slab.shape[1], slab.shape[2]
    piece = width // W_PIECES
    tm, space = lax.axis_index("tm"), lax.axis_index("space")
    core, z_lo = lax.rem(tm, 2), lax.div(tm, 2)
    me, z_hi = lax.div(space, 2), lax.rem(space, 2)
    z = z_hi * half + z_lo
    other = 1 - core
    inv_root = 1.0 / math.sqrt(HEAD_DIM)

    def mod_ring(value):
        return lax.rem(value + ring, ring)

    def device(plane, of_core, column):
        return (lax.rem(plane, half) * 2 + of_core, column * 2 + lax.div(plane, half))

    right = device(mod_ring(z + 1), core, me)
    left = device(mod_ring(z - 1), core, me)
    partner = device(z, other, me)
    tm_next = (lax.rem(tm + 1, slabs), space)
    tm_far = (lax.rem(tm + jnp.where(core == 1, 1, slabs - 1), slabs), space)

    def remote(src, dst, send_sem, recv_sem, target):
        return pltpu.make_async_remote_copy(
            src_ref=src, dst_ref=dst, send_sem=send_sem, recv_sem=recv_sem,
            device_id=target, device_id_type=MESH,
        )

    barrier = pltpu.get_barrier_semaphore()
    right_of = [device(mod_ring(z + 1), at, me) for at in (0, 1)]
    left_of = [device(mod_ring(z - 1), at, me) for at in (0, 1)]
    for target in (*right_of, *left_of, partner, tm_far):
        pl.semaphore_signal(barrier, inc=1, device_id=target, device_id_type=MESH)

    def greet(step, carry):
        column = lax.rem(me + step, cols)
        pl.semaphore_signal(barrier, inc=1, device_id=device(z, core, column), device_id_type=MESH)
        return carry

    lax.fori_loop(1, cols, greet, 0)

    def greet_class(step, carry):
        target = device(mod_ring(z + stride * step), core, me)
        pl.semaphore_signal(barrier, inc=1, device_id=target, device_id_type=MESH)
        return carry

    lax.fori_loop(1, peers, greet_class, 0)

    own_head = core == z_hi
    fetch_levels = pltpu.make_async_copy(levels_in, levels, loc_sem.at[2])
    fetch_mod = pltpu.make_async_copy(mod_in, mod, loc_sem.at[3])
    fetch_slab = pltpu.make_async_copy(slab_in, slab, loc_sem.at[4])
    local_w = pltpu.make_async_copy(w_qkv, w_buf, loc_sem.at[0])
    local_wo = pltpu.make_async_copy(w_out, wo.at[0, core], loc_sem.at[1])
    local_gq = pltpu.make_async_copy(q_gain, gq, loc_sem.at[5])
    local_gk = pltpu.make_async_copy(k_gain, gk, loc_sem.at[6])
    fetch_levels.start()
    fetch_mod.start()
    fetch_slab.start()

    @pl.when(own_head)
    def _():
        local_gq.start()
        local_gk.start()
        local_w.start()

    local_wo.start()
    fetch_levels.wait()
    fetch_mod.wait()

    tm_before = lax.rem(tm + slabs - 1, slabs)
    pick_row = lax.broadcasted_iota(jnp.int32, (16, mod.shape[1]), 0)
    pick_col = lax.broadcasted_iota(jnp.int32, (16, mod.shape[1]), 1)
    hot = jnp.zeros((16, mod.shape[1]), F32)
    for at, (batch, of_slab) in enumerate(((0, tm), (1, tm), (0, tm_before), (1, tm_before))):
        hot = jnp.where((pick_row == at) & (pick_col == levels[batch, of_slab]), 1.0, hot)
    for kind in range(3):
        picked = jnp.dot(hot.astype(BF16), mod[kind], preferred_element_type=F32)
        for at in range(4):
            rows_of[kind, at] = picked[at : at + 1]

    def modulate(batch):
        values = slab[batch].astype(F32)
        centre = jnp.mean(values, axis=-1, keepdims=True)
        moved = values - centre
        spread = jnp.mean(jnp.square(moved), axis=-1, keepdims=True)
        normed = moved * lax.rsqrt(spread + 1e-06)
        return (normed * (1.0 + rows_of[1, batch]) + rows_of[0, batch]).astype(BF16)

    fetch_slab.wait()
    mod_send[...] = modulate(other)
    tokens[z * 2 + core] = modulate(core)
    pl.semaphore_wait(barrier, 6 + cols - 1 + peers - 1)

    span = width // RING_PARTS

    def gather_copy(way, step, t, origin, at):
        block = tokens.at[origin * 2 + t, :, at * span : (at + 1) * span]
        return remote(
            block, block, ag_send.at[0], ag_recv.at[way, step, t, at], (right, left)[way]
        )

    def gather_start(t):
        for at in range(RING_PARTS):
            for way in (0, 1):
                gather_copy(way, 1, t, z, at).start()

    to_pair = remote(mod_send, tokens.at[z * 2 + core], pair_send.at[0], pair_recv.at[0], partner)
    to_pair.start()
    gather_start(core)
    from_pair = remote(mod_send, tokens.at[z * 2 + other], pair_send.at[0], pair_recv.at[0], partner)
    from_pair.wait_recv()
    gather_start(other)

    def give_w(at):
        rows = pl.ds(at * piece, piece)
        return remote(w_qkv.at[rows], w_buf.at[rows], w_send.at[0], w_recv.at[0], partner)

    whole_w = remote(w_qkv, w_buf, w_send.at[0], w_recv.at[0], partner)
    give_gq = remote(q_gain, gq, pair_send.at[2], pair_recv.at[2], partner)
    give_gk = remote(k_gain, gk, pair_send.at[3], pair_recv.at[3], partner)
    give_wo = remote(w_out, wo.at[0, core], pair_send.at[4], pair_recv.at[4], partner)
    take_wo = remote(w_out, wo.at[0, other], pair_send.at[4], pair_recv.at[4], partner)
    pass_slab = remote(slab, prev, misc_send.at[0], misc_recv.at[0], tm_next)

    @pl.when(own_head)
    def _():
        give_gq.start()
        give_gk.start()

    pairs = group
    rows_w = 2 * HEAD_DIM // cols
    cut_rows = pl.ds(pl.multiple_of(lax.div(me, 2) * rows_w, rows_w), rows_w)
    cut_cols = pl.ds(pl.multiple_of(lax.rem(me, 2) * (width // 2), width // 2), width // 2)

    def plane_piece(at):
        apart = stride * at if 2 * stride * at < half else stride * at - half
        if 2 * stride * at == half:
            apart = jnp.where(core == 0, half // 2, -(half // 2))
        return remote(
            w_out.at[cut_rows, cut_cols], wo.at[at, core, cut_rows, cut_cols],
            wz_send.at[at], wz_recv.at[at], device(mod_ring(z - apart), core, me),
        )

    def spread_piece(column, source):
        rows = pl.ds(pl.multiple_of(lax.div(source, 2) * rows_w, rows_w), rows_w)
        span = pl.ds(pl.multiple_of(lax.rem(source, 2) * (width // 2), width // 2), width // 2)
        piece_of = wo.at[1:pairs, core, rows, span]
        return remote(
            piece_of, piece_of, wp_send.at[column], wp_recv.at[source], device(z, core, column)
        )

    def pair_wo(of_core):
        block = wo.at[1:pairs, of_core]
        return remote(block, block, wd_sem.at[0], wd_sem.at[1], partner)

    for at in range(1, pairs):
        plane_piece(at).start()

    def slab_copy(hi, column, source):
        return remote(
            qkv.at[hi, column], sp_in.at[source, hi], aa_send.at[0], aa_recv.at[0],
            device(z, core, column),
        )

    first_dot = max(1, 3 * half // 8)
    give_steps = max(first_dot - 1, 1)
    per_step = W_PIECES // give_steps

    def reach(at):
        done = jnp.minimum(2 * (at - first_dot + 1), at + 1)
        return jnp.where(at < first_dot, 0, jnp.where(at == half, half + 1, done))

    def gather_step(step, carry):
        step = jnp.asarray(step, jnp.int32)
        plane_a = mod_ring(z - step)
        plane_b = mod_ring(z + step)
        first, last = reach(step - 1), reach(step)
        middle = jnp.where(last - first == 2, first + 1, first)

        def turn_step(turn, inner):
            t = jnp.where(turn == 0, core, other)
            for at in range(RING_PARTS):
                for way, origin in ((0, plane_a), (1, plane_b)):

                    @pl.when((step < half) | (t == way))
                    def _():
                        gather_copy(way, step, t, origin, at).wait_recv()

                    @pl.when((step < half - 1) | ((step == half - 1) & (t == way)))
                    def _():
                        gather_copy(way, step + 1, t, origin, at).start()

            if pairs > 1:

                @pl.when((step == 2) & (turn == 0))
                def _():
                    for at in range(1, pairs):
                        plane_piece(at).wait_recv()

                    def spread(ahead, most):
                        spread_piece(lax.rem(me + ahead, cols), me).start()
                        return most

                    lax.fori_loop(1, cols, spread, 0)

            @pl.when(own_head & (step <= give_steps))
            def _():
                def one(at, most):
                    give_w(at).start()
                    return most

                share = per_step // 2
                begin = (2 * (step - 1) + turn) * share
                lax.fori_loop(begin, begin + share, one, 0)

            @pl.when((step == first_dot) & (turn == 0))
            def _():
                give_wo.start()

                @pl.when(own_head)
                def _():
                    local_w.wait()
                    local_gq.wait()
                    local_gk.wait()

                @pl.when(jnp.logical_not(own_head))
                def _():
                    whole_w.wait_recv()
                    give_gq.wait_recv()
                    give_gk.wait_recv()

            lax.fori_loop(
                jnp.where(turn == 0, first, middle), jnp.where(turn == 0, middle, last),
                project_step, 0,
            )
            return inner

        lax.fori_loop(0, 2, turn_step, 0)
        return carry

    def project_step(step, carry):
        planes = (mod_ring(z - step), mod_ring(z + step))
        rows = jnp.concatenate(
            [tokens[pl.ds(plane * 2, 2)].reshape(2 * tok, width) for plane in planes], axis=0
        )
        projected = jnp.dot(rows, w_buf[...], preferred_element_type=F32).astype(BF16)
        queries = head_norm(projected[:, :HEAD_DIM], gq[...])
        keys = head_norm(projected[:, HEAD_DIM : 2 * HEAD_DIM], gk[...])
        values = projected[:, 2 * HEAD_DIM :]
        def place(at):
            hi, lo = lax.div(planes[at], half), lax.rem(planes[at], half)
            for t in (0, 1):
                cut = slice((at * 2 + t) * tok, (at * 2 + t + 1) * tok)
                column = lo * 2 + t
                qkv[hi, column, :, 0:HEAD_DIM] = queries[cut]
                qkv[hi, column, :, HEAD_DIM : 2 * HEAD_DIM] = keys[cut]
                qkv[hi, column, :, 2 * HEAD_DIM :] = values[cut]

                @pl.when(column != me)
                def _():
                    slab_copy(hi, column, me).start()

        place(0)

        @pl.when(lax.rem(step, half) != 0)
        def _():
            place(1)

        return carry

    rows_t = slabs * tok
    at_row = lax.broadcasted_iota(jnp.int32, (rows_t, rows_t), 0) & (tok - 1)
    at_col = lax.broadcasted_iota(jnp.int32, (rows_t, rows_t), 1) & (tok - 1)
    same = at_row == at_col

    def temporal(hi):
        queries = qkv[hi, :, :, 0:HEAD_DIM].reshape(rows_t, HEAD_DIM)
        keys = qkv[hi, :, :, HEAD_DIM : 2 * HEAD_DIM].reshape(rows_t, HEAD_DIM)
        values = qkv[hi, :, :, 2 * HEAD_DIM :].reshape(rows_t, HEAD_DIM)
        scores = jnp.where(same, dot_t(queries, keys) * inv_root, -jnp.inf)
        weights = jnp.exp(scores - jnp.max(scores, axis=-1, keepdims=True))
        total = jnp.sum(weights, axis=-1, keepdims=True)
        mixed = jnp.dot(weights.astype(BF16), values, preferred_element_type=F32) / total
        tmp_out[hi] = mixed.reshape(slabs, tok, HEAD_DIM)

    lax.fori_loop(1, half, gather_step, 0)
    temporal(z_hi)
    gather_step(half, 0)
    pass_slab.start()
    sp_in[me] = qkv[:, me]

    if pairs > 1:

        def await_spread(ahead, carry):
            spread_piece(me, lax.rem(me + ahead, cols)).wait_recv()
            return carry

        lax.fori_loop(1, cols, await_spread, 0)
        pair_wo(core).start()

    mine_late = lax.div(me, 2) == z_lo

    @pl.when(mine_late)
    def _():
        temporal(1 - z_hi)

    part_in = sp_in.at[0 : cols - 1]
    remote(part_in, part_in, aa_send.at[0], aa_recv.at[0], partner).wait_recv()

    is_late = jnp.where(mine_late, 1, 0)

    def back_copy(column, of_slab):
        return remote(
            sp_out.at[column], sp_back.at[:, of_slab], rt_send.at[0], rt_recv.at[is_late],
            device(z, core, column),
        )

    batch_s = 4
    rows_s = batch_s * 2 * tok

    def spatial_step(step, carry):
        keys = sp_in[:, :, :, HEAD_DIM : 2 * HEAD_DIM].reshape(cols * 2 * tok, HEAD_DIM)
        values = sp_in[:, :, :, 2 * HEAD_DIM :].reshape(cols * 2 * tok, HEAD_DIM)
        queries = sp_in[pl.ds(step * batch_s, batch_s), :, :, 0:HEAD_DIM].reshape(rows_s, HEAD_DIM)
        scores = dot_t(queries, keys) * inv_root
        weights = jnp.exp(scores - jnp.max(scores, axis=-1, keepdims=True))
        total = jnp.sum(weights, axis=-1, keepdims=True)
        mixed = jnp.dot(weights.astype(BF16), values, preferred_element_type=F32) / total
        sp_out[pl.ds(step * batch_s, batch_s)] = mixed.astype(BF16).reshape(batch_s, 2, tok, HEAD_DIM)
        for at in range(batch_s):
            column = step * batch_s + at

            @pl.when(column != me)
            def _():
                back_copy(column, me).start()

        return carry

    lax.fori_loop(0, cols // batch_s, spatial_step, 0)
    sp_back[:, me] = sp_out[me]

    @pl.when(jnp.logical_not(mine_late))
    def _():
        temporal(1 - z_hi)


    def await_back(late, count):
        block = sp_back.at[:, 0:count]
        remote(block, block, rt_send.at[0], rt_recv.at[late], partner).wait_recv()

    def combine(ahead, carry):
        of_slab = lax.rem(2 * z_lo + ahead, slabs)
        both = sp_back[:, of_slab].astype(F32) + tmp_out[:, of_slab]
        comb[:, of_slab] = both.astype(BF16)
        return carry

    @pl.when(mine_late)
    def _():
        await_back(0, slabs - 2)

    @pl.when(jnp.logical_not(mine_late))
    def _():
        await_back(0, slabs - 3)

    lax.fori_loop(2, slabs, combine, 0)

    def fill(dst, plane, piece_at):
        def one(at, carry):
            step = lax.div(at, 2)
            block = jnp.where(lax.rem(at, 2) == 0, 2 * stride - 1 - step, step)
            place = lax.rem(2 * plane + 2 * ring - (stride - 1) + block, 2 * ring)
            from_slab = lax.rem(lax.rem(place, slabs) + slabs - 1, slabs)
            dst[at] = comb[lax.div(place, slabs), from_slab]
            return carry

        lax.fori_loop(4 * piece_at, 4 * piece_at + 4, one, 0)

    def head_copy(step, at):
        plane = mod_ring(z + stride * step)
        slot = lax.div(lax.rem(z_lo - lax.rem(plane, half) + half, half), stride)
        rows = pl.ds(4 * at, 4)
        return remote(
            x_send.at[step, rows], x_recv.at[slot, z_hi, rows],
            xs_send.at[step, at], xs_recv.at[slot, z_hi, at], device(plane, core, me),
        )

    def send_heads(step, at):
        fill(x_send.at[step], mod_ring(z + stride * step), at)
        head_copy(step, at).start()

    far = peers // 2
    for at in range(pieces):
        for step in range(1, peers):
            if step != far or at < pieces - 1:
                send_heads(step, at)
    for at in range(pieces - 1):
        fill(x_recv.at[0, z_hi], z, at)

    @pl.when(mine_late)
    def _():
        await_back(1, 1)

    @pl.when(jnp.logical_not(mine_late))
    def _():
        await_back(1, 2)

    lax.fori_loop(0, 2, combine, 0)
    send_heads(far, pieces - 1)
    fill(x_recv.at[0, z_hi], z, pieces - 1)
    local_wo.wait()
    take_wo.wait_recv()
    if pairs > 1:
        pair_wo(other).wait_recv()

    to_pair.wait_send()

    @pl.when(own_head)
    def _():
        whole_w.wait_send()
        give_gq.wait_send()
        give_gk.wait_send()

    give_wo.wait_send()
    pass_slab.wait_send()
    pass_slab.wait_recv()
    for at in range(1, pairs):
        plane_piece(at).wait_send()
    if pairs > 1:
        pair_wo(core).wait_send()

        def drain_spread(ahead, carry):
            spread_piece(lax.rem(me + ahead, cols), me).wait_send()
            return carry

        lax.fori_loop(1, cols, drain_spread, 0)
    sent = tokens.at[0 : 2 * ring - 2]
    remote(sent, sent, ag_send.at[0], ag_recv.at[0, 0, 0, 0], partner).wait_send()
    sent = qkv.at[:, 0 : cols - 1]
    remote(sent, sent, aa_send.at[0], aa_recv.at[0], partner).wait_send()
    sent = sp_out.at[0 : cols - 1]
    remote(sent, sent, rt_send.at[0], rt_recv.at[0], partner).wait_send()

    def await_heads(at):
        for step in range(1, peers):
            plane = mod_ring(z + stride * step)
            slot = lax.div(lax.rem(lax.rem(plane, half) - z_lo + half, half), stride)
            hi = lax.div(plane, half)
            rows = pl.ds(4 * at, 4)
            remote(
                x_send.at[step, rows], x_recv.at[slot, hi, rows],
                xs_send.at[step, at], xs_recv.at[slot, hi, at], device(plane, core, me),
            ).wait_recv()

    def final_core(way, step):
        if step < stride - 3:
            return None
        return (step == stride - 3) != (way == 1) and 1 or 0

    def sum_copy(way, step, at):
        mine, theirs, ends = ((r_send, r_recv, r_last), (l_send, l_recv, l_last))[way]
        span_s = slice(at * sum_span, (at + 1) * sum_span)
        dst = theirs.at[step, :, span_s]
        sem = rs_recv.at[way, step, at]
        target = (right, left)[way]
        to_core = final_core(way, step)
        if to_core is not None:
            dst = ends.at[core, :, span_s]
            sem = last_recv.at[way, core, at]
            target = (right_of, left_of)[way][to_core]
        return remote(mine.at[step, :, span_s], dst, rs_send.at[way, step, at], sem, target)

    sum_span = width // SUM_PARTS
    chunk = width // SUM_PIECES
    rows_x = 4 * tok
    for step in range(stride - 1):
        if step % 2 == 0:
            await_heads(step // 2)
            rows = slice(2 * step, 2 * step + 4)
            heads = jnp.concatenate(
                [x_recv[at // 2, at % 2, rows].reshape(rows_x, HEAD_DIM) for at in range(2 * pairs)],
                axis=1,
            )
        for part_at in range(SUM_PARTS):
            span_s = slice(part_at * sum_span, (part_at + 1) * sum_span)
            if step % 2 == 0:
                for at in range(part_at * sum_span, (part_at + 1) * sum_span, chunk):
                    weights = wo[:, :, :, at : at + chunk].reshape(2 * pairs * HEAD_DIM, chunk)
                    product = jnp.dot(heads, weights, preferred_element_type=F32)
                    part[rows, :, at : at + chunk] = product.reshape(4, tok, chunk)
            for way, mine, theirs in ((0, r_send, r_recv), (1, l_send, l_recv)):
                share = part[step * 2 + way, :, span_s]
                if step >= 2:
                    sum_copy(way, step - 2, part_at).wait_recv()
                    share = share + theirs[step - 2, :, span_s].astype(F32)
                mine[step, :, span_s] = share.astype(BF16)
                sum_copy(way, step, part_at).start()

    fin_send[...] = part[2 * stride - 1 - other].astype(BF16)
    give_fin = remote(fin_send, fin_recv, misc_send.at[1], misc_recv.at[1], partner)
    give_fin.start()

    def await_last(way, batch):
        ends = (r_last, l_last)[way]
        for at in range(SUM_PARTS):
            dst = ends.at[batch, :, at * sum_span : (at + 1) * sum_span]
            remote(
                dst, dst, rs_send.at[way, 0, at], last_recv.at[way, batch, at], partner
            ).wait_recv()

    def attend(batch, own_share):
        gate = rows_of[2, 2 + batch]
        if stride > 2:
            for way in (0, 1):
                await_last(way, batch)
            sides = r_last[batch].astype(F32) + l_last[batch].astype(F32)
        else:
            for way in (0, 1):

                @pl.when(core == way)
                def _():
                    await_last(way, batch)

            sides = jnp.where(core == 0, r_last[batch].astype(F32), l_last[batch].astype(F32))
        projection = own_share + sides
        out[batch] = (prev[batch].astype(F32) + gate * projection).astype(BF16)

    attend(core, part[2 * stride - 1 - core])
    give_fin.wait_recv()
    attend(other, fin_recv[...].astype(F32))

    give_fin.wait_send()
    for step in range(1, peers):
        for at in range(pieces):
            head_copy(step, at).wait_send()
    for step in range(stride - 1):
        for way in (0, 1):
            for at in range(SUM_PARTS):
                sum_copy(way, step, at).wait_send()


def body(slab_queue, levels, mod_table, w_qkv, q_gain, k_gain, w_out):
    batch, _, tok, width = slab_queue.shape
    ring = lax.axis_size("tm")
    cols = lax.axis_size("space") // 2
    half = ring // 2
    group = 2 if ring > 4 else 1
    stride = half // group
    vmem = pl.BlockSpec(memory_space=pltpu.VMEM)
    hbm = pl.BlockSpec(memory_space=pltpu.HBM)
    dma = pltpu.SemaphoreType.DMA
    block = (tok, width)
    return pl.pallas_call(
        functools.partial(kernel, ring, cols),
        out_shape=pltpu.VMEM((batch, tok, width), BF16),
        in_specs=[hbm] * 7,
        out_specs=vmem,
        scratch_shapes=[
            pltpu.VMEM((batch,) + block, BF16),
            pltpu.SMEM(levels.shape, jnp.int32),
            pltpu.VMEM((3, mod_table.shape[0], width), BF16),
            pltpu.VMEM((3, 4, 1, width), F32),
            pltpu.VMEM(block, BF16),
            pltpu.VMEM((2 * ring,) + block, BF16),
            pltpu.VMEM((width, 3 * HEAD_DIM), BF16),
            pltpu.VMEM((1, HEAD_DIM), F32),
            pltpu.VMEM((1, HEAD_DIM), F32),
            pltpu.VMEM((group, 2, HEAD_DIM, width), BF16),
            pltpu.VMEM((2, ring, tok, 3 * HEAD_DIM), BF16),
            pltpu.VMEM((cols, 2, tok, 3 * HEAD_DIM), BF16),
            pltpu.VMEM((cols, 2, tok, HEAD_DIM), BF16),
            pltpu.VMEM((2, ring, tok, HEAD_DIM), BF16),
            pltpu.VMEM((2, ring, tok, HEAD_DIM), F32),
            pltpu.VMEM((2, ring, tok, HEAD_DIM), BF16),
            pltpu.VMEM((ring // stride, 2 * stride, tok, HEAD_DIM), BF16),
            pltpu.VMEM((group, 2, 2 * stride, tok, HEAD_DIM), BF16),
            pltpu.VMEM((2 * stride,) + block, F32),
            pltpu.VMEM((stride - 1,) + block, BF16),
            pltpu.VMEM((stride - 1,) + block, BF16),
            pltpu.VMEM((stride - 1,) + block, BF16),
            pltpu.VMEM((stride - 1,) + block, BF16),
            pltpu.VMEM((batch,) + block, BF16),
            pltpu.VMEM((batch,) + block, BF16),
            pltpu.VMEM((batch,) + block, BF16),
            pltpu.VMEM(block, BF16),
            pltpu.VMEM(block, BF16),
            dma((7,)),
            dma((5,)),
            dma((5,)),
            dma((1,)),
            dma((2, half + 1, 2, RING_PARTS)),
            dma((1,)),
            dma((1,)),
            dma((1,)),
            dma((2,)),
            dma((ring // stride, stride // 2)),
            dma((group, 2, stride // 2)),
            dma((2, stride - 1, SUM_PARTS)),
            dma((2, stride - 1, SUM_PARTS)),
            dma((2, batch, SUM_PARTS)),
            dma((2,)),
            dma((2,)),
            dma((1,)),
            dma((1,)),
            dma((group,)),
            dma((group,)),
            dma((cols,)),
            dma((cols,)),
            dma((2,)),
        ],
        compiler_params=pltpu.CompilerParams(
            collective_id=0, has_side_effects=True, vmem_limit_bytes=VMEM_BYTES
        ),
        cost_estimate=pl.CostEstimate(
            flops=4 * 10**9, bytes_accessed=8 * 10**6, transcendentals=4 * 10**5
        ),
    )(
        slab_queue.reshape(batch, tok, width), levels, jnp.swapaxes(mod_table, 0, 1),
        w_qkv.reshape(width, 3 * HEAD_DIM), q_gain, k_gain, w_out,
    ).reshape(batch, 1, tok, width)


def solution(mesh):
    placed = (
        P(None, "tm", "space", None),
        P(),
        P(),
        P(None, "tm", None),
        P("tm", None),
        P("tm", None),
        P("tm", None),
    )
    return jax.shard_map(
        body, mesh=mesh, in_specs=placed, out_specs=P(None, "tm", "space", None), check_vma=False
    )
```

```python
import functools
import math

import jax
import jax.numpy as jnp
from jax import lax
from jax.experimental import pallas as pl
from jax.experimental.pallas import tpu as pltpu
from jax.sharding import PartitionSpec as P

HEAD_DIM = 128
W_PIECES = 12
RING_PARTS = 2
SUM_PIECES = 4
SUM_PARTS = 2
VMEM_BYTES = 63 * 1024 * 1024
MESH = pl.DeviceIdType.MESH
F32 = jnp.float32
BF16 = jnp.bfloat16


def dot_t(left, right):
    return lax.dot_general(left, right, (((1,), (1,)), ((), ())), preferred_element_type=F32)


def head_norm(values, gain):
    values = values.astype(F32)
    factor = lax.rsqrt(jnp.mean(jnp.square(values), axis=-1, keepdims=True) + 1e-06)
    return (values * factor * gain).astype(BF16)


def kernel(
    ring, cols,
    slab_in, levels_in, mod_in, w_qkv, q_gain, k_gain, w_out,
    out,
    slab, levels, mod, rows_of, mod_send, tokens, w_buf, gq, gk, wo, qkv, sp_in, sp_out, sp_back, tmp_out, comb,
    x_send, x_recv, part, r_send, r_recv, l_send, l_recv, r_last, l_last, prev, fin_send, fin_recv,
    loc_sem, pair_send, pair_recv, ag_send, ag_recv, aa_send, aa_recv, rt_send, rt_recv,
    xs_send, xs_recv, rs_send, rs_recv, last_recv, misc_send, misc_recv, w_send, w_recv,
    wz_send, wz_recv, wp_send, wp_recv, wd_sem,
):
    half = ring // 2
    group = 2 if ring > 4 else 1
    stride = half // group
    peers = ring // stride
    pieces = stride // 2
    slabs = ring
    tok, width = slab.shape[1], slab.shape[2]
    piece = width // W_PIECES
    tm, space = lax.axis_index("tm"), lax.axis_index("space")
    core, z_lo = lax.rem(tm, 2), lax.div(tm, 2)
    me, z_hi = lax.div(space, 2), lax.rem(space, 2)
    z = z_hi * half + z_lo
    other = 1 - core
    inv_root = 1.0 / math.sqrt(HEAD_DIM)

    def mod_ring(value):
        return lax.rem(value + ring, ring)

    def device(plane, of_core, column):
        return (lax.rem(plane, half) * 2 + of_core, column * 2 + lax.div(plane, half))

    def here(column):
        return (tm, column * 2 + z_hi)

    right = device(mod_ring(z + 1), core, me)
    left = device(mod_ring(z - 1), core, me)
    partner = (z_lo * 2 + other, space)
    tm_next = (lax.rem(tm + 1, slabs), space)
    tm_far = (lax.rem(tm + jnp.where(core == 1, 1, slabs - 1), slabs), space)

    def remote(src, dst, send_sem, recv_sem, target):
        return pltpu.make_async_remote_copy(
            src_ref=src, dst_ref=dst, send_sem=send_sem, recv_sem=recv_sem,
            device_id=target, device_id_type=MESH,
        )

    own_head = core == z_hi
    fetch_levels = pltpu.make_async_copy(levels_in, levels, loc_sem.at[2])
    fetch_mod = pltpu.make_async_copy(mod_in, mod, loc_sem.at[3])
    fetch_slab = pltpu.make_async_copy(slab_in, slab, loc_sem.at[4])
    local_w = pltpu.make_async_copy(w_qkv, w_buf, loc_sem.at[0])
    local_wo = pltpu.make_async_copy(w_out, wo.at[0, core], loc_sem.at[1])
    local_gq = pltpu.make_async_copy(q_gain, gq, loc_sem.at[5])
    local_gk = pltpu.make_async_copy(k_gain, gk, loc_sem.at[6])
    fetch_levels.start()
    fetch_mod.start()
    fetch_slab.start()

    barrier = pltpu.get_barrier_semaphore()
    right_of = [device(mod_ring(z + 1), at, me) for at in (0, 1)]
    left_of = [device(mod_ring(z - 1), at, me) for at in (0, 1)]
    for target in (*right_of, *left_of, partner, tm_far):
        pl.semaphore_signal(barrier, inc=1, device_id=target, device_id_type=MESH)

    def greet(step, carry):
        column = lax.rem(me + step, cols)
        pl.semaphore_signal(barrier, inc=1, device_id=here(column), device_id_type=MESH)
        return carry

    lax.fori_loop(1, cols, greet, 0)

    def greet_class(step, carry):
        target = device(mod_ring(z + stride * step), core, me)
        pl.semaphore_signal(barrier, inc=1, device_id=target, device_id_type=MESH)
        return carry

    lax.fori_loop(1, peers, greet_class, 0)

    fetch_levels.wait()
    fetch_mod.wait()

    tm_before = lax.rem(tm + slabs - 1, slabs)
    pick_row = lax.broadcasted_iota(jnp.int32, (16, mod.shape[1]), 0)
    pick_col = lax.broadcasted_iota(jnp.int32, (16, mod.shape[1]), 1)
    hot = jnp.zeros((16, mod.shape[1]), F32)
    for at, (batch, of_slab) in enumerate(((0, tm), (1, tm), (0, tm_before), (1, tm_before))):
        hot = jnp.where((pick_row == at) & (pick_col == levels[batch, of_slab]), 1.0, hot)
    for kind in range(3):
        picked = jnp.dot(hot.astype(BF16), mod[kind], preferred_element_type=F32)
        for at in range(4):
            rows_of[kind, at] = picked[at : at + 1]

    def modulate(batch):
        values = slab[batch].astype(F32)
        centre = jnp.mean(values, axis=-1, keepdims=True)
        moved = values - centre
        spread = jnp.mean(jnp.square(moved), axis=-1, keepdims=True)
        normed = moved * lax.rsqrt(spread + 1e-06)
        return (normed * (1.0 + rows_of[1, batch]) + rows_of[0, batch]).astype(BF16)

    fetch_slab.wait()

    @pl.when(own_head)
    def _():
        local_gq.start()
        local_gk.start()
        local_w.start()

    local_wo.start()

    tokens[z * 2 + core] = modulate(core)
    pl.semaphore_wait(barrier, 6 + cols - 1 + peers - 1)

    span = width // RING_PARTS

    def gather_copy(way, step, t, origin, at):
        block = tokens.at[origin * 2 + t, :, at * span : (at + 1) * span]
        return remote(
            block, block, ag_send.at[0], ag_recv.at[way, step, t, at], (right, left)[way]
        )

    def gather_start(t):
        for at in range(RING_PARTS):
            for way in (0, 1):
                gather_copy(way, 1, t, z, at).start()

    gather_start(core)
    mod_send[...] = modulate(other)
    to_pair = remote(mod_send, tokens.at[z * 2 + core], pair_send.at[0], pair_recv.at[0], partner)
    to_pair.start()
    from_pair = remote(mod_send, tokens.at[z * 2 + other], pair_send.at[0], pair_recv.at[0], partner)
    from_pair.wait_recv()
    gather_start(other)

    def give_w(at):
        rows = pl.ds(at * piece, piece)
        return remote(w_qkv.at[rows], w_buf.at[rows], w_send.at[0], w_recv.at[0], partner)

    whole_w = remote(w_qkv, w_buf, w_send.at[0], w_recv.at[0], partner)
    give_gq = remote(q_gain, gq, pair_send.at[2], pair_recv.at[2], partner)
    give_gk = remote(k_gain, gk, pair_send.at[3], pair_recv.at[3], partner)
    give_wo = remote(w_out, wo.at[0, core], pair_send.at[4], pair_recv.at[4], partner)
    take_wo = remote(w_out, wo.at[0, other], pair_send.at[4], pair_recv.at[4], partner)
    pass_slab = remote(slab, prev, misc_send.at[0], misc_recv.at[0], tm_next)

    @pl.when(own_head)
    def _():
        give_gq.start()
        give_gk.start()

    pairs = group
    rows_w = 2 * HEAD_DIM // cols
    cut_rows = pl.ds(pl.multiple_of(lax.div(me, 2) * rows_w, rows_w), rows_w)
    cut_cols = pl.ds(pl.multiple_of(lax.rem(me, 2) * (width // 2), width // 2), width // 2)

    def plane_piece(at):
        apart = stride * at if 2 * stride * at < half else stride * at - half
        if 2 * stride * at == half:
            apart = jnp.where(core == 0, half // 2, -(half // 2))
        return remote(
            w_out.at[cut_rows, cut_cols], wo.at[at, core, cut_rows, cut_cols],
            wz_send.at[at], wz_recv.at[at], device(mod_ring(z - apart), core, me),
        )

    def spread_piece(column, source):
        rows = pl.ds(pl.multiple_of(lax.div(source, 2) * rows_w, rows_w), rows_w)
        span = pl.ds(pl.multiple_of(lax.rem(source, 2) * (width // 2), width // 2), width // 2)
        piece_of = wo.at[1:pairs, core, rows, span]
        return remote(
            piece_of, piece_of, wp_send.at[column], wp_recv.at[source], here(column)
        )

    def pair_wo(of_core):
        block = wo.at[1:pairs, of_core]
        return remote(block, block, wd_sem.at[0], wd_sem.at[1], partner)

    for at in range(1, pairs):
        plane_piece(at).start()

    def slab_copy(hi, column, source):
        return remote(
            qkv.at[hi, column], sp_in.at[source, hi], aa_send.at[0], aa_recv.at[0],
            here(column),
        )

    first_dot = max(1, 3 * half // 8)
    give_steps = max(first_dot - 1, 1)
    per_step = W_PIECES // give_steps

    def reach(at):
        done = jnp.minimum(2 * (at - first_dot + 1), at + 1)
        return jnp.where(at < first_dot, 0, jnp.where(at == half, half + 1, done))

    def gather_step(step, carry):
        step = jnp.asarray(step, jnp.int32)
        plane_a = mod_ring(z - step)
        plane_b = mod_ring(z + step)
        first, last = reach(step - 1), reach(step)
        middle = jnp.where(last - first == 2, first + 1, first)

        def turn_step(turn, inner):
            t = jnp.where(turn == 0, core, other)
            for at in range(RING_PARTS):
                for way, origin in ((0, plane_a), (1, plane_b)):

                    @pl.when((step < half) | (t == way))
                    def _():
                        gather_copy(way, step, t, origin, at).wait_recv()

                    @pl.when((step < half - 1) | ((step == half - 1) & (t == way)))
                    def _():
                        gather_copy(way, step + 1, t, origin, at).start()

            if pairs > 1:

                @pl.when((step == 2) & (turn == 0))
                def _():
                    for at in range(1, pairs):
                        plane_piece(at).wait_recv()

                    def spread(ahead, most):
                        spread_piece(lax.rem(me + ahead, cols), me).start()
                        return most

                    lax.fori_loop(1, cols, spread, 0)

                @pl.when((step == half - 1) & (turn == 0))
                def _():
                    def await_spread(ahead, most):
                        spread_piece(me, lax.rem(me + ahead, cols)).wait_recv()
                        return most

                    lax.fori_loop(1, cols, await_spread, 0)
                    pair_wo(core).start()

            @pl.when(own_head & (step <= give_steps))
            def _():
                def one(at, most):
                    give_w(at).start()
                    return most

                share = per_step // 2
                begin = (2 * (step - 1) + turn) * share
                lax.fori_loop(begin, begin + share, one, 0)

            @pl.when((step == first_dot) & (turn == 0))
            def _():
                give_wo.start()

                @pl.when(own_head)
                def _():
                    local_w.wait()
                    local_gq.wait()
                    local_gk.wait()

                @pl.when(jnp.logical_not(own_head))
                def _():
                    whole_w.wait_recv()
                    give_gq.wait_recv()
                    give_gk.wait_recv()

            lax.fori_loop(
                jnp.where(turn == 0, first, middle), jnp.where(turn == 0, middle, last),
                project_step, 0,
            )
            return inner

        lax.fori_loop(0, 2, turn_step, 0)
        return carry

    def project_step(step, carry):
        planes = (mod_ring(z - step), mod_ring(z + step))
        rows = jnp.concatenate(
            [tokens[pl.ds(plane * 2, 2)].reshape(2 * tok, width) for plane in planes], axis=0
        )
        projected = jnp.dot(rows, w_buf[...], preferred_element_type=F32).astype(BF16)
        queries = head_norm(projected[:, :HEAD_DIM], gq[...])
        keys = head_norm(projected[:, HEAD_DIM : 2 * HEAD_DIM], gk[...])
        values = projected[:, 2 * HEAD_DIM :]
        def place(at):
            hi, lo = lax.div(planes[at], half), lax.rem(planes[at], half)
            for t in (0, 1):
                cut = slice((at * 2 + t) * tok, (at * 2 + t + 1) * tok)
                column = lo * 2 + t
                qkv[hi, column, :, 0:HEAD_DIM] = queries[cut]
                qkv[hi, column, :, HEAD_DIM : 2 * HEAD_DIM] = keys[cut]
                qkv[hi, column, :, 2 * HEAD_DIM :] = values[cut]

                @pl.when(column != me)
                def _():
                    slab_copy(hi, column, me).start()

        place(0)

        @pl.when(lax.rem(step, half) != 0)
        def _():
            place(1)

        return carry

    rows_t = slabs * tok
    at_row = lax.broadcasted_iota(jnp.int32, (rows_t, rows_t), 0) & (tok - 1)
    at_col = lax.broadcasted_iota(jnp.int32, (rows_t, rows_t), 1) & (tok - 1)
    same = at_row == at_col

    def temporal(hi):
        queries = qkv[hi, :, :, 0:HEAD_DIM].reshape(rows_t, HEAD_DIM)
        keys = qkv[hi, :, :, HEAD_DIM : 2 * HEAD_DIM].reshape(rows_t, HEAD_DIM)
        values = qkv[hi, :, :, 2 * HEAD_DIM :].reshape(rows_t, HEAD_DIM)
        scores = jnp.where(same, dot_t(queries, keys) * inv_root, -jnp.inf)
        weights = jnp.exp(scores - jnp.max(scores, axis=-1, keepdims=True))
        total = jnp.sum(weights, axis=-1, keepdims=True)
        mixed = jnp.dot(weights.astype(BF16), values, preferred_element_type=F32) / total
        tmp_out[hi] = mixed.reshape(slabs, tok, HEAD_DIM)

    lax.fori_loop(1, half, gather_step, 0)
    temporal(z_hi)
    gather_step(half, 0)
    pass_slab.start()
    sp_in[me] = qkv[:, me]

    mine_late = lax.div(me, 2) == z_lo

    @pl.when(mine_late)
    def _():
        temporal(1 - z_hi)

    part_in = sp_in.at[0 : cols - 1]
    remote(part_in, part_in, aa_send.at[0], aa_recv.at[0], partner).wait_recv()

    is_late = jnp.where(mine_late, 1, 0)

    def back_copy(column, of_slab):
        return remote(
            sp_out.at[column], sp_back.at[:, of_slab], rt_send.at[0], rt_recv.at[is_late],
            here(column),
        )

    batch_s = 4
    rows_s = batch_s * 2 * tok

    def spatial_step(step, carry):
        keys = sp_in[:, :, :, HEAD_DIM : 2 * HEAD_DIM].reshape(cols * 2 * tok, HEAD_DIM)
        values = sp_in[:, :, :, 2 * HEAD_DIM :].reshape(cols * 2 * tok, HEAD_DIM)
        queries = sp_in[pl.ds(step * batch_s, batch_s), :, :, 0:HEAD_DIM].reshape(rows_s, HEAD_DIM)
        scores = dot_t(queries, keys) * inv_root
        weights = jnp.exp(scores - jnp.max(scores, axis=-1, keepdims=True))
        total = jnp.sum(weights, axis=-1, keepdims=True)
        mixed = jnp.dot(weights.astype(BF16), values, preferred_element_type=F32) / total
        sp_out[pl.ds(step * batch_s, batch_s)] = mixed.astype(BF16).reshape(batch_s, 2, tok, HEAD_DIM)
        for at in range(batch_s):
            column = step * batch_s + at

            @pl.when(column != me)
            def _():
                back_copy(column, me).start()

        return carry

    lax.fori_loop(0, cols // batch_s, spatial_step, 0)
    sp_back[:, me] = sp_out[me]

    @pl.when(jnp.logical_not(mine_late))
    def _():
        temporal(1 - z_hi)


    def await_back(late, count):
        block = sp_back.at[:, 0:count]
        remote(block, block, rt_send.at[0], rt_recv.at[late], partner).wait_recv()

    def combine(ahead, carry):
        of_slab = lax.rem(2 * z_lo + ahead, slabs)
        both = sp_back[:, of_slab].astype(F32) + tmp_out[:, of_slab]
        comb[:, of_slab] = both.astype(BF16)
        return carry

    @pl.when(mine_late)
    def _():
        await_back(0, slabs - 2)

    @pl.when(jnp.logical_not(mine_late))
    def _():
        await_back(0, slabs - 3)

    lax.fori_loop(2, slabs, combine, 0)

    def fill(dst, plane, piece_at):
        def one(at, carry):
            step = lax.div(at, 2)
            block = jnp.where(lax.rem(at, 2) == 0, 2 * stride - 1 - step, step)
            place = lax.rem(2 * plane + 2 * ring - (stride - 1) + block, 2 * ring)
            from_slab = lax.rem(lax.rem(place, slabs) + slabs - 1, slabs)
            dst[at] = comb[lax.div(place, slabs), from_slab]
            return carry

        lax.fori_loop(4 * piece_at, 4 * piece_at + 4, one, 0)

    def head_copy(step, at):
        plane = mod_ring(z + stride * step)
        slot = lax.div(lax.rem(z_lo - lax.rem(plane, half) + half, half), stride)
        rows = pl.ds(4 * at, 4)
        return remote(
            x_send.at[step, rows], x_recv.at[slot, z_hi, rows],
            xs_send.at[step, at], xs_recv.at[slot, z_hi, at], device(plane, core, me),
        )

    def send_heads(step, at):
        fill(x_send.at[step], mod_ring(z + stride * step), at)
        head_copy(step, at).start()

    far = peers // 2
    for at in range(pieces):
        for step in range(1, peers):
            if step != far or at < pieces - 1:
                send_heads(step, at)
    for at in range(pieces - 1):
        fill(x_recv.at[0, z_hi], z, at)

    @pl.when(mine_late)
    def _():
        await_back(1, 1)

    @pl.when(jnp.logical_not(mine_late))
    def _():
        await_back(1, 2)

    lax.fori_loop(0, 2, combine, 0)
    send_heads(far, pieces - 1)
    fill(x_recv.at[0, z_hi], z, pieces - 1)
    local_wo.wait()
    take_wo.wait_recv()
    if pairs > 1:
        pair_wo(other).wait_recv()

    to_pair.wait_send()

    @pl.when(own_head)
    def _():
        whole_w.wait_send()
        give_gq.wait_send()
        give_gk.wait_send()

    give_wo.wait_send()
    pass_slab.wait_send()
    pass_slab.wait_recv()
    for at in range(1, pairs):
        plane_piece(at).wait_send()
    if pairs > 1:
        pair_wo(core).wait_send()

        def drain_spread(ahead, carry):
            spread_piece(lax.rem(me + ahead, cols), me).wait_send()
            return carry

        lax.fori_loop(1, cols, drain_spread, 0)
    sent = tokens.at[0 : 2 * ring - 2]
    remote(sent, sent, ag_send.at[0], ag_recv.at[0, 0, 0, 0], partner).wait_send()
    sent = qkv.at[:, 0 : cols - 1]
    remote(sent, sent, aa_send.at[0], aa_recv.at[0], partner).wait_send()
    sent = sp_out.at[0 : cols - 1]
    remote(sent, sent, rt_send.at[0], rt_recv.at[0], partner).wait_send()

    def await_heads(at):
        for step in range(1, peers):
            plane = mod_ring(z + stride * step)
            slot = lax.div(lax.rem(lax.rem(plane, half) - z_lo + half, half), stride)
            hi = lax.div(plane, half)
            rows = pl.ds(4 * at, 4)
            remote(
                x_send.at[step, rows], x_recv.at[slot, hi, rows],
                xs_send.at[step, at], xs_recv.at[slot, hi, at], device(plane, core, me),
            ).wait_recv()

    def final_core(way, step):
        if step < stride - 3:
            return None
        return (step == stride - 3) != (way == 1) and 1 or 0

    def sum_copy(way, step, at):
        mine, theirs, ends = ((r_send, r_recv, r_last), (l_send, l_recv, l_last))[way]
        span_s = slice(at * sum_span, (at + 1) * sum_span)
        dst = theirs.at[step, :, span_s]
        sem = rs_recv.at[way, step, at]
        target = (right, left)[way]
        to_core = final_core(way, step)
        if to_core is not None:
            dst = ends.at[core, :, span_s]
            sem = last_recv.at[way, core, at]
            target = (right_of, left_of)[way][to_core]
        return remote(mine.at[step, :, span_s], dst, rs_send.at[way, step, at], sem, target)

    sum_span = width // SUM_PARTS
    chunk = width // SUM_PIECES
    rows_x = 4 * tok
    for step in range(stride - 1):
        if step % 2 == 0:
            await_heads(step // 2)
            rows = slice(2 * step, 2 * step + 4)
            heads = jnp.concatenate(
                [x_recv[at // 2, at % 2, rows].reshape(rows_x, HEAD_DIM) for at in range(2 * pairs)],
                axis=1,
            )
        for part_at in range(SUM_PARTS):
            span_s = slice(part_at * sum_span, (part_at + 1) * sum_span)
            if step % 2 == 0:
                for at in range(part_at * sum_span, (part_at + 1) * sum_span, chunk):
                    weights = wo[:, :, :, at : at + chunk].reshape(2 * pairs * HEAD_DIM, chunk)
                    product = jnp.dot(heads, weights, preferred_element_type=F32)
                    part[rows, :, at : at + chunk] = product.reshape(4, tok, chunk)
            for way, mine, theirs in ((0, r_send, r_recv), (1, l_send, l_recv)):
                share = part[step * 2 + way, :, span_s]
                if step >= 2:
                    sum_copy(way, step - 2, part_at).wait_recv()
                    share = share + theirs[step - 2, :, span_s].astype(F32)
                mine[step, :, span_s] = share.astype(BF16)
                sum_copy(way, step, part_at).start()

    fin_send[...] = part[2 * stride - 1 - other].astype(BF16)
    give_fin = remote(fin_send, fin_recv, misc_send.at[1], misc_recv.at[1], partner)
    give_fin.start()

    def await_last(way, batch):
        ends = (r_last, l_last)[way]
        for at in range(SUM_PARTS):
            dst = ends.at[batch, :, at * sum_span : (at + 1) * sum_span]
            remote(
                dst, dst, rs_send.at[way, 0, at], last_recv.at[way, batch, at], partner
            ).wait_recv()

    def attend(batch, own_share):
        gate = rows_of[2, 2 + batch]
        if stride > 2:
            for way in (0, 1):
                await_last(way, batch)
            sides = r_last[batch].astype(F32) + l_last[batch].astype(F32)
        else:
            for way in (0, 1):

                @pl.when(core == way)
                def _():
                    await_last(way, batch)

            sides = jnp.where(core == 0, r_last[batch].astype(F32), l_last[batch].astype(F32))
        projection = own_share + sides
        out[batch] = (prev[batch].astype(F32) + gate * projection).astype(BF16)

    attend(core, part[2 * stride - 1 - core])
    give_fin.wait_recv()
    attend(other, fin_recv[...].astype(F32))

    give_fin.wait_send()
    for step in range(1, peers):
        for at in range(pieces):
            head_copy(step, at).wait_send()
    for step in range(stride - 1):
        for way in (0, 1):
            for at in range(SUM_PARTS):
                sum_copy(way, step, at).wait_send()


def body(slab_queue, levels, mod_table, w_qkv, q_gain, k_gain, w_out):
    batch, _, tok, width = slab_queue.shape
    ring = lax.axis_size("tm")
    cols = lax.axis_size("space") // 2
    half = ring // 2
    group = 2 if ring > 4 else 1
    stride = half // group
    vmem = pl.BlockSpec(memory_space=pltpu.VMEM)
    hbm = pl.BlockSpec(memory_space=pltpu.HBM)
    dma = pltpu.SemaphoreType.DMA
    block = (tok, width)
    return pl.pallas_call(
        functools.partial(kernel, ring, cols),
        out_shape=pltpu.VMEM((batch, tok, width), BF16),
        in_specs=[hbm] * 7,
        out_specs=vmem,
        scratch_shapes=[
            pltpu.VMEM((batch,) + block, BF16),
            pltpu.SMEM(levels.shape, jnp.int32),
            pltpu.VMEM((3, mod_table.shape[0], width), BF16),
            pltpu.VMEM((3, 4, 1, width), F32),
            pltpu.VMEM(block, BF16),
            pltpu.VMEM((2 * ring,) + block, BF16),
            pltpu.VMEM((width, 3 * HEAD_DIM), BF16),
            pltpu.VMEM((1, HEAD_DIM), F32),
            pltpu.VMEM((1, HEAD_DIM), F32),
            pltpu.VMEM((group, 2, HEAD_DIM, width), BF16),
            pltpu.VMEM((2, ring, tok, 3 * HEAD_DIM), BF16),
            pltpu.VMEM((cols, 2, tok, 3 * HEAD_DIM), BF16),
            pltpu.VMEM((cols, 2, tok, HEAD_DIM), BF16),
            pltpu.VMEM((2, ring, tok, HEAD_DIM), BF16),
            pltpu.VMEM((2, ring, tok, HEAD_DIM), F32),
            pltpu.VMEM((2, ring, tok, HEAD_DIM), BF16),
            pltpu.VMEM((ring // stride, 2 * stride, tok, HEAD_DIM), BF16),
            pltpu.VMEM((group, 2, 2 * stride, tok, HEAD_DIM), BF16),
            pltpu.VMEM((2 * stride,) + block, F32),
            pltpu.VMEM((stride - 1,) + block, BF16),
            pltpu.VMEM((stride - 1,) + block, BF16),
            pltpu.VMEM((stride - 1,) + block, BF16),
            pltpu.VMEM((stride - 1,) + block, BF16),
            pltpu.VMEM((batch,) + block, BF16),
            pltpu.VMEM((batch,) + block, BF16),
            pltpu.VMEM((batch,) + block, BF16),
            pltpu.VMEM(block, BF16),
            pltpu.VMEM(block, BF16),
            dma((7,)),
            dma((5,)),
            dma((5,)),
            dma((1,)),
            dma((2, half + 1, 2, RING_PARTS)),
            dma((1,)),
            dma((1,)),
            dma((1,)),
            dma((2,)),
            dma((ring // stride, stride // 2)),
            dma((group, 2, stride // 2)),
            dma((2, stride - 1, SUM_PARTS)),
            dma((2, stride - 1, SUM_PARTS)),
            dma((2, batch, SUM_PARTS)),
            dma((2,)),
            dma((2,)),
            dma((1,)),
            dma((1,)),
            dma((group,)),
            dma((group,)),
            dma((cols,)),
            dma((cols,)),
            dma((2,)),
        ],
        compiler_params=pltpu.CompilerParams(
            collective_id=0, has_side_effects=True, vmem_limit_bytes=VMEM_BYTES
        ),
        cost_estimate=pl.CostEstimate(
            flops=4 * 10**9, bytes_accessed=8 * 10**6, transcendentals=4 * 10**5
        ),
    )(
        slab_queue.reshape(batch, tok, width), levels, jnp.swapaxes(mod_table, 0, 1),
        w_qkv.reshape(width, 3 * HEAD_DIM), q_gain, k_gain, w_out,
    ).reshape(batch, 1, tok, width)


def solution(mesh):
    placed = (
        P(None, "tm", "space", None),
        P(),
        P(),
        P(None, "tm", None),
        P("tm", None),
        P("tm", None),
        P("tm", None),
    )
    return jax.shard_map(
        body, mesh=mesh, in_specs=placed, out_specs=P(None, "tm", "space", None), check_vma=False
    )
```

```python
import functools
import math

import jax
import jax.numpy as jnp
from jax import lax
from jax.experimental import pallas as pl
from jax.experimental.pallas import tpu as pltpu
from jax.sharding import PartitionSpec as P

HEAD_DIM = 128
W_PIECES = 12
RING_PARTS = 4
SUM_PIECES = 4
SUM_PARTS = 2
VMEM_BYTES = 63 * 1024 * 1024
MESH = pl.DeviceIdType.MESH
F32 = jnp.float32
BF16 = jnp.bfloat16


def dot_t(left, right):
    return lax.dot_general(left, right, (((1,), (1,)), ((), ())), preferred_element_type=F32)


def head_norm(values, gain):
    values = values.astype(F32)
    factor = lax.rsqrt(jnp.mean(jnp.square(values), axis=-1, keepdims=True) + 1e-06)
    return (values * factor * gain).astype(BF16)


def kernel(
    ring, cols,
    slab_in, levels_in, mod_in, w_qkv, q_gain, k_gain, w_out,
    out,
    slab, levels, mod, rows_of, mod_send, tokens, w_buf, gq, gk, wo, qkv, sp_in, sp_out, sp_back, tmp_out, comb,
    x_send, x_recv, part, r_send, r_recv, l_send, l_recv, r_last, l_last, prev, fin_send, fin_recv,
    loc_sem, pair_send, pair_recv, ag_send, ag_recv, aa_send, aa_recv, rt_send, rt_recv,
    xs_send, xs_recv, rs_send, rs_recv, last_recv, misc_send, misc_recv, w_send, w_recv,
    wz_send, wz_recv, wp_send, wp_recv, wd_sem,
):
    half = ring // 2
    group = 2 if ring > 4 else 1
    stride = half // group
    peers = ring // stride
    pieces = stride // 2
    slabs = ring
    tok, width = slab.shape[1], slab.shape[2]
    piece = width // W_PIECES
    tm, space = lax.axis_index("tm"), lax.axis_index("space")
    core, z_lo = lax.rem(tm, 2), lax.div(tm, 2)
    me, z_hi = lax.div(space, 2), lax.rem(space, 2)
    z = z_hi * half + z_lo
    other = 1 - core
    inv_root = 1.0 / math.sqrt(HEAD_DIM)

    def mod_ring(value):
        return lax.rem(value + ring, ring)

    def device(plane, of_core, column):
        return (lax.rem(plane, half) * 2 + of_core, column * 2 + lax.div(plane, half))

    def here(column):
        return (tm, column * 2 + z_hi)

    right = device(mod_ring(z + 1), core, me)
    left = device(mod_ring(z - 1), core, me)
    partner = (z_lo * 2 + other, space)
    tm_next = (lax.rem(tm + 1, slabs), space)
    tm_far = (lax.rem(tm + jnp.where(core == 1, 1, slabs - 1), slabs), space)

    def remote(src, dst, send_sem, recv_sem, target):
        return pltpu.make_async_remote_copy(
            src_ref=src, dst_ref=dst, send_sem=send_sem, recv_sem=recv_sem,
            device_id=target, device_id_type=MESH,
        )

    own_head = core == z_hi
    fetch_levels = pltpu.make_async_copy(levels_in, levels, loc_sem.at[2])
    fetch_mod = pltpu.make_async_copy(mod_in, mod, loc_sem.at[3])
    fetch_slab = pltpu.make_async_copy(slab_in, slab, loc_sem.at[4])
    local_w = pltpu.make_async_copy(w_qkv, w_buf, loc_sem.at[0])
    local_wo = pltpu.make_async_copy(w_out, wo.at[0, core], loc_sem.at[1])
    local_gq = pltpu.make_async_copy(q_gain, gq, loc_sem.at[5])
    local_gk = pltpu.make_async_copy(k_gain, gk, loc_sem.at[6])
    fetch_levels.start()
    fetch_mod.start()
    fetch_slab.start()

    barrier = pltpu.get_barrier_semaphore()
    right_of = [device(mod_ring(z + 1), at, me) for at in (0, 1)]
    left_of = [device(mod_ring(z - 1), at, me) for at in (0, 1)]
    for target in (*right_of, *left_of, partner, tm_far):
        pl.semaphore_signal(barrier, inc=1, device_id=target, device_id_type=MESH)

    def greet(step, carry):
        column = lax.rem(me + step, cols)
        pl.semaphore_signal(barrier, inc=1, device_id=here(column), device_id_type=MESH)
        return carry

    lax.fori_loop(1, cols, greet, 0)

    def greet_class(step, carry):
        target = device(mod_ring(z + stride * step), core, me)
        pl.semaphore_signal(barrier, inc=1, device_id=target, device_id_type=MESH)
        return carry

    lax.fori_loop(1, peers, greet_class, 0)

    fetch_levels.wait()
    fetch_mod.wait()

    tm_before = lax.rem(tm + slabs - 1, slabs)
    pick_row = lax.broadcasted_iota(jnp.int32, (16, mod.shape[1]), 0)
    pick_col = lax.broadcasted_iota(jnp.int32, (16, mod.shape[1]), 1)
    hot = jnp.zeros((16, mod.shape[1]), F32)
    for at, (batch, of_slab) in enumerate(((0, tm), (1, tm), (0, tm_before), (1, tm_before))):
        hot = jnp.where((pick_row == at) & (pick_col == levels[batch, of_slab]), 1.0, hot)
    for kind in range(3):
        picked = jnp.dot(hot.astype(BF16), mod[kind], preferred_element_type=F32)
        for at in range(4):
            rows_of[kind, at] = picked[at : at + 1]

    def modulate(batch):
        values = slab[batch].astype(F32)
        centre = jnp.mean(values, axis=-1, keepdims=True)
        moved = values - centre
        spread = jnp.mean(jnp.square(moved), axis=-1, keepdims=True)
        normed = moved * lax.rsqrt(spread + 1e-06)
        return (normed * (1.0 + rows_of[1, batch]) + rows_of[0, batch]).astype(BF16)

    fetch_slab.wait()

    @pl.when(own_head)
    def _():
        local_gq.start()
        local_gk.start()
        local_w.start()

    local_wo.start()

    tokens[z * 2 + core] = modulate(core)
    pl.semaphore_wait(barrier, 6 + cols - 1 + peers - 1)

    span = width // RING_PARTS

    def gather_copy(way, step, t, origin, at):
        block = tokens.at[origin * 2 + t, :, at * span : (at + 1) * span]
        return remote(
            block, block, ag_send.at[0], ag_recv.at[way, step, t, at], (right, left)[way]
        )

    def gather_start(t):
        for at in range(RING_PARTS):
            for way in (0, 1):
                gather_copy(way, 1, t, z, at).start()

    gather_start(core)
    mod_send[...] = modulate(other)
    to_pair = remote(mod_send, tokens.at[z * 2 + core], pair_send.at[0], pair_recv.at[0], partner)
    to_pair.start()
    from_pair = remote(mod_send, tokens.at[z * 2 + other], pair_send.at[0], pair_recv.at[0], partner)
    from_pair.wait_recv()
    gather_start(other)

    def give_w(at):
        rows = pl.ds(at * piece, piece)
        return remote(w_qkv.at[rows], w_buf.at[rows], w_send.at[0], w_recv.at[0], partner)

    whole_w = remote(w_qkv, w_buf, w_send.at[0], w_recv.at[0], partner)
    give_gq = remote(q_gain, gq, pair_send.at[2], pair_recv.at[2], partner)
    give_gk = remote(k_gain, gk, pair_send.at[3], pair_recv.at[3], partner)
    give_wo = remote(w_out, wo.at[0, core], pair_send.at[4], pair_recv.at[4], partner)
    take_wo = remote(w_out, wo.at[0, other], pair_send.at[4], pair_recv.at[4], partner)
    pass_slab = remote(slab, prev, misc_send.at[0], misc_recv.at[0], tm_next)

    @pl.when(own_head)
    def _():
        give_gq.start()
        give_gk.start()

    pairs = group
    rows_w = 2 * HEAD_DIM // cols
    cut_rows = pl.ds(pl.multiple_of(lax.div(me, 2) * rows_w, rows_w), rows_w)
    cut_cols = pl.ds(pl.multiple_of(lax.rem(me, 2) * (width // 2), width // 2), width // 2)

    def plane_piece(at):
        apart = stride * at if 2 * stride * at < half else stride * at - half
        if 2 * stride * at == half:
            apart = jnp.where(core == 0, half // 2, -(half // 2))
        return remote(
            w_out.at[cut_rows, cut_cols], wo.at[at, core, cut_rows, cut_cols],
            wz_send.at[at], wz_recv.at[at], device(mod_ring(z - apart), core, me),
        )

    def spread_piece(column, source):
        rows = pl.ds(pl.multiple_of(lax.div(source, 2) * rows_w, rows_w), rows_w)
        span = pl.ds(pl.multiple_of(lax.rem(source, 2) * (width // 2), width // 2), width // 2)
        piece_of = wo.at[1:pairs, core, rows, span]
        return remote(
            piece_of, piece_of, wp_send.at[column], wp_recv.at[source], here(column)
        )

    def pair_wo(of_core):
        block = wo.at[1:pairs, of_core]
        return remote(block, block, wd_sem.at[0], wd_sem.at[1], partner)

    for at in range(1, pairs):
        plane_piece(at).start()

    def slab_copy(hi, column, source):
        return remote(
            qkv.at[hi, column], sp_in.at[source, hi], aa_send.at[0], aa_recv.at[0],
            here(column),
        )

    first_dot = max(1, 3 * half // 8)
    give_steps = max(first_dot - 1, 1)
    per_step = W_PIECES // give_steps

    def reach(at):
        done = jnp.minimum(2 * (at - first_dot + 1), at + 1)
        return jnp.where(at < first_dot, 0, jnp.where(at == half, half + 1, done))

    def gather_step(step, carry):
        step = jnp.asarray(step, jnp.int32)
        plane_a = mod_ring(z - step)
        plane_b = mod_ring(z + step)
        first, last = reach(step - 1), reach(step)
        middle = jnp.where(last - first == 2, first + 1, first)

        def turn_step(turn, inner):
            t = jnp.where(turn == 0, core, other)
            for at in range(RING_PARTS):
                for way, origin in ((0, plane_a), (1, plane_b)):

                    @pl.when((step < half) | (t == way))
                    def _():
                        gather_copy(way, step, t, origin, at).wait_recv()

                    @pl.when((step < half - 1) | ((step == half - 1) & (t == way)))
                    def _():
                        gather_copy(way, step + 1, t, origin, at).start()

            if pairs > 1:

                @pl.when((step == 2) & (turn == 0))
                def _():
                    for at in range(1, pairs):
                        plane_piece(at).wait_recv()

                    def spread(ahead, most):
                        spread_piece(lax.rem(me + ahead, cols), me).start()
                        return most

                    lax.fori_loop(1, cols, spread, 0)

                @pl.when((step == half - 1) & (turn == 0))
                def _():
                    def await_spread(ahead, most):
                        spread_piece(me, lax.rem(me + ahead, cols)).wait_recv()
                        return most

                    lax.fori_loop(1, cols, await_spread, 0)
                    pair_wo(core).start()

            @pl.when(own_head & (step <= give_steps))
            def _():
                def one(at, most):
                    give_w(at).start()
                    return most

                share = per_step // 2
                begin = (2 * (step - 1) + turn) * share
                lax.fori_loop(begin, begin + share, one, 0)

            @pl.when((step == first_dot) & (turn == 0))
            def _():
                give_wo.start()

                @pl.when(own_head)
                def _():
                    local_w.wait()
                    local_gq.wait()
                    local_gk.wait()

                @pl.when(jnp.logical_not(own_head))
                def _():
                    whole_w.wait_recv()
                    give_gq.wait_recv()
                    give_gk.wait_recv()

            lax.fori_loop(
                jnp.where(turn == 0, first, middle), jnp.where(turn == 0, middle, last),
                project_step, 0,
            )
            return inner

        lax.fori_loop(0, 2, turn_step, 0)
        return carry

    def project_step(step, carry):
        planes = (mod_ring(z - step), mod_ring(z + step))
        rows = jnp.concatenate(
            [tokens[pl.ds(plane * 2, 2)].reshape(2 * tok, width) for plane in planes], axis=0
        )
        projected = jnp.dot(rows, w_buf[...], preferred_element_type=F32).astype(BF16)
        queries = head_norm(projected[:, :HEAD_DIM], gq[...])
        keys = head_norm(projected[:, HEAD_DIM : 2 * HEAD_DIM], gk[...])
        values = projected[:, 2 * HEAD_DIM :]
        def place(at):
            hi, lo = lax.div(planes[at], half), lax.rem(planes[at], half)
            for t in (0, 1):
                cut = slice((at * 2 + t) * tok, (at * 2 + t + 1) * tok)
                column = lo * 2 + t
                qkv[hi, column, :, 0:HEAD_DIM] = queries[cut]
                qkv[hi, column, :, HEAD_DIM : 2 * HEAD_DIM] = keys[cut]
                qkv[hi, column, :, 2 * HEAD_DIM :] = values[cut]

                @pl.when(column != me)
                def _():
                    slab_copy(hi, column, me).start()

        place(0)

        @pl.when(lax.rem(step, half) != 0)
        def _():
            place(1)

        return carry

    rows_t = slabs * tok
    at_row = lax.broadcasted_iota(jnp.int32, (rows_t, rows_t), 0) & (tok - 1)
    at_col = lax.broadcasted_iota(jnp.int32, (rows_t, rows_t), 1) & (tok - 1)
    same = at_row == at_col

    def temporal(hi):
        queries = qkv[hi, :, :, 0:HEAD_DIM].reshape(rows_t, HEAD_DIM)
        keys = qkv[hi, :, :, HEAD_DIM : 2 * HEAD_DIM].reshape(rows_t, HEAD_DIM)
        values = qkv[hi, :, :, 2 * HEAD_DIM :].reshape(rows_t, HEAD_DIM)
        scores = jnp.where(same, dot_t(queries, keys) * inv_root, -jnp.inf)
        weights = jnp.exp(scores - jnp.max(scores, axis=-1, keepdims=True))
        total = jnp.sum(weights, axis=-1, keepdims=True)
        mixed = jnp.dot(weights.astype(BF16), values, preferred_element_type=F32) / total
        tmp_out[hi] = mixed.reshape(slabs, tok, HEAD_DIM)

    lax.fori_loop(1, half, gather_step, 0)
    temporal(z_hi)
    gather_step(half, 0)
    pass_slab.start()
    sp_in[me] = qkv[:, me]

    mine_late = lax.div(me, 2) == z_lo

    @pl.when(mine_late)
    def _():
        temporal(1 - z_hi)

    part_in = sp_in.at[0 : cols - 1]
    remote(part_in, part_in, aa_send.at[0], aa_recv.at[0], partner).wait_recv()

    is_late = jnp.where(mine_late, 1, 0)

    def back_copy(column, of_slab):
        return remote(
            sp_out.at[column], sp_back.at[:, of_slab], rt_send.at[0], rt_recv.at[is_late],
            here(column),
        )

    batch_s = 4
    rows_s = batch_s * 2 * tok

    def spatial_step(step, carry):
        keys = sp_in[:, :, :, HEAD_DIM : 2 * HEAD_DIM].reshape(cols * 2 * tok, HEAD_DIM)
        values = sp_in[:, :, :, 2 * HEAD_DIM :].reshape(cols * 2 * tok, HEAD_DIM)
        queries = sp_in[pl.ds(step * batch_s, batch_s), :, :, 0:HEAD_DIM].reshape(rows_s, HEAD_DIM)
        scores = dot_t(queries, keys) * inv_root
        weights = jnp.exp(scores - jnp.max(scores, axis=-1, keepdims=True))
        total = jnp.sum(weights, axis=-1, keepdims=True)
        mixed = jnp.dot(weights.astype(BF16), values, preferred_element_type=F32) / total
        sp_out[pl.ds(step * batch_s, batch_s)] = mixed.astype(BF16).reshape(batch_s, 2, tok, HEAD_DIM)
        for at in range(batch_s):
            column = step * batch_s + at

            @pl.when(column != me)
            def _():
                back_copy(column, me).start()

        return carry

    lax.fori_loop(0, cols // batch_s, spatial_step, 0)
    sp_back[:, me] = sp_out[me]

    @pl.when(jnp.logical_not(mine_late))
    def _():
        temporal(1 - z_hi)


    def await_back(late, count):
        block = sp_back.at[:, 0:count]
        remote(block, block, rt_send.at[0], rt_recv.at[late], partner).wait_recv()

    def combine(ahead, carry):
        of_slab = lax.rem(2 * z_lo + ahead, slabs)
        both = sp_back[:, of_slab].astype(F32) + tmp_out[:, of_slab]
        comb[:, of_slab] = both.astype(BF16)
        return carry

    @pl.when(mine_late)
    def _():
        await_back(0, slabs - 2)

    @pl.when(jnp.logical_not(mine_late))
    def _():
        await_back(0, slabs - 3)

    lax.fori_loop(2, slabs, combine, 0)

    def fill(dst, plane, piece_at):
        def one(at, carry):
            step = lax.div(at, 2)
            block = jnp.where(lax.rem(at, 2) == 0, 2 * stride - 1 - step, step)
            place = lax.rem(2 * plane + 2 * ring - (stride - 1) + block, 2 * ring)
            from_slab = lax.rem(lax.rem(place, slabs) + slabs - 1, slabs)
            dst[at] = comb[lax.div(place, slabs), from_slab]
            return carry

        lax.fori_loop(4 * piece_at, 4 * piece_at + 4, one, 0)

    def head_copy(step, at):
        plane = mod_ring(z + stride * step)
        slot = lax.div(lax.rem(z_lo - lax.rem(plane, half) + half, half), stride)
        rows = pl.ds(4 * at, 4)
        return remote(
            x_send.at[step, rows], x_recv.at[slot, z_hi, rows],
            xs_send.at[step, at], xs_recv.at[slot, z_hi, at], device(plane, core, me),
        )

    def send_heads(step, at):
        fill(x_send.at[step], mod_ring(z + stride * step), at)
        head_copy(step, at).start()

    far = peers // 2
    for at in range(pieces):
        for step in range(1, peers):
            if step != far or at < pieces - 1:
                send_heads(step, at)
    for at in range(pieces - 1):
        fill(x_recv.at[0, z_hi], z, at)

    @pl.when(mine_late)
    def _():
        await_back(1, 1)

    @pl.when(jnp.logical_not(mine_late))
    def _():
        await_back(1, 2)

    lax.fori_loop(0, 2, combine, 0)
    send_heads(far, pieces - 1)
    fill(x_recv.at[0, z_hi], z, pieces - 1)
    local_wo.wait()
    take_wo.wait_recv()
    if pairs > 1:
        pair_wo(other).wait_recv()

    to_pair.wait_send()

    @pl.when(own_head)
    def _():
        whole_w.wait_send()
        give_gq.wait_send()
        give_gk.wait_send()

    give_wo.wait_send()
    pass_slab.wait_send()
    pass_slab.wait_recv()
    for at in range(1, pairs):
        plane_piece(at).wait_send()
    if pairs > 1:
        pair_wo(core).wait_send()

        def drain_spread(ahead, carry):
            spread_piece(lax.rem(me + ahead, cols), me).wait_send()
            return carry

        lax.fori_loop(1, cols, drain_spread, 0)
    sent = tokens.at[0 : 2 * ring - 2]
    remote(sent, sent, ag_send.at[0], ag_recv.at[0, 0, 0, 0], partner).wait_send()
    sent = qkv.at[:, 0 : cols - 1]
    remote(sent, sent, aa_send.at[0], aa_recv.at[0], partner).wait_send()
    sent = sp_out.at[0 : cols - 1]
    remote(sent, sent, rt_send.at[0], rt_recv.at[0], partner).wait_send()

    def await_heads(at):
        for step in range(1, peers):
            plane = mod_ring(z + stride * step)
            slot = lax.div(lax.rem(lax.rem(plane, half) - z_lo + half, half), stride)
            hi = lax.div(plane, half)
            rows = pl.ds(4 * at, 4)
            remote(
                x_send.at[step, rows], x_recv.at[slot, hi, rows],
                xs_send.at[step, at], xs_recv.at[slot, hi, at], device(plane, core, me),
            ).wait_recv()

    def final_core(way, step):
        if step < stride - 3:
            return None
        return (step == stride - 3) != (way == 1) and 1 or 0

    def sum_copy(way, step, at):
        mine, theirs, ends = ((r_send, r_recv, r_last), (l_send, l_recv, l_last))[way]
        span_s = slice(at * sum_span, (at + 1) * sum_span)
        dst = theirs.at[step, :, span_s]
        sem = rs_recv.at[way, step, at]
        target = (right, left)[way]
        to_core = final_core(way, step)
        if to_core is not None:
            dst = ends.at[core, :, span_s]
            sem = last_recv.at[way, core, at]
            target = (right_of, left_of)[way][to_core]
        return remote(mine.at[step, :, span_s], dst, rs_send.at[way, step, at], sem, target)

    sum_span = width // SUM_PARTS
    chunk = width // SUM_PIECES
    rows_x = 4 * tok
    for step in range(stride - 1):
        if step % 2 == 0:
            await_heads(step // 2)
            rows = slice(2 * step, 2 * step + 4)
            heads = jnp.concatenate(
                [x_recv[at // 2, at % 2, rows].reshape(rows_x, HEAD_DIM) for at in range(2 * pairs)],
                axis=1,
            )
        for part_at in range(SUM_PARTS):
            span_s = slice(part_at * sum_span, (part_at + 1) * sum_span)
            if step % 2 == 0:
                for at in range(part_at * sum_span, (part_at + 1) * sum_span, chunk):
                    weights = wo[:, :, :, at : at + chunk].reshape(2 * pairs * HEAD_DIM, chunk)
                    product = jnp.dot(heads, weights, preferred_element_type=F32)
                    part[rows, :, at : at + chunk] = product.reshape(4, tok, chunk)
            for way, mine, theirs in ((0, r_send, r_recv), (1, l_send, l_recv)):
                share = part[step * 2 + way, :, span_s]
                if step >= 2:
                    sum_copy(way, step - 2, part_at).wait_recv()
                    share = share + theirs[step - 2, :, span_s].astype(F32)
                mine[step, :, span_s] = share.astype(BF16)
                sum_copy(way, step, part_at).start()

    fin_send[...] = part[2 * stride - 1 - other].astype(BF16)
    give_fin = remote(fin_send, fin_recv, misc_send.at[1], misc_recv.at[1], partner)
    give_fin.start()

    def await_last(way, batch):
        ends = (r_last, l_last)[way]
        for at in range(SUM_PARTS):
            dst = ends.at[batch, :, at * sum_span : (at + 1) * sum_span]
            remote(
                dst, dst, rs_send.at[way, 0, at], last_recv.at[way, batch, at], partner
            ).wait_recv()

    def attend(batch, own_share):
        gate = rows_of[2, 2 + batch]
        if stride > 2:
            for way in (0, 1):
                await_last(way, batch)
            sides = r_last[batch].astype(F32) + l_last[batch].astype(F32)
        else:
            for way in (0, 1):

                @pl.when(core == way)
                def _():
                    await_last(way, batch)

            sides = jnp.where(core == 0, r_last[batch].astype(F32), l_last[batch].astype(F32))
        projection = own_share + sides
        out[batch] = (prev[batch].astype(F32) + gate * projection).astype(BF16)

    attend(core, part[2 * stride - 1 - core])
    give_fin.wait_recv()
    attend(other, fin_recv[...].astype(F32))

    give_fin.wait_send()
    for step in range(1, peers):
        for at in range(pieces):
            head_copy(step, at).wait_send()
    for step in range(stride - 1):
        for way in (0, 1):
            for at in range(SUM_PARTS):
                sum_copy(way, step, at).wait_send()


def body(slab_queue, levels, mod_table, w_qkv, q_gain, k_gain, w_out):
    batch, _, tok, width = slab_queue.shape
    ring = lax.axis_size("tm")
    cols = lax.axis_size("space") // 2
    half = ring // 2
    group = 2 if ring > 4 else 1
    stride = half // group
    vmem = pl.BlockSpec(memory_space=pltpu.VMEM)
    hbm = pl.BlockSpec(memory_space=pltpu.HBM)
    dma = pltpu.SemaphoreType.DMA
    block = (tok, width)
    return pl.pallas_call(
        functools.partial(kernel, ring, cols),
        out_shape=pltpu.VMEM((batch, tok, width), BF16),
        in_specs=[hbm] * 7,
        out_specs=vmem,
        scratch_shapes=[
            pltpu.VMEM((batch,) + block, BF16),
            pltpu.SMEM(levels.shape, jnp.int32),
            pltpu.VMEM((3, mod_table.shape[0], width), BF16),
            pltpu.VMEM((3, 4, 1, width), F32),
            pltpu.VMEM(block, BF16),
            pltpu.VMEM((2 * ring,) + block, BF16),
            pltpu.VMEM((width, 3 * HEAD_DIM), BF16),
            pltpu.VMEM((1, HEAD_DIM), F32),
            pltpu.VMEM((1, HEAD_DIM), F32),
            pltpu.VMEM((group, 2, HEAD_DIM, width), BF16),
            pltpu.VMEM((2, ring, tok, 3 * HEAD_DIM), BF16),
            pltpu.VMEM((cols, 2, tok, 3 * HEAD_DIM), BF16),
            pltpu.VMEM((cols, 2, tok, HEAD_DIM), BF16),
            pltpu.VMEM((2, ring, tok, HEAD_DIM), BF16),
            pltpu.VMEM((2, ring, tok, HEAD_DIM), F32),
            pltpu.VMEM((2, ring, tok, HEAD_DIM), BF16),
            pltpu.VMEM((ring // stride, 2 * stride, tok, HEAD_DIM), BF16),
            pltpu.VMEM((group, 2, 2 * stride, tok, HEAD_DIM), BF16),
            pltpu.VMEM((2 * stride,) + block, F32),
            pltpu.VMEM((stride - 1,) + block, BF16),
            pltpu.VMEM((stride - 1,) + block, BF16),
            pltpu.VMEM((stride - 1,) + block, BF16),
            pltpu.VMEM((stride - 1,) + block, BF16),
            pltpu.VMEM((batch,) + block, BF16),
            pltpu.VMEM((batch,) + block, BF16),
            pltpu.VMEM((batch,) + block, BF16),
            pltpu.VMEM(block, BF16),
            pltpu.VMEM(block, BF16),
            dma((7,)),
            dma((5,)),
            dma((5,)),
            dma((1,)),
            dma((2, half + 1, 2, RING_PARTS)),
            dma((1,)),
            dma((1,)),
            dma((1,)),
            dma((2,)),
            dma((ring // stride, stride // 2)),
            dma((group, 2, stride // 2)),
            dma((2, stride - 1, SUM_PARTS)),
            dma((2, stride - 1, SUM_PARTS)),
            dma((2, batch, SUM_PARTS)),
            dma((2,)),
            dma((2,)),
            dma((1,)),
            dma((1,)),
            dma((group,)),
            dma((group,)),
            dma((cols,)),
            dma((cols,)),
            dma((2,)),
        ],
        compiler_params=pltpu.CompilerParams(
            collective_id=0, has_side_effects=True, vmem_limit_bytes=VMEM_BYTES
        ),
        cost_estimate=pl.CostEstimate(
            flops=4 * 10**9, bytes_accessed=8 * 10**6, transcendentals=4 * 10**5
        ),
    )(
        slab_queue.reshape(batch, tok, width), levels, jnp.swapaxes(mod_table, 0, 1),
        w_qkv.reshape(width, 3 * HEAD_DIM), q_gain, k_gain, w_out,
    ).reshape(batch, 1, tok, width)


def solution(mesh):
    placed = (
        P(None, "tm", "space", None),
        P(),
        P(),
        P(None, "tm", None),
        P("tm", None),
        P("tm", None),
        P("tm", None),
    )
    return jax.shard_map(
        body, mesh=mesh, in_specs=placed, out_specs=P(None, "tm", "space", None), check_vma=False
    )
```

```python
import functools
import math

import jax
import jax.numpy as jnp
from jax import lax
from jax.experimental import pallas as pl
from jax.experimental.pallas import tpu as pltpu
from jax.sharding import PartitionSpec as P

HEAD_DIM = 128
W_PIECES = 12
RING_PARTS = 2
SUM_PIECES = 4
SUM_PARTS = 2
VMEM_BYTES = 63 * 1024 * 1024
MESH = pl.DeviceIdType.MESH
F32 = jnp.float32
BF16 = jnp.bfloat16


def dot_t(left, right):
    return lax.dot_general(left, right, (((1,), (1,)), ((), ())), preferred_element_type=F32)


def head_norm(values, gain):
    values = values.astype(F32)
    factor = lax.rsqrt(jnp.mean(jnp.square(values), axis=-1, keepdims=True) + 1e-06)
    return (values * factor * gain).astype(BF16)


def kernel(
    ring, cols,
    slab_in, levels_in, mod_in, w_qkv, q_gain, k_gain, w_out,
    out,
    slab, levels, mod, rows_of, mod_send, tokens, w_buf, gq, gk, wo, qkv, sp_in, sp_out, sp_back, tmp_out, comb,
    x_send, x_recv, part, r_send, r_recv, l_send, l_recv, r_last, l_last, prev, fin_send, fin_recv,
    loc_sem, pair_send, pair_recv, ag_send, ag_recv, aa_send, aa_recv, rt_send, rt_recv,
    xs_send, xs_recv, rs_send, rs_recv, last_recv, misc_send, misc_recv, w_send, w_recv,
    wz_send, wz_recv, wp_send, wp_recv, wd_sem,
):
    half = ring // 2
    group = 2 if ring > 4 else 1
    stride = half // group
    peers = ring // stride
    pieces = stride // 2
    slabs = ring
    tok, width = slab.shape[1], slab.shape[2]
    piece = width // W_PIECES
    tm, space = lax.axis_index("tm"), lax.axis_index("space")
    core, z_lo = lax.rem(tm, 2), lax.div(tm, 2)
    me, z_hi = lax.div(space, 2), lax.rem(space, 2)
    z = z_hi * half + z_lo
    other = 1 - core
    inv_root = 1.0 / math.sqrt(HEAD_DIM)

    def mod_ring(value):
        return lax.rem(value + ring, ring)

    def device(plane, of_core, column):
        return (lax.rem(plane, half) * 2 + of_core, column * 2 + lax.div(plane, half))

    def here(column):
        return (tm, column * 2 + z_hi)

    right = device(mod_ring(z + 1), core, me)
    left = device(mod_ring(z - 1), core, me)
    partner = (z_lo * 2 + other, space)
    tm_next = (lax.rem(tm + 1, slabs), space)
    tm_far = (lax.rem(tm + jnp.where(core == 1, 1, slabs - 1), slabs), space)

    def remote(src, dst, send_sem, recv_sem, target):
        return pltpu.make_async_remote_copy(
            src_ref=src, dst_ref=dst, send_sem=send_sem, recv_sem=recv_sem,
            device_id=target, device_id_type=MESH,
        )

    own_head = core == z_hi
    fetch_levels = pltpu.make_async_copy(levels_in, levels, loc_sem.at[2])
    fetch_mod = pltpu.make_async_copy(mod_in, mod, loc_sem.at[3])
    fetch_slab = pltpu.make_async_copy(slab_in, slab, loc_sem.at[4])
    local_w = pltpu.make_async_copy(w_qkv, w_buf, loc_sem.at[0])
    local_wo = pltpu.make_async_copy(w_out, wo.at[0, core], loc_sem.at[1])
    local_gq = pltpu.make_async_copy(q_gain, gq, loc_sem.at[5])
    local_gk = pltpu.make_async_copy(k_gain, gk, loc_sem.at[6])
    fetch_levels.start()
    fetch_mod.start()
    fetch_slab.start()

    barrier = pltpu.get_barrier_semaphore()
    right_of = [device(mod_ring(z + 1), at, me) for at in (0, 1)]
    left_of = [device(mod_ring(z - 1), at, me) for at in (0, 1)]
    for target in (*right_of, *left_of, partner, tm_far):
        pl.semaphore_signal(barrier, inc=1, device_id=target, device_id_type=MESH)

    def greet(step, carry):
        column = lax.rem(me + step, cols)
        pl.semaphore_signal(barrier, inc=1, device_id=here(column), device_id_type=MESH)
        return carry

    lax.fori_loop(1, cols, greet, 0)

    def greet_class(step, carry):
        target = device(mod_ring(z + stride * step), core, me)
        pl.semaphore_signal(barrier, inc=1, device_id=target, device_id_type=MESH)
        return carry

    lax.fori_loop(1, peers, greet_class, 0)

    fetch_levels.wait()
    fetch_mod.wait()

    tm_before = lax.rem(tm + slabs - 1, slabs)
    pick_row = lax.broadcasted_iota(jnp.int32, (16, mod.shape[1]), 0)
    pick_col = lax.broadcasted_iota(jnp.int32, (16, mod.shape[1]), 1)
    hot = jnp.zeros((16, mod.shape[1]), F32)
    for at, (batch, of_slab) in enumerate(((0, tm), (1, tm), (0, tm_before), (1, tm_before))):
        hot = jnp.where((pick_row == at) & (pick_col == levels[batch, of_slab]), 1.0, hot)
    for kind in range(3):
        picked = jnp.dot(hot.astype(BF16), mod[kind], preferred_element_type=F32)
        for at in range(4):
            rows_of[kind, at] = picked[at : at + 1]

    def modulate(batch):
        values = slab[batch].astype(F32)
        centre = jnp.mean(values, axis=-1, keepdims=True)
        moved = values - centre
        spread = jnp.mean(jnp.square(moved), axis=-1, keepdims=True)
        normed = moved * lax.rsqrt(spread + 1e-06)
        return (normed * (1.0 + rows_of[1, batch]) + rows_of[0, batch]).astype(BF16)

    fetch_slab.wait()

    @pl.when(own_head)
    def _():
        local_gq.start()
        local_gk.start()
        local_w.start()

    local_wo.start()

    tokens[z * 2 + core] = modulate(core)
    pl.semaphore_wait(barrier, 6 + cols - 1 + peers - 1)

    span = width // RING_PARTS

    def gather_copy(way, step, t, origin, at):
        block = tokens.at[origin * 2 + t, :, at * span : (at + 1) * span]
        return remote(
            block, block, ag_send.at[0], ag_recv.at[way, step, t, at], (right, left)[way]
        )

    def gather_start(t):
        for at in range(RING_PARTS):
            for way in (0, 1):
                gather_copy(way, 1, t, z, at).start()

    gather_start(core)
    mod_send[...] = modulate(other)
    to_pair = remote(mod_send, tokens.at[z * 2 + core], pair_send.at[0], pair_recv.at[0], partner)
    to_pair.start()
    from_pair = remote(mod_send, tokens.at[z * 2 + other], pair_send.at[0], pair_recv.at[0], partner)
    from_pair.wait_recv()
    gather_start(other)

    def give_w(at):
        rows = pl.ds(at * piece, piece)
        return remote(w_qkv.at[rows], w_buf.at[rows], w_send.at[0], w_recv.at[0], partner)

    whole_w = remote(w_qkv, w_buf, w_send.at[0], w_recv.at[0], partner)
    give_gq = remote(q_gain, gq, pair_send.at[2], pair_recv.at[2], partner)
    give_gk = remote(k_gain, gk, pair_send.at[3], pair_recv.at[3], partner)
    give_wo = remote(w_out, wo.at[0, core], pair_send.at[4], pair_recv.at[4], partner)
    take_wo = remote(w_out, wo.at[0, other], pair_send.at[4], pair_recv.at[4], partner)
    pass_slab = remote(slab, prev, misc_send.at[0], misc_recv.at[0], tm_next)

    @pl.when(own_head)
    def _():
        give_gq.start()
        give_gk.start()

    pairs = group
    rows_w = 2 * HEAD_DIM // cols
    cut_rows = pl.ds(pl.multiple_of(lax.div(me, 2) * rows_w, rows_w), rows_w)
    cut_cols = pl.ds(pl.multiple_of(lax.rem(me, 2) * (width // 2), width // 2), width // 2)

    def plane_piece(at):
        apart = stride * at if 2 * stride * at < half else stride * at - half
        if 2 * stride * at == half:
            apart = jnp.where(core == 0, half // 2, -(half // 2))
        return remote(
            w_out.at[cut_rows, cut_cols], wo.at[at, core, cut_rows, cut_cols],
            wz_send.at[at], wz_recv.at[at], device(mod_ring(z - apart), core, me),
        )

    def spread_piece(column, source):
        rows = pl.ds(pl.multiple_of(lax.div(source, 2) * rows_w, rows_w), rows_w)
        span = pl.ds(pl.multiple_of(lax.rem(source, 2) * (width // 2), width // 2), width // 2)
        piece_of = wo.at[1:pairs, core, rows, span]
        return remote(
            piece_of, piece_of, wp_send.at[column], wp_recv.at[source], here(column)
        )

    def pair_wo(of_core):
        block = wo.at[1:pairs, of_core]
        return remote(block, block, wd_sem.at[0], wd_sem.at[1], partner)

    for at in range(1, pairs):
        plane_piece(at).start()

    def slab_copy(hi, column, source):
        return remote(
            qkv.at[hi, column], sp_in.at[source, hi], aa_send.at[0], aa_recv.at[0],
            here(column),
        )

    first_dot = max(1, 3 * half // 8)
    give_steps = max(first_dot - 1, 1)
    per_step = W_PIECES // give_steps

    def reach(at):
        done = jnp.minimum(2 * (at - first_dot + 1), at + 1)
        return jnp.where(at < first_dot, 0, jnp.where(at == half, half + 1, done))

    def gather_step(step, carry):
        step = jnp.asarray(step, jnp.int32)
        plane_a = mod_ring(z - step)
        plane_b = mod_ring(z + step)
        first, last = reach(step - 1), reach(step)
        middle = jnp.where(last - first == 2, first + 1, first)

        def turn_step(turn, inner):
            t = jnp.where(turn == 0, core, other)
            for at in range(RING_PARTS):
                for way, origin in ((0, plane_a), (1, plane_b)):

                    @pl.when((step < half) | (t == way))
                    def _():
                        gather_copy(way, step, t, origin, at).wait_recv()

                    @pl.when((step < half - 1) | ((step == half - 1) & (t == way)))
                    def _():
                        gather_copy(way, step + 1, t, origin, at).start()

            if pairs > 1:

                @pl.when((step == 2) & (turn == 0))
                def _():
                    for at in range(1, pairs):
                        plane_piece(at).wait_recv()

                    def spread(ahead, most):
                        spread_piece(lax.rem(me + ahead, cols), me).start()
                        return most

                    lax.fori_loop(1, cols, spread, 0)

                @pl.when((step == half - 1) & (turn == 0))
                def _():
                    def await_spread(ahead, most):
                        spread_piece(me, lax.rem(me + ahead, cols)).wait_recv()
                        return most

                    lax.fori_loop(1, cols, await_spread, 0)
                    pair_wo(core).start()

            @pl.when(own_head & (step <= give_steps))
            def _():
                def one(at, most):
                    give_w(at).start()
                    return most

                share = per_step // 2
                begin = (2 * (step - 1) + turn) * share
                lax.fori_loop(begin, begin + share, one, 0)

            @pl.when((step == first_dot) & (turn == 0))
            def _():
                give_wo.start()

                @pl.when(own_head)
                def _():
                    local_w.wait()
                    local_gq.wait()
                    local_gk.wait()

                @pl.when(jnp.logical_not(own_head))
                def _():
                    whole_w.wait_recv()
                    give_gq.wait_recv()
                    give_gk.wait_recv()

            lax.fori_loop(
                jnp.where(turn == 0, first, middle), jnp.where(turn == 0, middle, last),
                project_step, 0,
            )
            return inner

        lax.fori_loop(0, 2, turn_step, 0)
        return carry

    def project_step(step, carry):
        planes = (mod_ring(z - step), mod_ring(z + step))
        rows = jnp.concatenate(
            [tokens[pl.ds(plane * 2, 2)].reshape(2 * tok, width) for plane in planes], axis=0
        )
        projected = jnp.dot(rows, w_buf[...], preferred_element_type=F32).astype(BF16)
        queries = head_norm(projected[:, :HEAD_DIM], gq[...])
        keys = head_norm(projected[:, HEAD_DIM : 2 * HEAD_DIM], gk[...])
        values = projected[:, 2 * HEAD_DIM :]
        def place(at):
            hi, lo = lax.div(planes[at], half), lax.rem(planes[at], half)
            for t in (0, 1):
                cut = slice((at * 2 + t) * tok, (at * 2 + t + 1) * tok)
                column = lo * 2 + t
                qkv[hi, column, :, 0:HEAD_DIM] = queries[cut]
                qkv[hi, column, :, HEAD_DIM : 2 * HEAD_DIM] = keys[cut]
                qkv[hi, column, :, 2 * HEAD_DIM :] = values[cut]

                @pl.when(column != me)
                def _():
                    slab_copy(hi, column, me).start()

        place(0)

        @pl.when(lax.rem(step, half) != 0)
        def _():
            place(1)

        return carry

    rows_t = slabs * tok
    at_row = lax.broadcasted_iota(jnp.int32, (rows_t, rows_t), 0) & (tok - 1)
    at_col = lax.broadcasted_iota(jnp.int32, (rows_t, rows_t), 1) & (tok - 1)
    same = at_row == at_col

    def temporal(hi):
        queries = qkv[hi, :, :, 0:HEAD_DIM].reshape(rows_t, HEAD_DIM)
        keys = qkv[hi, :, :, HEAD_DIM : 2 * HEAD_DIM].reshape(rows_t, HEAD_DIM)
        values = qkv[hi, :, :, 2 * HEAD_DIM :].reshape(rows_t, HEAD_DIM)
        scores = jnp.where(same, dot_t(queries, keys) * inv_root, -jnp.inf)
        weights = jnp.exp(scores - jnp.max(scores, axis=-1, keepdims=True))
        total = jnp.sum(weights, axis=-1, keepdims=True)
        mixed = jnp.dot(weights.astype(BF16), values, preferred_element_type=F32) / total
        tmp_out[hi] = mixed.reshape(slabs, tok, HEAD_DIM)

    lax.fori_loop(1, half, gather_step, 0)
    temporal(z_hi)
    gather_step(half, 0)
    pass_slab.start()
    sp_in[me] = qkv[:, me]

    mine_late = lax.div(me, 2) == z_lo

    @pl.when(mine_late)
    def _():
        temporal(1 - z_hi)

    part_in = sp_in.at[0 : cols - 1]
    remote(part_in, part_in, aa_send.at[0], aa_recv.at[0], partner).wait_recv()

    is_late = jnp.where(mine_late, 1, 0)

    def back_copy(column, of_slab):
        return remote(
            sp_out.at[column], sp_back.at[:, of_slab], rt_send.at[0], rt_recv.at[is_late],
            here(column),
        )

    batch_s = min(8, cols)
    rows_s = batch_s * 2 * tok

    def spatial_step(step, carry):
        keys = sp_in[:, :, :, HEAD_DIM : 2 * HEAD_DIM].reshape(cols * 2 * tok, HEAD_DIM)
        values = sp_in[:, :, :, 2 * HEAD_DIM :].reshape(cols * 2 * tok, HEAD_DIM)
        queries = sp_in[pl.ds(step * batch_s, batch_s), :, :, 0:HEAD_DIM].reshape(rows_s, HEAD_DIM)
        scores = dot_t(queries, keys) * inv_root
        weights = jnp.exp(scores - jnp.max(scores, axis=-1, keepdims=True))
        total = jnp.sum(weights, axis=-1, keepdims=True)
        mixed = jnp.dot(weights.astype(BF16), values, preferred_element_type=F32) / total
        sp_out[pl.ds(step * batch_s, batch_s)] = mixed.astype(BF16).reshape(batch_s, 2, tok, HEAD_DIM)
        for at in range(batch_s):
            column = step * batch_s + at

            @pl.when(column != me)
            def _():
                back_copy(column, me).start()

        return carry

    lax.fori_loop(0, cols // batch_s, spatial_step, 0)
    sp_back[:, me] = sp_out[me]

    @pl.when(jnp.logical_not(mine_late))
    def _():
        temporal(1 - z_hi)


    def await_back(late, count):
        block = sp_back.at[:, 0:count]
        remote(block, block, rt_send.at[0], rt_recv.at[late], partner).wait_recv()

    def combine(ahead, carry):
        of_slab = lax.rem(2 * z_lo + ahead, slabs)
        both = sp_back[:, of_slab].astype(F32) + tmp_out[:, of_slab]
        comb[:, of_slab] = both.astype(BF16)
        return carry

    @pl.when(mine_late)
    def _():
        await_back(0, slabs - 2)

    @pl.when(jnp.logical_not(mine_late))
    def _():
        await_back(0, slabs - 3)

    lax.fori_loop(2, slabs, combine, 0)

    def fill(dst, plane, piece_at):
        def one(at, carry):
            step = lax.div(at, 2)
            block = jnp.where(lax.rem(at, 2) == 0, 2 * stride - 1 - step, step)
            place = lax.rem(2 * plane + 2 * ring - (stride - 1) + block, 2 * ring)
            from_slab = lax.rem(lax.rem(place, slabs) + slabs - 1, slabs)
            dst[at] = comb[lax.div(place, slabs), from_slab]
            return carry

        lax.fori_loop(4 * piece_at, 4 * piece_at + 4, one, 0)

    def head_copy(step, at):
        plane = mod_ring(z + stride * step)
        slot = lax.div(lax.rem(z_lo - lax.rem(plane, half) + half, half), stride)
        rows = pl.ds(4 * at, 4)
        return remote(
            x_send.at[step, rows], x_recv.at[slot, z_hi, rows],
            xs_send.at[step, at], xs_recv.at[slot, z_hi, at], device(plane, core, me),
        )

    def send_heads(step, at):
        fill(x_send.at[step], mod_ring(z + stride * step), at)
        head_copy(step, at).start()

    far = peers // 2
    for at in range(pieces):
        if at < pieces - 1:
            send_heads(far, at)
        for step in range(1, peers):
            if step != far:
                send_heads(step, at)
    for at in range(pieces - 1):
        fill(x_recv.at[0, z_hi], z, at)

    @pl.when(mine_late)
    def _():
        await_back(1, 1)

    @pl.when(jnp.logical_not(mine_late))
    def _():
        await_back(1, 2)

    lax.fori_loop(0, 2, combine, 0)
    send_heads(far, pieces - 1)
    fill(x_recv.at[0, z_hi], z, pieces - 1)
    local_wo.wait()
    take_wo.wait_recv()
    if pairs > 1:
        pair_wo(other).wait_recv()

    to_pair.wait_send()

    @pl.when(own_head)
    def _():
        whole_w.wait_send()
        give_gq.wait_send()
        give_gk.wait_send()

    give_wo.wait_send()
    pass_slab.wait_send()
    pass_slab.wait_recv()
    for at in range(1, pairs):
        plane_piece(at).wait_send()
    if pairs > 1:
        pair_wo(core).wait_send()

        def drain_spread(ahead, carry):
            spread_piece(lax.rem(me + ahead, cols), me).wait_send()
            return carry

        lax.fori_loop(1, cols, drain_spread, 0)
    sent = tokens.at[0 : 2 * ring - 2]
    remote(sent, sent, ag_send.at[0], ag_recv.at[0, 0, 0, 0], partner).wait_send()
    sent = qkv.at[:, 0 : cols - 1]
    remote(sent, sent, aa_send.at[0], aa_recv.at[0], partner).wait_send()
    sent = sp_out.at[0 : cols - 1]
    remote(sent, sent, rt_send.at[0], rt_recv.at[0], partner).wait_send()

    def await_heads(at):
        for step in range(1, peers):
            plane = mod_ring(z + stride * step)
            slot = lax.div(lax.rem(lax.rem(plane, half) - z_lo + half, half), stride)
            hi = lax.div(plane, half)
            rows = pl.ds(4 * at, 4)
            remote(
                x_send.at[step, rows], x_recv.at[slot, hi, rows],
                xs_send.at[step, at], xs_recv.at[slot, hi, at], device(plane, core, me),
            ).wait_recv()

    def final_core(way, step):
        if step < stride - 3:
            return None
        return (step == stride - 3) != (way == 1) and 1 or 0

    def sum_copy(way, step, at):
        mine, theirs, ends = ((r_send, r_recv, r_last), (l_send, l_recv, l_last))[way]
        span_s = slice(at * sum_span, (at + 1) * sum_span)
        dst = theirs.at[step, :, span_s]
        sem = rs_recv.at[way, step, at]
        target = (right, left)[way]
        to_core = final_core(way, step)
        if to_core is not None:
            dst = ends.at[core, :, span_s]
            sem = last_recv.at[way, core, at]
            target = (right_of, left_of)[way][to_core]
        return remote(mine.at[step, :, span_s], dst, rs_send.at[way, step, at], sem, target)

    sum_span = width // SUM_PARTS
    chunk = width // SUM_PIECES
    rows_x = 4 * tok
    for step in range(stride - 1):
        if step % 2 == 0:
            await_heads(step // 2)
            rows = slice(2 * step, 2 * step + 4)
            heads = jnp.concatenate(
                [x_recv[at // 2, at % 2, rows].reshape(rows_x, HEAD_DIM) for at in range(2 * pairs)],
                axis=1,
            )
        for part_at in range(SUM_PARTS):
            span_s = slice(part_at * sum_span, (part_at + 1) * sum_span)
            if step % 2 == 0:
                for at in range(part_at * sum_span, (part_at + 1) * sum_span, chunk):
                    weights = wo[:, :, :, at : at + chunk].reshape(2 * pairs * HEAD_DIM, chunk)
                    product = jnp.dot(heads, weights, preferred_element_type=F32)
                    part[rows, :, at : at + chunk] = product.reshape(4, tok, chunk)
            for way, mine, theirs in ((0, r_send, r_recv), (1, l_send, l_recv)):
                share = part[step * 2 + way, :, span_s]
                if step >= 2:
                    sum_copy(way, step - 2, part_at).wait_recv()
                    share = share + theirs[step - 2, :, span_s].astype(F32)
                mine[step, :, span_s] = share.astype(BF16)
                sum_copy(way, step, part_at).start()

    fin_send[...] = part[2 * stride - 1 - other].astype(BF16)
    give_fin = remote(fin_send, fin_recv, misc_send.at[1], misc_recv.at[1], partner)
    give_fin.start()

    def drain_sum(step):
        for way in (0, 1):
            for at in range(SUM_PARTS):
                sum_copy(way, step, at).wait_send()

    for step in range(1, peers):
        for at in range(pieces):
            head_copy(step, at).wait_send()
    for step in range(stride - 2):
        drain_sum(step)

    def await_last(way, batch):
        ends = (r_last, l_last)[way]
        for at in range(SUM_PARTS):
            dst = ends.at[batch, :, at * sum_span : (at + 1) * sum_span]
            remote(
                dst, dst, rs_send.at[way, 0, at], last_recv.at[way, batch, at], partner
            ).wait_recv()

    def attend(batch, own_share):
        gate = rows_of[2, 2 + batch]
        if stride > 2:
            for way in (0, 1):
                await_last(way, batch)
            sides = r_last[batch].astype(F32) + l_last[batch].astype(F32)
        else:
            for way in (0, 1):

                @pl.when(core == way)
                def _():
                    await_last(way, batch)

            sides = jnp.where(core == 0, r_last[batch].astype(F32), l_last[batch].astype(F32))
        projection = own_share + sides
        out[batch] = (prev[batch].astype(F32) + gate * projection).astype(BF16)

    attend(core, part[2 * stride - 1 - core])
    give_fin.wait_recv()
    attend(other, fin_recv[...].astype(F32))

    give_fin.wait_send()
    drain_sum(stride - 2)


def body(slab_queue, levels, mod_table, w_qkv, q_gain, k_gain, w_out):
    batch, _, tok, width = slab_queue.shape
    ring = lax.axis_size("tm")
    cols = lax.axis_size("space") // 2
    half = ring // 2
    group = 2 if ring > 4 else 1
    stride = half // group
    vmem = pl.BlockSpec(memory_space=pltpu.VMEM)
    hbm = pl.BlockSpec(memory_space=pltpu.HBM)
    dma = pltpu.SemaphoreType.DMA
    block = (tok, width)
    return pl.pallas_call(
        functools.partial(kernel, ring, cols),
        out_shape=pltpu.VMEM((batch, tok, width), BF16),
        in_specs=[hbm] * 7,
        out_specs=vmem,
        scratch_shapes=[
            pltpu.VMEM((batch,) + block, BF16),
            pltpu.SMEM(levels.shape, jnp.int32),
            pltpu.VMEM((3, mod_table.shape[0], width), BF16),
            pltpu.VMEM((3, 4, 1, width), F32),
            pltpu.VMEM(block, BF16),
            pltpu.VMEM((2 * ring,) + block, BF16),
            pltpu.VMEM((width, 3 * HEAD_DIM), BF16),
            pltpu.VMEM((1, HEAD_DIM), F32),
            pltpu.VMEM((1, HEAD_DIM), F32),
            pltpu.VMEM((group, 2, HEAD_DIM, width), BF16),
            pltpu.VMEM((2, ring, tok, 3 * HEAD_DIM), BF16),
            pltpu.VMEM((cols, 2, tok, 3 * HEAD_DIM), BF16),
            pltpu.VMEM((cols, 2, tok, HEAD_DIM), BF16),
            pltpu.VMEM((2, ring, tok, HEAD_DIM), BF16),
            pltpu.VMEM((2, ring, tok, HEAD_DIM), F32),
            pltpu.VMEM((2, ring, tok, HEAD_DIM), BF16),
            pltpu.VMEM((ring // stride, 2 * stride, tok, HEAD_DIM), BF16),
            pltpu.VMEM((group, 2, 2 * stride, tok, HEAD_DIM), BF16),
            pltpu.VMEM((2 * stride,) + block, F32),
            pltpu.VMEM((stride - 1,) + block, BF16),
            pltpu.VMEM((stride - 1,) + block, BF16),
            pltpu.VMEM((stride - 1,) + block, BF16),
            pltpu.VMEM((stride - 1,) + block, BF16),
            pltpu.VMEM((batch,) + block, BF16),
            pltpu.VMEM((batch,) + block, BF16),
            pltpu.VMEM((batch,) + block, BF16),
            pltpu.VMEM(block, BF16),
            pltpu.VMEM(block, BF16),
            dma((7,)),
            dma((5,)),
            dma((5,)),
            dma((1,)),
            dma((2, half + 1, 2, RING_PARTS)),
            dma((1,)),
            dma((1,)),
            dma((1,)),
            dma((2,)),
            dma((ring // stride, stride // 2)),
            dma((group, 2, stride // 2)),
            dma((2, stride - 1, SUM_PARTS)),
            dma((2, stride - 1, SUM_PARTS)),
            dma((2, batch, SUM_PARTS)),
            dma((2,)),
            dma((2,)),
            dma((1,)),
            dma((1,)),
            dma((group,)),
            dma((group,)),
            dma((cols,)),
            dma((cols,)),
            dma((2,)),
        ],
        compiler_params=pltpu.CompilerParams(
            collective_id=0, has_side_effects=True, vmem_limit_bytes=VMEM_BYTES
        ),
        cost_estimate=pl.CostEstimate(
            flops=4 * 10**9, bytes_accessed=8 * 10**6, transcendentals=4 * 10**5
        ),
    )(
        slab_queue.reshape(batch, tok, width), levels, jnp.swapaxes(mod_table, 0, 1),
        w_qkv.reshape(width, 3 * HEAD_DIM), q_gain, k_gain, w_out,
    ).reshape(batch, 1, tok, width)


def solution(mesh):
    placed = (
        P(None, "tm", "space", None),
        P(),
        P(),
        P(None, "tm", None),
        P("tm", None),
        P("tm", None),
        P("tm", None),
    )
    return jax.shard_map(
        body, mesh=mesh, in_specs=placed, out_specs=P(None, "tm", "space", None), check_vma=False
    )
```

```python
import functools
import math

import jax
import jax.numpy as jnp
from jax import lax
from jax.experimental import pallas as pl
from jax.experimental.pallas import tpu as pltpu
from jax.sharding import PartitionSpec as P

HEAD_DIM = 128
W_PIECES = 12
RING_PARTS = 2
SUM_PIECES = 4
SUM_PARTS = 2
VMEM_BYTES = 63 * 1024 * 1024
MESH = pl.DeviceIdType.MESH
F32 = jnp.float32
BF16 = jnp.bfloat16


def dot_t(left, right):
    return lax.dot_general(left, right, (((1,), (1,)), ((), ())), preferred_element_type=F32)


def head_norm(values, gain):
    values = values.astype(F32)
    factor = lax.rsqrt(jnp.mean(jnp.square(values), axis=-1, keepdims=True) + 1e-06)
    return (values * factor * gain).astype(BF16)


def kernel(
    ring, cols,
    slab_in, levels_in, mod_in, w_qkv, q_gain, k_gain, w_out,
    out,
    slab, levels, mod, rows_of, mod_send, tokens, w_buf, gq, gk, wo, qkv, sp_in, sp_out, sp_back, tmp_out, comb,
    x_send, x_recv, part, r_send, r_recv, l_send, l_recv, r_last, l_last, prev, fin_send, fin_recv,
    loc_sem, pair_send, pair_recv, ag_send, ag_recv, aa_send, aa_recv, rt_send, rt_recv,
    xs_send, xs_recv, rs_send, rs_recv, last_recv, misc_send, misc_recv, w_send, w_recv,
    wz_send, wz_recv, wp_send, wp_recv, wd_sem,
):
    half = ring // 2
    group = 2 if ring > 4 else 1
    stride = half // group
    peers = ring // stride
    pieces = stride // 2
    slabs = ring
    tok, width = slab.shape[1], slab.shape[2]
    piece = width // W_PIECES
    tm, space = lax.axis_index("tm"), lax.axis_index("space")
    core, z_lo = lax.rem(tm, 2), lax.div(tm, 2)
    me, z_hi = lax.div(space, 2), lax.rem(space, 2)
    z = z_hi * half + z_lo
    other = 1 - core
    inv_root = 1.0 / math.sqrt(HEAD_DIM)

    def mod_ring(value):
        return lax.rem(value + ring, ring)

    def device(plane, of_core, column):
        return (lax.rem(plane, half) * 2 + of_core, column * 2 + lax.div(plane, half))

    def here(column):
        return (tm, column * 2 + z_hi)

    right = device(mod_ring(z + 1), core, me)
    left = device(mod_ring(z - 1), core, me)
    partner = (z_lo * 2 + other, space)
    tm_next = (lax.rem(tm + 1, slabs), space)
    tm_far = (lax.rem(tm + jnp.where(core == 1, 1, slabs - 1), slabs), space)

    def remote(src, dst, send_sem, recv_sem, target):
        return pltpu.make_async_remote_copy(
            src_ref=src, dst_ref=dst, send_sem=send_sem, recv_sem=recv_sem,
            device_id=target, device_id_type=MESH,
        )

    own_head = core == z_hi
    fetch_levels = pltpu.make_async_copy(levels_in, levels, loc_sem.at[2])
    fetch_mod = pltpu.make_async_copy(mod_in, mod, loc_sem.at[3])
    fetch_slab = pltpu.make_async_copy(slab_in, slab, loc_sem.at[4])
    local_w = pltpu.make_async_copy(w_qkv, w_buf, loc_sem.at[0])
    local_wo = pltpu.make_async_copy(w_out, wo.at[0, core], loc_sem.at[1])
    local_gq = pltpu.make_async_copy(q_gain, gq, loc_sem.at[5])
    local_gk = pltpu.make_async_copy(k_gain, gk, loc_sem.at[6])
    fetch_levels.start()
    fetch_mod.start()
    fetch_slab.start()

    barrier = pltpu.get_barrier_semaphore()
    right_of = [device(mod_ring(z + 1), at, me) for at in (0, 1)]
    left_of = [device(mod_ring(z - 1), at, me) for at in (0, 1)]
    for target in (*right_of, *left_of, partner, tm_far):
        pl.semaphore_signal(barrier, inc=1, device_id=target, device_id_type=MESH)

    def greet(step, carry):
        column = lax.rem(me + step, cols)
        pl.semaphore_signal(barrier, inc=1, device_id=here(column), device_id_type=MESH)
        return carry

    lax.fori_loop(1, cols, greet, 0)

    def greet_class(step, carry):
        target = device(mod_ring(z + stride * step), core, me)
        pl.semaphore_signal(barrier, inc=1, device_id=target, device_id_type=MESH)
        return carry

    lax.fori_loop(1, peers, greet_class, 0)

    fetch_levels.wait()
    fetch_mod.wait()

    tm_before = lax.rem(tm + slabs - 1, slabs)
    pick_row = lax.broadcasted_iota(jnp.int32, (16, mod.shape[1]), 0)
    pick_col = lax.broadcasted_iota(jnp.int32, (16, mod.shape[1]), 1)
    hot = jnp.zeros((16, mod.shape[1]), F32)
    for at, (batch, of_slab) in enumerate(((0, tm), (1, tm), (0, tm_before), (1, tm_before))):
        hot = jnp.where((pick_row == at) & (pick_col == levels[batch, of_slab]), 1.0, hot)

    def pick(kind, places):
        picked = jnp.dot(hot.astype(BF16), mod[kind], preferred_element_type=F32)
        for at in places:
            rows_of[kind, at] = picked[at : at + 1]

    pick(0, (0, 1))
    pick(1, (0, 1))

    def modulate(batch):
        values = slab[batch].astype(F32)
        centre = jnp.mean(values, axis=-1, keepdims=True)
        moved = values - centre
        spread = jnp.mean(jnp.square(moved), axis=-1, keepdims=True)
        normed = moved * lax.rsqrt(spread + 1e-06)
        return (normed * (1.0 + rows_of[1, batch]) + rows_of[0, batch]).astype(BF16)

    fetch_slab.wait()

    @pl.when(own_head)
    def _():
        local_gq.start()
        local_gk.start()
        local_w.start()

    local_wo.start()

    tokens[z * 2 + core] = modulate(core)
    pl.semaphore_wait(barrier, 6 + cols - 1 + peers - 1)

    span = width // RING_PARTS

    def gather_copy(way, step, t, origin, at):
        block = tokens.at[origin * 2 + t, :, at * span : (at + 1) * span]
        return remote(
            block, block, ag_send.at[0], ag_recv.at[way, step, t, at], (right, left)[way]
        )

    def gather_start(t):
        for at in range(RING_PARTS):
            for way in (0, 1):
                gather_copy(way, 1, t, z, at).start()

    gather_start(core)
    mod_send[...] = modulate(other)
    to_pair = remote(mod_send, tokens.at[z * 2 + core], pair_send.at[0], pair_recv.at[0], partner)
    to_pair.start()
    from_pair = remote(mod_send, tokens.at[z * 2 + other], pair_send.at[0], pair_recv.at[0], partner)
    from_pair.wait_recv()
    gather_start(other)

    pick(2, (2, 3))

    def give_w(at):
        rows = pl.ds(at * piece, piece)
        return remote(w_qkv.at[rows], w_buf.at[rows], w_send.at[0], w_recv.at[0], partner)

    whole_w = remote(w_qkv, w_buf, w_send.at[0], w_recv.at[0], partner)
    give_gq = remote(q_gain, gq, pair_send.at[2], pair_recv.at[2], partner)
    give_gk = remote(k_gain, gk, pair_send.at[3], pair_recv.at[3], partner)
    give_wo = remote(w_out, wo.at[0, core], pair_send.at[4], pair_recv.at[4], partner)
    take_wo = remote(w_out, wo.at[0, other], pair_send.at[4], pair_recv.at[4], partner)
    pass_slab = remote(slab, prev, misc_send.at[0], misc_recv.at[0], tm_next)

    @pl.when(own_head)
    def _():
        give_gq.start()
        give_gk.start()

    pairs = group
    rows_w = 2 * HEAD_DIM // cols
    cut_rows = pl.ds(pl.multiple_of(lax.div(me, 2) * rows_w, rows_w), rows_w)
    cut_cols = pl.ds(pl.multiple_of(lax.rem(me, 2) * (width // 2), width // 2), width // 2)

    def plane_piece(at):
        apart = stride * at if 2 * stride * at < half else stride * at - half
        if 2 * stride * at == half:
            apart = jnp.where(core == 0, half // 2, -(half // 2))
        return remote(
            w_out.at[cut_rows, cut_cols], wo.at[at, core, cut_rows, cut_cols],
            wz_send.at[at], wz_recv.at[at], device(mod_ring(z - apart), core, me),
        )

    def spread_piece(column, source):
        rows = pl.ds(pl.multiple_of(lax.div(source, 2) * rows_w, rows_w), rows_w)
        span = pl.ds(pl.multiple_of(lax.rem(source, 2) * (width // 2), width // 2), width // 2)
        piece_of = wo.at[1:pairs, core, rows, span]
        return remote(
            piece_of, piece_of, wp_send.at[column], wp_recv.at[source], here(column)
        )

    def pair_wo(of_core):
        block = wo.at[1:pairs, of_core]
        return remote(block, block, wd_sem.at[0], wd_sem.at[1], partner)

    for at in range(1, pairs):
        plane_piece(at).start()

    def slab_copy(hi, column, source):
        return remote(
            qkv.at[hi, column], sp_in.at[source, hi], aa_send.at[0], aa_recv.at[0],
            here(column),
        )

    first_dot = max(1, 3 * half // 8)
    give_steps = max(first_dot - 1, 1)
    per_step = W_PIECES // give_steps

    def reach(at):
        done = jnp.minimum(2 * (at - first_dot + 1), at + 1)
        return jnp.where(at < first_dot, 0, jnp.where(at == half, half + 1, done))

    def gather_step(step, carry):
        step = jnp.asarray(step, jnp.int32)
        plane_a = mod_ring(z - step)
        plane_b = mod_ring(z + step)
        first, last = reach(step - 1), reach(step)
        middle = jnp.where(last - first == 2, first + 1, first)

        def turn_step(turn, inner):
            t = jnp.where(turn == 0, core, other)
            for at in range(RING_PARTS):
                for way, origin in ((0, plane_a), (1, plane_b)):

                    @pl.when((step < half) | (t == way))
                    def _():
                        gather_copy(way, step, t, origin, at).wait_recv()

                    @pl.when((step < half - 1) | ((step == half - 1) & (t == way)))
                    def _():
                        gather_copy(way, step + 1, t, origin, at).start()

            if pairs > 1:

                @pl.when((step == 2) & (turn == 0))
                def _():
                    for at in range(1, pairs):
                        plane_piece(at).wait_recv()

                    def spread(ahead, most):
                        spread_piece(lax.rem(me + ahead, cols), me).start()
                        return most

                    lax.fori_loop(1, cols, spread, 0)

                @pl.when((step == half - 1) & (turn == 0))
                def _():
                    def await_spread(ahead, most):
                        spread_piece(me, lax.rem(me + ahead, cols)).wait_recv()
                        return most

                    lax.fori_loop(1, cols, await_spread, 0)
                    pair_wo(core).start()

            @pl.when(own_head & (step <= give_steps))
            def _():
                def one(at, most):
                    give_w(at).start()
                    return most

                share = per_step // 2
                begin = (2 * (step - 1) + turn) * share
                lax.fori_loop(begin, begin + share, one, 0)

            @pl.when((step == first_dot) & (turn == 0))
            def _():
                give_wo.start()

                @pl.when(own_head)
                def _():
                    local_w.wait()
                    local_gq.wait()
                    local_gk.wait()

                @pl.when(jnp.logical_not(own_head))
                def _():
                    whole_w.wait_recv()
                    give_gq.wait_recv()
                    give_gk.wait_recv()

            lax.fori_loop(
                jnp.where(turn == 0, first, middle), jnp.where(turn == 0, middle, last),
                project_step, 0,
            )
            return inner

        lax.fori_loop(0, 2, turn_step, 0)
        return carry

    def project_step(step, carry):
        planes = (mod_ring(z - step), mod_ring(z + step))
        rows = jnp.concatenate(
            [tokens[pl.ds(plane * 2, 2)].reshape(2 * tok, width) for plane in planes], axis=0
        )
        projected = jnp.dot(rows, w_buf[...], preferred_element_type=F32).astype(BF16)
        queries = head_norm(projected[:, :HEAD_DIM], gq[...])
        keys = head_norm(projected[:, HEAD_DIM : 2 * HEAD_DIM], gk[...])
        values = projected[:, 2 * HEAD_DIM :]
        def place(at):
            hi, lo = lax.div(planes[at], half), lax.rem(planes[at], half)
            for t in (0, 1):
                cut = slice((at * 2 + t) * tok, (at * 2 + t + 1) * tok)
                column = lo * 2 + t
                qkv[hi, column, :, 0:HEAD_DIM] = queries[cut]
                qkv[hi, column, :, HEAD_DIM : 2 * HEAD_DIM] = keys[cut]
                qkv[hi, column, :, 2 * HEAD_DIM :] = values[cut]

                @pl.when(column != me)
                def _():
                    slab_copy(hi, column, me).start()

        place(0)

        @pl.when(lax.rem(step, half) != 0)
        def _():
            place(1)

        return carry

    rows_t = slabs * tok
    at_row = lax.broadcasted_iota(jnp.int32, (rows_t, rows_t), 0) & (tok - 1)
    at_col = lax.broadcasted_iota(jnp.int32, (rows_t, rows_t), 1) & (tok - 1)
    same = at_row == at_col

    def temporal(hi):
        queries = qkv[hi, :, :, 0:HEAD_DIM].reshape(rows_t, HEAD_DIM)
        keys = qkv[hi, :, :, HEAD_DIM : 2 * HEAD_DIM].reshape(rows_t, HEAD_DIM)
        values = qkv[hi, :, :, 2 * HEAD_DIM :].reshape(rows_t, HEAD_DIM)
        scores = jnp.where(same, dot_t(queries, keys) * inv_root, -jnp.inf)
        weights = jnp.exp(scores - jnp.max(scores, axis=-1, keepdims=True))
        total = jnp.sum(weights, axis=-1, keepdims=True)
        mixed = jnp.dot(weights.astype(BF16), values, preferred_element_type=F32) / total
        tmp_out[hi] = mixed.reshape(slabs, tok, HEAD_DIM)

    lax.fori_loop(1, half, gather_step, 0)
    temporal(z_hi)
    gather_step(half, 0)
    pass_slab.start()
    sp_in[me] = qkv[:, me]

    mine_late = lax.div(me, 2) == z_lo

    @pl.when(mine_late)
    def _():
        temporal(1 - z_hi)

    part_in = sp_in.at[0 : cols - 1]
    remote(part_in, part_in, aa_send.at[0], aa_recv.at[0], partner).wait_recv()

    is_late = jnp.where(mine_late, 1, 0)

    def back_copy(column, of_slab):
        return remote(
            sp_out.at[column], sp_back.at[:, of_slab], rt_send.at[0], rt_recv.at[is_late],
            here(column),
        )

    batch_s = cols
    rows_s = batch_s * 2 * tok

    def spatial_step(step, carry):
        keys = sp_in[:, :, :, HEAD_DIM : 2 * HEAD_DIM].reshape(cols * 2 * tok, HEAD_DIM)
        values = sp_in[:, :, :, 2 * HEAD_DIM :].reshape(cols * 2 * tok, HEAD_DIM)
        queries = sp_in[pl.ds(step * batch_s, batch_s), :, :, 0:HEAD_DIM].reshape(rows_s, HEAD_DIM)
        scores = dot_t(queries, keys) * inv_root
        weights = jnp.exp(scores - jnp.max(scores, axis=-1, keepdims=True))
        total = jnp.sum(weights, axis=-1, keepdims=True)
        mixed = jnp.dot(weights.astype(BF16), values, preferred_element_type=F32) / total
        sp_out[pl.ds(step * batch_s, batch_s)] = mixed.astype(BF16).reshape(batch_s, 2, tok, HEAD_DIM)
        for at in range(batch_s):
            column = step * batch_s + at

            @pl.when(column != me)
            def _():
                back_copy(column, me).start()

        return carry

    lax.fori_loop(0, cols // batch_s, spatial_step, 0)
    sp_back[:, me] = sp_out[me]

    @pl.when(jnp.logical_not(mine_late))
    def _():
        temporal(1 - z_hi)


    def await_back(late, count):
        block = sp_back.at[:, 0:count]
        remote(block, block, rt_send.at[0], rt_recv.at[late], partner).wait_recv()

    def combine(ahead, carry):
        of_slab = lax.rem(2 * z_lo + ahead, slabs)
        both = sp_back[:, of_slab].astype(F32) + tmp_out[:, of_slab]
        comb[:, of_slab] = both.astype(BF16)
        return carry

    @pl.when(mine_late)
    def _():
        await_back(0, slabs - 2)

    @pl.when(jnp.logical_not(mine_late))
    def _():
        await_back(0, slabs - 3)

    lax.fori_loop(2, slabs, combine, 0)

    def fill(dst, plane, piece_at):
        def one(at, carry):
            step = lax.div(at, 2)
            block = jnp.where(lax.rem(at, 2) == 0, 2 * stride - 1 - step, step)
            place = lax.rem(2 * plane + 2 * ring - (stride - 1) + block, 2 * ring)
            from_slab = lax.rem(lax.rem(place, slabs) + slabs - 1, slabs)
            dst[at] = comb[lax.div(place, slabs), from_slab]
            return carry

        lax.fori_loop(4 * piece_at, 4 * piece_at + 4, one, 0)

    def head_copy(step, at):
        plane = mod_ring(z + stride * step)
        slot = lax.div(lax.rem(z_lo - lax.rem(plane, half) + half, half), stride)
        rows = pl.ds(4 * at, 4)
        return remote(
            x_send.at[step, rows], x_recv.at[slot, z_hi, rows],
            xs_send.at[step, at], xs_recv.at[slot, z_hi, at], device(plane, core, me),
        )

    def send_heads(step, at):
        fill(x_send.at[step], mod_ring(z + stride * step), at)
        head_copy(step, at).start()

    far = peers // 2
    for at in range(pieces):
        if at < pieces - 1:
            send_heads(far, at)
        for step in range(1, peers):
            if step != far:
                send_heads(step, at)
    for at in range(pieces - 1):
        fill(x_recv.at[0, z_hi], z, at)

    @pl.when(mine_late)
    def _():
        await_back(1, 1)

    @pl.when(jnp.logical_not(mine_late))
    def _():
        await_back(1, 2)

    lax.fori_loop(0, 2, combine, 0)
    send_heads(far, pieces - 1)
    fill(x_recv.at[0, z_hi], z, pieces - 1)
    local_wo.wait()
    take_wo.wait_recv()
    if pairs > 1:
        pair_wo(other).wait_recv()

    to_pair.wait_send()

    @pl.when(own_head)
    def _():
        whole_w.wait_send()
        give_gq.wait_send()
        give_gk.wait_send()

    give_wo.wait_send()
    pass_slab.wait_send()
    pass_slab.wait_recv()
    for at in range(1, pairs):
        plane_piece(at).wait_send()
    if pairs > 1:
        pair_wo(core).wait_send()

        def drain_spread(ahead, carry):
            spread_piece(lax.rem(me + ahead, cols), me).wait_send()
            return carry

        lax.fori_loop(1, cols, drain_spread, 0)
    sent = tokens.at[0 : 2 * ring - 2]
    remote(sent, sent, ag_send.at[0], ag_recv.at[0, 0, 0, 0], partner).wait_send()
    sent = qkv.at[:, 0 : cols - 1]
    remote(sent, sent, aa_send.at[0], aa_recv.at[0], partner).wait_send()
    sent = sp_out.at[0 : cols - 1]
    remote(sent, sent, rt_send.at[0], rt_recv.at[0], partner).wait_send()

    def await_heads(at):
        for step in range(1, peers):
            plane = mod_ring(z + stride * step)
            slot = lax.div(lax.rem(lax.rem(plane, half) - z_lo + half, half), stride)
            hi = lax.div(plane, half)
            rows = pl.ds(4 * at, 4)
            remote(
                x_send.at[step, rows], x_recv.at[slot, hi, rows],
                xs_send.at[step, at], xs_recv.at[slot, hi, at], device(plane, core, me),
            ).wait_recv()

    def final_core(way, step):
        if step < stride - 3:
            return None
        return (step == stride - 3) != (way == 1) and 1 or 0

    def sum_copy(way, step, at):
        mine, theirs, ends = ((r_send, r_recv, r_last), (l_send, l_recv, l_last))[way]
        span_s = slice(at * sum_span, (at + 1) * sum_span)
        dst = theirs.at[step, :, span_s]
        sem = rs_recv.at[way, step, at]
        target = (right, left)[way]
        to_core = final_core(way, step)
        if to_core is not None:
            dst = ends.at[core, :, span_s]
            sem = last_recv.at[way, core, at]
            target = (right_of, left_of)[way][to_core]
        return remote(mine.at[step, :, span_s], dst, rs_send.at[way, step, at], sem, target)

    sum_span = width // SUM_PARTS
    chunk = width // SUM_PIECES
    rows_x = 4 * tok
    for step in range(stride - 1):
        if step % 2 == 0:
            await_heads(step // 2)
            rows = slice(2 * step, 2 * step + 4)
            heads = jnp.concatenate(
                [x_recv[at // 2, at % 2, rows].reshape(rows_x, HEAD_DIM) for at in range(2 * pairs)],
                axis=1,
            )
        for part_at in range(SUM_PARTS):
            span_s = slice(part_at * sum_span, (part_at + 1) * sum_span)
            if step % 2 == 0:
                for at in range(part_at * sum_span, (part_at + 1) * sum_span, chunk):
                    weights = wo[:, :, :, at : at + chunk].reshape(2 * pairs * HEAD_DIM, chunk)
                    product = jnp.dot(heads, weights, preferred_element_type=F32)
                    part[rows, :, at : at + chunk] = product.reshape(4, tok, chunk)
            for way, mine, theirs in ((0, r_send, r_recv), (1, l_send, l_recv)):
                share = part[step * 2 + way, :, span_s]
                if step >= 2:
                    sum_copy(way, step - 2, part_at).wait_recv()
                    share = share + theirs[step - 2, :, span_s].astype(F32)
                mine[step, :, span_s] = share.astype(BF16)
                sum_copy(way, step, part_at).start()

    fin_send[...] = part[2 * stride - 1 - other].astype(BF16)
    give_fin = remote(fin_send, fin_recv, misc_send.at[1], misc_recv.at[1], partner)
    give_fin.start()

    def drain_sum(step):
        for way in (0, 1):
            for at in range(SUM_PARTS):
                sum_copy(way, step, at).wait_send()

    for step in range(1, peers):
        for at in range(pieces):
            head_copy(step, at).wait_send()
    for step in range(stride - 2):
        drain_sum(step)

    def await_last(way, batch):
        ends = (r_last, l_last)[way]
        for at in range(SUM_PARTS):
            dst = ends.at[batch, :, at * sum_span : (at + 1) * sum_span]
            remote(
                dst, dst, rs_send.at[way, 0, at], last_recv.at[way, batch, at], partner
            ).wait_recv()

    def attend(batch, own_share):
        gate = rows_of[2, 2 + batch]
        if stride > 2:
            for way in (0, 1):
                await_last(way, batch)
            sides = r_last[batch].astype(F32) + l_last[batch].astype(F32)
        else:
            for way in (0, 1):

                @pl.when(core == way)
                def _():
                    await_last(way, batch)

            sides = jnp.where(core == 0, r_last[batch].astype(F32), l_last[batch].astype(F32))
        projection = own_share + sides
        out[batch] = (prev[batch].astype(F32) + gate * projection).astype(BF16)

    attend(core, part[2 * stride - 1 - core])
    give_fin.wait_recv()
    attend(other, fin_recv[...].astype(F32))

    give_fin.wait_send()
    drain_sum(stride - 2)


def body(slab_queue, levels, mod_table, w_qkv, q_gain, k_gain, w_out):
    batch, _, tok, width = slab_queue.shape
    ring = lax.axis_size("tm")
    cols = lax.axis_size("space") // 2
    half = ring // 2
    group = 2 if ring > 4 else 1
    stride = half // group
    vmem = pl.BlockSpec(memory_space=pltpu.VMEM)
    hbm = pl.BlockSpec(memory_space=pltpu.HBM)
    dma = pltpu.SemaphoreType.DMA
    block = (tok, width)
    return pl.pallas_call(
        functools.partial(kernel, ring, cols),
        out_shape=pltpu.VMEM((batch, tok, width), BF16),
        in_specs=[hbm] * 7,
        out_specs=vmem,
        scratch_shapes=[
            pltpu.VMEM((batch,) + block, BF16),
            pltpu.SMEM(levels.shape, jnp.int32),
            pltpu.VMEM((3, mod_table.shape[0], width), BF16),
            pltpu.VMEM((3, 4, 1, width), F32),
            pltpu.VMEM(block, BF16),
            pltpu.VMEM((2 * ring,) + block, BF16),
            pltpu.VMEM((width, 3 * HEAD_DIM), BF16),
            pltpu.VMEM((1, HEAD_DIM), F32),
            pltpu.VMEM((1, HEAD_DIM), F32),
            pltpu.VMEM((group, 2, HEAD_DIM, width), BF16),
            pltpu.VMEM((2, ring, tok, 3 * HEAD_DIM), BF16),
            pltpu.VMEM((cols, 2, tok, 3 * HEAD_DIM), BF16),
            pltpu.VMEM((cols, 2, tok, HEAD_DIM), BF16),
            pltpu.VMEM((2, ring, tok, HEAD_DIM), BF16),
            pltpu.VMEM((2, ring, tok, HEAD_DIM), F32),
            pltpu.VMEM((2, ring, tok, HEAD_DIM), BF16),
            pltpu.VMEM((ring // stride, 2 * stride, tok, HEAD_DIM), BF16),
            pltpu.VMEM((group, 2, 2 * stride, tok, HEAD_DIM), BF16),
            pltpu.VMEM((2 * stride,) + block, F32),
            pltpu.VMEM((stride - 1,) + block, BF16),
            pltpu.VMEM((stride - 1,) + block, BF16),
            pltpu.VMEM((stride - 1,) + block, BF16),
            pltpu.VMEM((stride - 1,) + block, BF16),
            pltpu.VMEM((batch,) + block, BF16),
            pltpu.VMEM((batch,) + block, BF16),
            pltpu.VMEM((batch,) + block, BF16),
            pltpu.VMEM(block, BF16),
            pltpu.VMEM(block, BF16),
            dma((7,)),
            dma((5,)),
            dma((5,)),
            dma((1,)),
            dma((2, half + 1, 2, RING_PARTS)),
            dma((1,)),
            dma((1,)),
            dma((1,)),
            dma((2,)),
            dma((ring // stride, stride // 2)),
            dma((group, 2, stride // 2)),
            dma((2, stride - 1, SUM_PARTS)),
            dma((2, stride - 1, SUM_PARTS)),
            dma((2, batch, SUM_PARTS)),
            dma((2,)),
            dma((2,)),
            dma((1,)),
            dma((1,)),
            dma((group,)),
            dma((group,)),
            dma((cols,)),
            dma((cols,)),
            dma((2,)),
        ],
        compiler_params=pltpu.CompilerParams(
            collective_id=0, has_side_effects=True, vmem_limit_bytes=VMEM_BYTES
        ),
        cost_estimate=pl.CostEstimate(
            flops=4 * 10**9, bytes_accessed=8 * 10**6, transcendentals=4 * 10**5
        ),
    )(
        slab_queue.reshape(batch, tok, width), levels, jnp.swapaxes(mod_table, 0, 1),
        w_qkv.reshape(width, 3 * HEAD_DIM), q_gain, k_gain, w_out,
    ).reshape(batch, 1, tok, width)


def solution(mesh):
    placed = (
        P(None, "tm", "space", None),
        P(),
        P(),
        P(None, "tm", None),
        P("tm", None),
        P("tm", None),
        P("tm", None),
    )
    return jax.shard_map(
        body, mesh=mesh, in_specs=placed, out_specs=P(None, "tm", "space", None), check_vma=False
    )
```

```python
import functools
import math

import jax
import jax.numpy as jnp
from jax import lax
from jax.experimental import pallas as pl
from jax.experimental.pallas import tpu as pltpu
from jax.sharding import PartitionSpec as P

HEAD_DIM = 128
W_PIECES = 12
RING_PARTS = 2
SUM_PIECES = 4
SUM_PARTS = 4
VMEM_BYTES = 63 * 1024 * 1024
MESH = pl.DeviceIdType.MESH
F32 = jnp.float32
BF16 = jnp.bfloat16


def dot_t(left, right):
    return lax.dot_general(left, right, (((1,), (1,)), ((), ())), preferred_element_type=F32)


def head_norm(values, gain):
    values = values.astype(F32)
    factor = lax.rsqrt(jnp.mean(jnp.square(values), axis=-1, keepdims=True) + 1e-06)
    return (values * factor * gain).astype(BF16)


def kernel(
    ring, cols,
    slab_in, levels_in, mod_in, w_qkv, q_gain, k_gain, w_out,
    out,
    slab, levels, mod, rows_of, mod_send, tokens, w_buf, gq, gk, wo, qkv, sp_in, sp_out, sp_back, tmp_out, comb,
    x_send, x_recv, part, r_send, r_recv, l_send, l_recv, r_last, l_last, prev, fin_send, fin_recv,
    loc_sem, pair_send, pair_recv, ag_send, ag_recv, aa_send, aa_recv, rt_send, rt_recv,
    xs_send, xs_recv, rs_send, rs_recv, last_recv, misc_send, misc_recv, w_send, w_recv,
    wz_send, wz_recv, wp_send, wp_recv, wd_sem,
):
    half = ring // 2
    group = 2 if ring > 4 else 1
    stride = half // group
    peers = ring // stride
    pieces = stride // 2
    slabs = ring
    tok, width = slab.shape[1], slab.shape[2]
    piece = width // W_PIECES
    tm, space = lax.axis_index("tm"), lax.axis_index("space")
    core, z_lo = lax.rem(tm, 2), lax.div(tm, 2)
    me, z_hi = lax.div(space, 2), lax.rem(space, 2)
    z = z_hi * half + z_lo
    other = 1 - core
    inv_root = 1.0 / math.sqrt(HEAD_DIM)

    def mod_ring(value):
        return lax.rem(value + ring, ring)

    def device(plane, of_core, column):
        return (lax.rem(plane, half) * 2 + of_core, column * 2 + lax.div(plane, half))

    def here(column):
        return (tm, column * 2 + z_hi)

    right = device(mod_ring(z + 1), core, me)
    left = device(mod_ring(z - 1), core, me)
    partner = (z_lo * 2 + other, space)
    tm_next = (lax.rem(tm + 1, slabs), space)
    tm_far = (lax.rem(tm + jnp.where(core == 1, 1, slabs - 1), slabs), space)

    def remote(src, dst, send_sem, recv_sem, target):
        return pltpu.make_async_remote_copy(
            src_ref=src, dst_ref=dst, send_sem=send_sem, recv_sem=recv_sem,
            device_id=target, device_id_type=MESH,
        )

    own_head = core == z_hi
    fetch_levels = pltpu.make_async_copy(levels_in, levels, loc_sem.at[2])
    fetch_mod = pltpu.make_async_copy(mod_in, mod, loc_sem.at[3])
    fetch_slab = pltpu.make_async_copy(slab_in, slab, loc_sem.at[4])
    local_w = pltpu.make_async_copy(w_qkv, w_buf, loc_sem.at[0])
    local_wo = pltpu.make_async_copy(w_out, wo.at[0, core], loc_sem.at[1])
    local_gq = pltpu.make_async_copy(q_gain, gq, loc_sem.at[5])
    local_gk = pltpu.make_async_copy(k_gain, gk, loc_sem.at[6])
    fetch_levels.start()
    fetch_mod.start()
    fetch_slab.start()

    barrier = pltpu.get_barrier_semaphore()
    right_of = [device(mod_ring(z + 1), at, me) for at in (0, 1)]
    left_of = [device(mod_ring(z - 1), at, me) for at in (0, 1)]
    for target in (*right_of, *left_of, partner, tm_far):
        pl.semaphore_signal(barrier, inc=1, device_id=target, device_id_type=MESH)

    def greet(step, carry):
        column = lax.rem(me + step, cols)
        pl.semaphore_signal(barrier, inc=1, device_id=here(column), device_id_type=MESH)
        return carry

    lax.fori_loop(1, cols, greet, 0)

    def greet_class(step, carry):
        target = device(mod_ring(z + stride * step), core, me)
        pl.semaphore_signal(barrier, inc=1, device_id=target, device_id_type=MESH)
        return carry

    lax.fori_loop(1, peers, greet_class, 0)

    fetch_levels.wait()
    fetch_mod.wait()

    tm_before = lax.rem(tm + slabs - 1, slabs)
    pick_row = lax.broadcasted_iota(jnp.int32, (16, mod.shape[1]), 0)
    pick_col = lax.broadcasted_iota(jnp.int32, (16, mod.shape[1]), 1)
    hot = jnp.zeros((16, mod.shape[1]), F32)
    for at, (batch, of_slab) in enumerate(((0, tm), (1, tm), (0, tm_before), (1, tm_before))):
        hot = jnp.where((pick_row == at) & (pick_col == levels[batch, of_slab]), 1.0, hot)
    for kind in range(3):
        picked = jnp.dot(hot.astype(BF16), mod[kind], preferred_element_type=F32)
        for at in range(4):
            rows_of[kind, at] = picked[at : at + 1]

    def modulate(batch):
        values = slab[batch].astype(F32)
        centre = jnp.mean(values, axis=-1, keepdims=True)
        moved = values - centre
        spread = jnp.mean(jnp.square(moved), axis=-1, keepdims=True)
        normed = moved * lax.rsqrt(spread + 1e-06)
        return (normed * (1.0 + rows_of[1, batch]) + rows_of[0, batch]).astype(BF16)

    fetch_slab.wait()

    @pl.when(own_head)
    def _():
        local_gq.start()
        local_gk.start()
        local_w.start()

    local_wo.start()

    tokens[z * 2 + core] = modulate(core)
    pl.semaphore_wait(barrier, 6 + cols - 1 + peers - 1)

    span = width // RING_PARTS

    def gather_copy(way, step, t, origin, at):
        block = tokens.at[origin * 2 + t, :, at * span : (at + 1) * span]
        return remote(
            block, block, ag_send.at[0], ag_recv.at[way, step, t, at], (right, left)[way]
        )

    def gather_start(t):
        for at in range(RING_PARTS):
            for way in (0, 1):
                gather_copy(way, 1, t, z, at).start()

    gather_start(core)
    mod_send[...] = modulate(other)
    to_pair = remote(mod_send, tokens.at[z * 2 + core], pair_send.at[0], pair_recv.at[0], partner)
    to_pair.start()
    from_pair = remote(mod_send, tokens.at[z * 2 + other], pair_send.at[0], pair_recv.at[0], partner)
    from_pair.wait_recv()
    gather_start(other)

    def give_w(at):
        rows = pl.ds(at * piece, piece)
        return remote(w_qkv.at[rows], w_buf.at[rows], w_send.at[0], w_recv.at[0], partner)

    whole_w = remote(w_qkv, w_buf, w_send.at[0], w_recv.at[0], partner)
    give_gq = remote(q_gain, gq, pair_send.at[2], pair_recv.at[2], partner)
    give_gk = remote(k_gain, gk, pair_send.at[3], pair_recv.at[3], partner)
    give_wo = remote(w_out, wo.at[0, core], pair_send.at[4], pair_recv.at[4], partner)
    take_wo = remote(w_out, wo.at[0, other], pair_send.at[4], pair_recv.at[4], partner)
    pass_slab = remote(slab, prev, misc_send.at[0], misc_recv.at[0], tm_next)

    @pl.when(own_head)
    def _():
        give_gq.start()
        give_gk.start()

    pairs = group
    rows_w = 2 * HEAD_DIM // cols
    cut_rows = pl.ds(pl.multiple_of(lax.div(me, 2) * rows_w, rows_w), rows_w)
    cut_cols = pl.ds(pl.multiple_of(lax.rem(me, 2) * (width // 2), width // 2), width // 2)

    def plane_piece(at):
        apart = stride * at if 2 * stride * at < half else stride * at - half
        if 2 * stride * at == half:
            apart = jnp.where(core == 0, half // 2, -(half // 2))
        return remote(
            w_out.at[cut_rows, cut_cols], wo.at[at, core, cut_rows, cut_cols],
            wz_send.at[at], wz_recv.at[at], device(mod_ring(z - apart), core, me),
        )

    def spread_piece(column, source):
        rows = pl.ds(pl.multiple_of(lax.div(source, 2) * rows_w, rows_w), rows_w)
        span = pl.ds(pl.multiple_of(lax.rem(source, 2) * (width // 2), width // 2), width // 2)
        piece_of = wo.at[1:pairs, core, rows, span]
        return remote(
            piece_of, piece_of, wp_send.at[column], wp_recv.at[source], here(column)
        )

    def pair_wo(of_core):
        block = wo.at[1:pairs, of_core]
        return remote(block, block, wd_sem.at[0], wd_sem.at[1], partner)

    for at in range(1, pairs):
        plane_piece(at).start()

    def slab_copy(hi, column, source):
        return remote(
            qkv.at[hi, column], sp_in.at[source, hi], aa_send.at[0], aa_recv.at[0],
            here(column),
        )

    first_dot = max(1, 3 * half // 8)
    give_steps = max(first_dot - 1, 1)
    per_step = W_PIECES // give_steps

    def reach(at):
        done = jnp.minimum(2 * (at - first_dot + 1), at + 1)
        return jnp.where(at < first_dot, 0, jnp.where(at == half, half + 1, done))

    def gather_step(step, carry):
        step = jnp.asarray(step, jnp.int32)
        plane_a = mod_ring(z - step)
        plane_b = mod_ring(z + step)
        first, last = reach(step - 1), reach(step)
        middle = jnp.where(last - first == 2, first + 1, first)

        def turn_step(turn, inner):
            t = jnp.where(turn == 0, core, other)
            for at in range(RING_PARTS):
                for way, origin in ((0, plane_a), (1, plane_b)):

                    @pl.when((step < half) | (t == way))
                    def _():
                        gather_copy(way, step, t, origin, at).wait_recv()

                    @pl.when((step < half - 1) | ((step == half - 1) & (t == way)))
                    def _():
                        gather_copy(way, step + 1, t, origin, at).start()

            if pairs > 1:

                @pl.when((step == 2) & (turn == 0))
                def _():
                    for at in range(1, pairs):
                        plane_piece(at).wait_recv()

                    def spread(ahead, most):
                        spread_piece(lax.rem(me + ahead, cols), me).start()
                        return most

                    lax.fori_loop(1, cols, spread, 0)

                @pl.when((step == half - 1) & (turn == 0))
                def _():
                    def await_spread(ahead, most):
                        spread_piece(me, lax.rem(me + ahead, cols)).wait_recv()
                        return most

                    lax.fori_loop(1, cols, await_spread, 0)
                    pair_wo(core).start()

            @pl.when(own_head & (step <= give_steps))
            def _():
                def one(at, most):
                    give_w(at).start()
                    return most

                share = per_step // 2
                begin = (2 * (step - 1) + turn) * share
                lax.fori_loop(begin, begin + share, one, 0)

            @pl.when((step == first_dot) & (turn == 0))
            def _():
                give_wo.start()

                @pl.when(own_head)
                def _():
                    local_w.wait()
                    local_gq.wait()
                    local_gk.wait()

                @pl.when(jnp.logical_not(own_head))
                def _():
                    whole_w.wait_recv()
                    give_gq.wait_recv()
                    give_gk.wait_recv()

            lax.fori_loop(
                jnp.where(turn == 0, first, middle), jnp.where(turn == 0, middle, last),
                project_step, 0,
            )
            return inner

        lax.fori_loop(0, 2, turn_step, 0)
        return carry

    def project_step(step, carry):
        planes = (mod_ring(z - step), mod_ring(z + step))
        rows = jnp.concatenate(
            [tokens[pl.ds(plane * 2, 2)].reshape(2 * tok, width) for plane in planes], axis=0
        )
        projected = jnp.dot(rows, w_buf[...], preferred_element_type=F32).astype(BF16)
        queries = head_norm(projected[:, :HEAD_DIM], gq[...])
        keys = head_norm(projected[:, HEAD_DIM : 2 * HEAD_DIM], gk[...])
        values = projected[:, 2 * HEAD_DIM :]
        def place(at):
            hi, lo = lax.div(planes[at], half), lax.rem(planes[at], half)
            for t in (0, 1):
                cut = slice((at * 2 + t) * tok, (at * 2 + t + 1) * tok)
                column = lo * 2 + t
                qkv[hi, column, :, 0:HEAD_DIM] = queries[cut]
                qkv[hi, column, :, HEAD_DIM : 2 * HEAD_DIM] = keys[cut]
                qkv[hi, column, :, 2 * HEAD_DIM :] = values[cut]

                @pl.when(column != me)
                def _():
                    slab_copy(hi, column, me).start()

        place(0)

        @pl.when(lax.rem(step, half) != 0)
        def _():
            place(1)

        return carry

    rows_t = slabs * tok
    at_row = lax.broadcasted_iota(jnp.int32, (rows_t, rows_t), 0) & (tok - 1)
    at_col = lax.broadcasted_iota(jnp.int32, (rows_t, rows_t), 1) & (tok - 1)
    same = at_row == at_col

    def temporal(hi):
        queries = qkv[hi, :, :, 0:HEAD_DIM].reshape(rows_t, HEAD_DIM)
        keys = qkv[hi, :, :, HEAD_DIM : 2 * HEAD_DIM].reshape(rows_t, HEAD_DIM)
        values = qkv[hi, :, :, 2 * HEAD_DIM :].reshape(rows_t, HEAD_DIM)
        scores = jnp.where(same, dot_t(queries, keys) * inv_root, -jnp.inf)
        weights = jnp.exp(scores - jnp.max(scores, axis=-1, keepdims=True))
        total = jnp.sum(weights, axis=-1, keepdims=True)
        mixed = jnp.dot(weights.astype(BF16), values, preferred_element_type=F32) / total
        tmp_out[hi] = mixed.reshape(slabs, tok, HEAD_DIM)

    lax.fori_loop(1, half, gather_step, 0)
    temporal(z_hi)
    gather_step(half, 0)
    pass_slab.start()
    sp_in[me] = qkv[:, me]

    mine_late = lax.div(me, 2) == z_lo

    @pl.when(mine_late)
    def _():
        temporal(1 - z_hi)

    part_in = sp_in.at[0 : cols - 1]
    remote(part_in, part_in, aa_send.at[0], aa_recv.at[0], partner).wait_recv()

    is_late = jnp.where(mine_late, 1, 0)

    def back_copy(column, of_slab):
        return remote(
            sp_out.at[column], sp_back.at[:, of_slab], rt_send.at[0], rt_recv.at[is_late],
            here(column),
        )

    batch_s = min(8, cols)
    rows_s = batch_s * 2 * tok

    def spatial_step(step, carry):
        keys = sp_in[:, :, :, HEAD_DIM : 2 * HEAD_DIM].reshape(cols * 2 * tok, HEAD_DIM)
        values = sp_in[:, :, :, 2 * HEAD_DIM :].reshape(cols * 2 * tok, HEAD_DIM)
        queries = sp_in[pl.ds(step * batch_s, batch_s), :, :, 0:HEAD_DIM].reshape(rows_s, HEAD_DIM)
        scores = dot_t(queries, keys) * inv_root
        weights = jnp.exp(scores - jnp.max(scores, axis=-1, keepdims=True))
        total = jnp.sum(weights, axis=-1, keepdims=True)
        mixed = jnp.dot(weights.astype(BF16), values, preferred_element_type=F32) / total
        sp_out[pl.ds(step * batch_s, batch_s)] = mixed.astype(BF16).reshape(batch_s, 2, tok, HEAD_DIM)
        for at in range(batch_s):
            column = step * batch_s + at

            @pl.when(column != me)
            def _():
                back_copy(column, me).start()

        return carry

    lax.fori_loop(0, cols // batch_s, spatial_step, 0)
    sp_back[:, me] = sp_out[me]

    @pl.when(jnp.logical_not(mine_late))
    def _():
        temporal(1 - z_hi)


    def await_back(late, count):
        block = sp_back.at[:, 0:count]
        remote(block, block, rt_send.at[0], rt_recv.at[late], partner).wait_recv()

    def combine(ahead, carry):
        of_slab = lax.rem(2 * z_lo + ahead, slabs)
        both = sp_back[:, of_slab].astype(F32) + tmp_out[:, of_slab]
        comb[:, of_slab] = both.astype(BF16)
        return carry

    @pl.when(mine_late)
    def _():
        await_back(0, slabs - 2)

    @pl.when(jnp.logical_not(mine_late))
    def _():
        await_back(0, slabs - 3)

    lax.fori_loop(2, slabs, combine, 0)

    def fill(dst, plane, piece_at):
        def one(at, carry):
            step = lax.div(at, 2)
            block = jnp.where(lax.rem(at, 2) == 0, 2 * stride - 1 - step, step)
            place = lax.rem(2 * plane + 2 * ring - (stride - 1) + block, 2 * ring)
            from_slab = lax.rem(lax.rem(place, slabs) + slabs - 1, slabs)
            dst[at] = comb[lax.div(place, slabs), from_slab]
            return carry

        lax.fori_loop(4 * piece_at, 4 * piece_at + 4, one, 0)

    def head_copy(step, at):
        plane = mod_ring(z + stride * step)
        slot = lax.div(lax.rem(z_lo - lax.rem(plane, half) + half, half), stride)
        rows = pl.ds(4 * at, 4)
        return remote(
            x_send.at[step, rows], x_recv.at[slot, z_hi, rows],
            xs_send.at[step, at], xs_recv.at[slot, z_hi, at], device(plane, core, me),
        )

    def send_heads(step, at):
        fill(x_send.at[step], mod_ring(z + stride * step), at)
        head_copy(step, at).start()

    far = peers // 2
    for at in range(pieces):
        if at < pieces - 1:
            send_heads(far, at)
        for step in range(1, peers):
            if step != far:
                send_heads(step, at)
    for at in range(pieces - 1):
        fill(x_recv.at[0, z_hi], z, at)

    @pl.when(mine_late)
    def _():
        await_back(1, 1)

    @pl.when(jnp.logical_not(mine_late))
    def _():
        await_back(1, 2)

    lax.fori_loop(0, 2, combine, 0)
    send_heads(far, pieces - 1)
    fill(x_recv.at[0, z_hi], z, pieces - 1)
    local_wo.wait()
    take_wo.wait_recv()
    if pairs > 1:
        pair_wo(other).wait_recv()

    to_pair.wait_send()

    @pl.when(own_head)
    def _():
        whole_w.wait_send()
        give_gq.wait_send()
        give_gk.wait_send()

    give_wo.wait_send()
    pass_slab.wait_send()
    pass_slab.wait_recv()
    for at in range(1, pairs):
        plane_piece(at).wait_send()
    if pairs > 1:
        pair_wo(core).wait_send()

        def drain_spread(ahead, carry):
            spread_piece(lax.rem(me + ahead, cols), me).wait_send()
            return carry

        lax.fori_loop(1, cols, drain_spread, 0)
    sent = tokens.at[0 : 2 * ring - 2]
    remote(sent, sent, ag_send.at[0], ag_recv.at[0, 0, 0, 0], partner).wait_send()
    sent = qkv.at[:, 0 : cols - 1]
    remote(sent, sent, aa_send.at[0], aa_recv.at[0], partner).wait_send()
    sent = sp_out.at[0 : cols - 1]
    remote(sent, sent, rt_send.at[0], rt_recv.at[0], partner).wait_send()

    def await_heads(at):
        for step in range(1, peers):
            plane = mod_ring(z + stride * step)
            slot = lax.div(lax.rem(lax.rem(plane, half) - z_lo + half, half), stride)
            hi = lax.div(plane, half)
            rows = pl.ds(4 * at, 4)
            remote(
                x_send.at[step, rows], x_recv.at[slot, hi, rows],
                xs_send.at[step, at], xs_recv.at[slot, hi, at], device(plane, core, me),
            ).wait_recv()

    def final_core(way, step):
        if step < stride - 3:
            return None
        return (step == stride - 3) != (way == 1) and 1 or 0

    def sum_copy(way, step, at):
        mine, theirs, ends = ((r_send, r_recv, r_last), (l_send, l_recv, l_last))[way]
        span_s = slice(at * sum_span, (at + 1) * sum_span)
        dst = theirs.at[step, :, span_s]
        sem = rs_recv.at[way, step, at]
        target = (right, left)[way]
        to_core = final_core(way, step)
        if to_core is not None:
            dst = ends.at[core, :, span_s]
            sem = last_recv.at[way, core, at]
            target = (right_of, left_of)[way][to_core]
        return remote(mine.at[step, :, span_s], dst, rs_send.at[way, step, at], sem, target)

    sum_span = width // SUM_PARTS
    chunk = width // SUM_PIECES
    rows_x = 4 * tok
    for step in range(stride - 1):
        if step % 2 == 0:
            await_heads(step // 2)
            rows = slice(2 * step, 2 * step + 4)
            heads = jnp.concatenate(
                [x_recv[at // 2, at % 2, rows].reshape(rows_x, HEAD_DIM) for at in range(2 * pairs)],
                axis=1,
            )
        for part_at in range(SUM_PARTS):
            span_s = slice(part_at * sum_span, (part_at + 1) * sum_span)
            if step % 2 == 0:
                for at in range(part_at * sum_span, (part_at + 1) * sum_span, chunk):
                    weights = wo[:, :, :, at : at + chunk].reshape(2 * pairs * HEAD_DIM, chunk)
                    product = jnp.dot(heads, weights, preferred_element_type=F32)
                    part[rows, :, at : at + chunk] = product.reshape(4, tok, chunk)
            for way, mine, theirs in ((0, r_send, r_recv), (1, l_send, l_recv)):
                share = part[step * 2 + way, :, span_s]
                if step >= 2:
                    sum_copy(way, step - 2, part_at).wait_recv()
                    share = share + theirs[step - 2, :, span_s].astype(F32)
                mine[step, :, span_s] = share.astype(BF16)
                sum_copy(way, step, part_at).start()

    fin_send[...] = part[2 * stride - 1 - other].astype(BF16)
    give_fin = remote(fin_send, fin_recv, misc_send.at[1], misc_recv.at[1], partner)
    give_fin.start()

    def drain_sum(step):
        for way in (0, 1):
            for at in range(SUM_PARTS):
                sum_copy(way, step, at).wait_send()

    for step in range(1, peers):
        for at in range(pieces):
            head_copy(step, at).wait_send()
    for step in range(stride - 2):
        drain_sum(step)

    def await_last(way, batch):
        ends = (r_last, l_last)[way]
        for at in range(SUM_PARTS):
            dst = ends.at[batch, :, at * sum_span : (at + 1) * sum_span]
            remote(
                dst, dst, rs_send.at[way, 0, at], last_recv.at[way, batch, at], partner
            ).wait_recv()

    def attend(batch, own_share):
        gate = rows_of[2, 2 + batch]
        if stride > 2:
            for way in (0, 1):
                await_last(way, batch)
            sides = r_last[batch].astype(F32) + l_last[batch].astype(F32)
        else:
            for way in (0, 1):

                @pl.when(core == way)
                def _():
                    await_last(way, batch)

            sides = jnp.where(core == 0, r_last[batch].astype(F32), l_last[batch].astype(F32))
        projection = own_share + sides
        out[batch] = (prev[batch].astype(F32) + gate * projection).astype(BF16)

    attend(core, part[2 * stride - 1 - core])
    give_fin.wait_recv()
    attend(other, fin_recv[...].astype(F32))

    give_fin.wait_send()
    drain_sum(stride - 2)


def body(slab_queue, levels, mod_table, w_qkv, q_gain, k_gain, w_out):
    batch, _, tok, width = slab_queue.shape
    ring = lax.axis_size("tm")
    cols = lax.axis_size("space") // 2
    half = ring // 2
    group = 2 if ring > 4 else 1
    stride = half // group
    vmem = pl.BlockSpec(memory_space=pltpu.VMEM)
    hbm = pl.BlockSpec(memory_space=pltpu.HBM)
    dma = pltpu.SemaphoreType.DMA
    block = (tok, width)
    return pl.pallas_call(
        functools.partial(kernel, ring, cols),
        out_shape=pltpu.VMEM((batch, tok, width), BF16),
        in_specs=[hbm] * 7,
        out_specs=vmem,
        scratch_shapes=[
            pltpu.VMEM((batch,) + block, BF16),
            pltpu.SMEM(levels.shape, jnp.int32),
            pltpu.VMEM((3, mod_table.shape[0], width), BF16),
            pltpu.VMEM((3, 4, 1, width), F32),
            pltpu.VMEM(block, BF16),
            pltpu.VMEM((2 * ring,) + block, BF16),
            pltpu.VMEM((width, 3 * HEAD_DIM), BF16),
            pltpu.VMEM((1, HEAD_DIM), F32),
            pltpu.VMEM((1, HEAD_DIM), F32),
            pltpu.VMEM((group, 2, HEAD_DIM, width), BF16),
            pltpu.VMEM((2, ring, tok, 3 * HEAD_DIM), BF16),
            pltpu.VMEM((cols, 2, tok, 3 * HEAD_DIM), BF16),
            pltpu.VMEM((cols, 2, tok, HEAD_DIM), BF16),
            pltpu.VMEM((2, ring, tok, HEAD_DIM), BF16),
            pltpu.VMEM((2, ring, tok, HEAD_DIM), F32),
            pltpu.VMEM((2, ring, tok, HEAD_DIM), BF16),
            pltpu.VMEM((ring // stride, 2 * stride, tok, HEAD_DIM), BF16),
            pltpu.VMEM((group, 2, 2 * stride, tok, HEAD_DIM), BF16),
            pltpu.VMEM((2 * stride,) + block, F32),
            pltpu.VMEM((stride - 1,) + block, BF16),
            pltpu.VMEM((stride - 1,) + block, BF16),
            pltpu.VMEM((stride - 1,) + block, BF16),
            pltpu.VMEM((stride - 1,) + block, BF16),
            pltpu.VMEM((batch,) + block, BF16),
            pltpu.VMEM((batch,) + block, BF16),
            pltpu.VMEM((batch,) + block, BF16),
            pltpu.VMEM(block, BF16),
            pltpu.VMEM(block, BF16),
            dma((7,)),
            dma((5,)),
            dma((5,)),
            dma((1,)),
            dma((2, half + 1, 2, RING_PARTS)),
            dma((1,)),
            dma((1,)),
            dma((1,)),
            dma((2,)),
            dma((ring // stride, stride // 2)),
            dma((group, 2, stride // 2)),
            dma((2, stride - 1, SUM_PARTS)),
            dma((2, stride - 1, SUM_PARTS)),
            dma((2, batch, SUM_PARTS)),
            dma((2,)),
            dma((2,)),
            dma((1,)),
            dma((1,)),
            dma((group,)),
            dma((group,)),
            dma((cols,)),
            dma((cols,)),
            dma((2,)),
        ],
        compiler_params=pltpu.CompilerParams(
            collective_id=0, has_side_effects=True, vmem_limit_bytes=VMEM_BYTES
        ),
        cost_estimate=pl.CostEstimate(
            flops=4 * 10**9, bytes_accessed=8 * 10**6, transcendentals=4 * 10**5
        ),
    )(
        slab_queue.reshape(batch, tok, width), levels, jnp.swapaxes(mod_table, 0, 1),
        w_qkv.reshape(width, 3 * HEAD_DIM), q_gain, k_gain, w_out,
    ).reshape(batch, 1, tok, width)


def solution(mesh):
    placed = (
        P(None, "tm", "space", None),
        P(),
        P(),
        P(None, "tm", None),
        P("tm", None),
        P("tm", None),
        P("tm", None),
    )
    return jax.shard_map(
        body, mesh=mesh, in_specs=placed, out_specs=P(None, "tm", "space", None), check_vma=False
    )
```

```python
import functools
import math

import jax
import jax.numpy as jnp
from jax import lax
from jax.experimental import pallas as pl
from jax.experimental.pallas import tpu as pltpu
from jax.sharding import PartitionSpec as P

HEAD_DIM = 128
W_PIECES = 12
RING_PARTS = 2
SUM_PIECES = 4
SUM_PARTS = 2
VMEM_BYTES = 63 * 1024 * 1024
MESH = pl.DeviceIdType.MESH
F32 = jnp.float32
BF16 = jnp.bfloat16


def dot_t(left, right):
    return lax.dot_general(left, right, (((1,), (1,)), ((), ())), preferred_element_type=F32)


def head_norm(values, gain):
    values = values.astype(F32)
    factor = lax.rsqrt(jnp.mean(jnp.square(values), axis=-1, keepdims=True) + 1e-06)
    return (values * factor * gain).astype(BF16)


def kernel(
    ring, cols,
    slab_in, levels_in, mod_in, w_qkv, q_gain, k_gain, w_out,
    out,
    slab, levels, mod, rows_of, mod_send, tokens, w_buf, gq, gk, wo, qkv, sp_in, sp_out, sp_back, tmp_out, comb,
    x_send, x_recv, part, r_send, r_recv, l_send, l_recv, r_last, l_last, prev, fin_send, fin_recv,
    loc_sem, pair_send, pair_recv, ag_send, ag_recv, aa_send, aa_recv, rt_send, rt_recv,
    xs_send, xs_recv, rs_send, rs_recv, last_recv, misc_send, misc_recv, w_send, w_recv,
    wz_send, wz_recv, wp_send, wp_recv, wd_sem,
):
    half = ring // 2
    group = 2 if ring > 4 else 1
    stride = half // group
    peers = ring // stride
    pieces = stride // 2
    slabs = ring
    tok, width = slab.shape[1], slab.shape[2]
    piece = width // W_PIECES
    tm, space = lax.axis_index("tm"), lax.axis_index("space")
    core, z_lo = lax.rem(tm, 2), lax.div(tm, 2)
    me, z_hi = lax.div(space, 2), lax.rem(space, 2)
    z = z_hi * half + z_lo
    other = 1 - core
    inv_root = 1.0 / math.sqrt(HEAD_DIM)

    def mod_ring(value):
        return lax.rem(value + ring, ring)

    def device(plane, of_core, column):
        return (lax.rem(plane, half) * 2 + of_core, column * 2 + lax.div(plane, half))

    def here(column):
        return (tm, column * 2 + z_hi)

    right = device(mod_ring(z + 1), core, me)
    left = device(mod_ring(z - 1), core, me)
    partner = (z_lo * 2 + other, space)
    tm_next = (lax.rem(tm + 1, slabs), space)
    tm_far = (lax.rem(tm + jnp.where(core == 1, 1, slabs - 1), slabs), space)

    def remote(src, dst, send_sem, recv_sem, target):
        return pltpu.make_async_remote_copy(
            src_ref=src, dst_ref=dst, send_sem=send_sem, recv_sem=recv_sem,
            device_id=target, device_id_type=MESH,
        )

    own_head = core == z_hi
    fetch_levels = pltpu.make_async_copy(levels_in, levels, loc_sem.at[2])
    fetch_mod = pltpu.make_async_copy(mod_in, mod, loc_sem.at[3])
    fetch_slab = pltpu.make_async_copy(slab_in, slab, loc_sem.at[4])
    local_w = pltpu.make_async_copy(w_qkv, w_buf, loc_sem.at[0])
    local_wo = pltpu.make_async_copy(w_out, wo.at[0, core], loc_sem.at[1])
    local_gq = pltpu.make_async_copy(q_gain, gq, loc_sem.at[5])
    local_gk = pltpu.make_async_copy(k_gain, gk, loc_sem.at[6])
    fetch_levels.start()
    fetch_mod.start()
    fetch_slab.start()

    barrier = pltpu.get_barrier_semaphore()
    right_of = [device(mod_ring(z + 1), at, me) for at in (0, 1)]
    left_of = [device(mod_ring(z - 1), at, me) for at in (0, 1)]
    for target in (*right_of, *left_of, partner, tm_far):
        pl.semaphore_signal(barrier, inc=1, device_id=target, device_id_type=MESH)

    def greet(step, carry):
        column = lax.rem(me + step, cols)
        pl.semaphore_signal(barrier, inc=1, device_id=here(column), device_id_type=MESH)
        return carry

    lax.fori_loop(1, cols, greet, 0)

    def greet_class(step, carry):
        target = device(mod_ring(z + stride * step), core, me)
        pl.semaphore_signal(barrier, inc=1, device_id=target, device_id_type=MESH)
        return carry

    lax.fori_loop(1, peers, greet_class, 0)

    fetch_levels.wait()
    fetch_mod.wait()

    tm_before = lax.rem(tm + slabs - 1, slabs)
    pick_row = lax.broadcasted_iota(jnp.int32, (16, mod.shape[1]), 0)
    pick_col = lax.broadcasted_iota(jnp.int32, (16, mod.shape[1]), 1)
    hot = jnp.zeros((16, mod.shape[1]), F32)
    for at, (batch, of_slab) in enumerate(((0, tm), (1, tm), (0, tm_before), (1, tm_before))):
        hot = jnp.where((pick_row == at) & (pick_col == levels[batch, of_slab]), 1.0, hot)
    for kind in range(3):
        picked = jnp.dot(hot.astype(BF16), mod[kind], preferred_element_type=F32)
        for at in range(4):
            rows_of[kind, at] = picked[at : at + 1]

    def modulate(batch):
        values = slab[batch].astype(F32)
        centre = jnp.mean(values, axis=-1, keepdims=True)
        moved = values - centre
        spread = jnp.mean(jnp.square(moved), axis=-1, keepdims=True)
        normed = moved * lax.rsqrt(spread + 1e-06)
        return (normed * (1.0 + rows_of[1, batch]) + rows_of[0, batch]).astype(BF16)

    fetch_slab.wait()

    @pl.when(own_head)
    def _():
        local_gq.start()
        local_gk.start()
        local_w.start()

    local_wo.start()

    tokens[z * 2 + core] = modulate(core)
    pl.semaphore_wait(barrier, 6 + cols - 1 + peers - 1)

    span = width // RING_PARTS

    def gather_copy(way, step, t, origin, at):
        block = tokens.at[origin * 2 + t, :, at * span : (at + 1) * span]
        return remote(
            block, block, ag_send.at[0], ag_recv.at[way, step, t, at], (right, left)[way]
        )

    def gather_start(t):
        for at in range(RING_PARTS):
            for way in (0, 1):
                gather_copy(way, 1, t, z, at).start()

    gather_start(core)
    mod_send[...] = modulate(other)
    to_pair = remote(mod_send, tokens.at[z * 2 + core], pair_send.at[0], pair_recv.at[0], partner)
    to_pair.start()
    from_pair = remote(mod_send, tokens.at[z * 2 + other], pair_send.at[0], pair_recv.at[0], partner)
    from_pair.wait_recv()
    gather_start(other)

    def give_w(at):
        rows = pl.ds(at * piece, piece)
        return remote(w_qkv.at[rows], w_buf.at[rows], w_send.at[0], w_recv.at[0], partner)

    whole_w = remote(w_qkv, w_buf, w_send.at[0], w_recv.at[0], partner)
    give_gq = remote(q_gain, gq, pair_send.at[2], pair_recv.at[2], partner)
    give_gk = remote(k_gain, gk, pair_send.at[3], pair_recv.at[3], partner)
    give_wo = remote(w_out, wo.at[0, core], pair_send.at[4], pair_recv.at[4], partner)
    take_wo = remote(w_out, wo.at[0, other], pair_send.at[4], pair_recv.at[4], partner)
    pass_slab = remote(slab, prev, misc_send.at[0], misc_recv.at[0], tm_next)

    @pl.when(own_head)
    def _():
        give_gq.start()
        give_gk.start()

    pairs = group
    rows_w = 2 * HEAD_DIM // cols
    cut_rows = pl.ds(pl.multiple_of(lax.div(me, 2) * rows_w, rows_w), rows_w)
    cut_cols = pl.ds(pl.multiple_of(lax.rem(me, 2) * (width // 2), width // 2), width // 2)

    def plane_piece(at):
        apart = stride * at if 2 * stride * at < half else stride * at - half
        if 2 * stride * at == half:
            apart = jnp.where(core == 0, half // 2, -(half // 2))
        return remote(
            w_out.at[cut_rows, cut_cols], wo.at[at, core, cut_rows, cut_cols],
            wz_send.at[at], wz_recv.at[at], device(mod_ring(z - apart), core, me),
        )

    def spread_piece(column, source):
        rows = pl.ds(pl.multiple_of(lax.div(source, 2) * rows_w, rows_w), rows_w)
        span = pl.ds(pl.multiple_of(lax.rem(source, 2) * (width // 2), width // 2), width // 2)
        piece_of = wo.at[1:pairs, core, rows, span]
        return remote(
            piece_of, piece_of, wp_send.at[column], wp_recv.at[source], here(column)
        )

    def pair_wo(of_core):
        block = wo.at[1:pairs, of_core]
        return remote(block, block, wd_sem.at[0], wd_sem.at[1], partner)

    for at in range(1, pairs):
        plane_piece(at).start()

    def slab_copy(hi, column, source):
        return remote(
            qkv.at[hi, column], sp_in.at[source, hi], aa_send.at[0], aa_recv.at[0],
            here(column),
        )

    first_dot = max(1, 3 * half // 8)
    give_steps = max(first_dot - 1, 1)
    per_step = W_PIECES // give_steps

    def reach(at):
        done = jnp.minimum(2 * (at - first_dot + 1), at + 1)
        return jnp.where(at < first_dot, 0, jnp.where(at == half, half + 1, done))

    def gather_step(step, carry):
        step = jnp.asarray(step, jnp.int32)
        plane_a = mod_ring(z - step)
        plane_b = mod_ring(z + step)
        first, last = reach(step - 1), reach(step)
        middle = jnp.where(last - first == 2, first + 1, first)

        def turn_step(turn, inner):
            t = jnp.where(turn == 0, core, other)
            for at in range(RING_PARTS):
                for way, origin in ((0, plane_a), (1, plane_b)):

                    @pl.when((step < half) | (t == way))
                    def _():
                        gather_copy(way, step, t, origin, at).wait_recv()

                    @pl.when((step < half - 1) | ((step == half - 1) & (t == way)))
                    def _():
                        gather_copy(way, step + 1, t, origin, at).start()

            if pairs > 1:

                @pl.when((step == 2) & (turn == 0))
                def _():
                    for at in range(1, pairs):
                        plane_piece(at).wait_recv()

                    def spread(ahead, most):
                        spread_piece(lax.rem(me + ahead, cols), me).start()
                        return most

                    lax.fori_loop(1, cols, spread, 0)

                @pl.when((step == half - 1) & (turn == 0))
                def _():
                    def await_spread(ahead, most):
                        spread_piece(me, lax.rem(me + ahead, cols)).wait_recv()
                        return most

                    lax.fori_loop(1, cols, await_spread, 0)
                    pair_wo(core).start()

            @pl.when(own_head & (step <= give_steps))
            def _():
                def one(at, most):
                    give_w(at).start()
                    return most

                share = per_step // 2
                begin = (2 * (step - 1) + turn) * share
                lax.fori_loop(begin, begin + share, one, 0)

            @pl.when((step == first_dot) & (turn == 0))
            def _():
                give_wo.start()

                @pl.when(own_head)
                def _():
                    local_w.wait()
                    local_gq.wait()
                    local_gk.wait()

                @pl.when(jnp.logical_not(own_head))
                def _():
                    whole_w.wait_recv()
                    give_gq.wait_recv()
                    give_gk.wait_recv()

            lax.fori_loop(
                jnp.where(turn == 0, first, middle), jnp.where(turn == 0, middle, last),
                project_step, 0,
            )
            return inner

        lax.fori_loop(0, 2, turn_step, 0)
        return carry

    def project_step(step, carry):
        planes = (mod_ring(z - step), mod_ring(z + step))
        rows = jnp.concatenate(
            [tokens[pl.ds(plane * 2, 2)].reshape(2 * tok, width) for plane in planes], axis=0
        )
        projected = jnp.dot(rows, w_buf[...], preferred_element_type=F32).astype(BF16)
        queries = head_norm(projected[:, :HEAD_DIM], gq[...])
        keys = head_norm(projected[:, HEAD_DIM : 2 * HEAD_DIM], gk[...])
        values = projected[:, 2 * HEAD_DIM :]
        def place(at):
            hi, lo = lax.div(planes[at], half), lax.rem(planes[at], half)
            for t in (0, 1):
                cut = slice((at * 2 + t) * tok, (at * 2 + t + 1) * tok)
                column = lo * 2 + t
                qkv[hi, column, :, 0:HEAD_DIM] = queries[cut]
                qkv[hi, column, :, HEAD_DIM : 2 * HEAD_DIM] = keys[cut]
                qkv[hi, column, :, 2 * HEAD_DIM :] = values[cut]

                @pl.when(column != me)
                def _():
                    slab_copy(hi, column, me).start()

        place(0)

        @pl.when(lax.rem(step, half) != 0)
        def _():
            place(1)

        return carry

    rows_t = slabs * tok
    at_row = lax.broadcasted_iota(jnp.int32, (rows_t, rows_t), 0) & (tok - 1)
    at_col = lax.broadcasted_iota(jnp.int32, (rows_t, rows_t), 1) & (tok - 1)
    same = at_row == at_col

    def temporal(hi):
        queries = qkv[hi, :, :, 0:HEAD_DIM].reshape(rows_t, HEAD_DIM)
        keys = qkv[hi, :, :, HEAD_DIM : 2 * HEAD_DIM].reshape(rows_t, HEAD_DIM)
        values = qkv[hi, :, :, 2 * HEAD_DIM :].reshape(rows_t, HEAD_DIM)
        scores = jnp.where(same, dot_t(queries, keys) * inv_root, -jnp.inf)
        weights = jnp.exp(scores - jnp.max(scores, axis=-1, keepdims=True))
        total = jnp.sum(weights, axis=-1, keepdims=True)
        mixed = jnp.dot(weights.astype(BF16), values, preferred_element_type=F32) / total
        tmp_out[hi] = mixed.reshape(slabs, tok, HEAD_DIM)

    lax.fori_loop(1, half, gather_step, 0)
    gather_step(half, 0)
    pass_slab.start()
    sp_in[me] = qkv[:, me]

    mine_late = lax.div(me, 2) == z_lo

    @pl.when(mine_late)
    def _():
        temporal(z_hi)
        temporal(1 - z_hi)

    part_in = sp_in.at[0 : cols - 1]
    remote(part_in, part_in, aa_send.at[0], aa_recv.at[0], partner).wait_recv()

    is_late = jnp.where(mine_late, 1, 0)

    def back_copy(column, of_slab):
        return remote(
            sp_out.at[column], sp_back.at[:, of_slab], rt_send.at[0], rt_recv.at[is_late],
            here(column),
        )

    batch_s = min(8, cols)
    rows_s = batch_s * 2 * tok

    def spatial_step(step, carry):
        keys = sp_in[:, :, :, HEAD_DIM : 2 * HEAD_DIM].reshape(cols * 2 * tok, HEAD_DIM)
        values = sp_in[:, :, :, 2 * HEAD_DIM :].reshape(cols * 2 * tok, HEAD_DIM)
        queries = sp_in[pl.ds(step * batch_s, batch_s), :, :, 0:HEAD_DIM].reshape(rows_s, HEAD_DIM)
        scores = dot_t(queries, keys) * inv_root
        weights = jnp.exp(scores - jnp.max(scores, axis=-1, keepdims=True))
        total = jnp.sum(weights, axis=-1, keepdims=True)
        mixed = jnp.dot(weights.astype(BF16), values, preferred_element_type=F32) / total
        sp_out[pl.ds(step * batch_s, batch_s)] = mixed.astype(BF16).reshape(batch_s, 2, tok, HEAD_DIM)
        for at in range(batch_s):
            column = step * batch_s + at

            @pl.when(column != me)
            def _():
                back_copy(column, me).start()

        return carry

    lax.fori_loop(0, cols // batch_s, spatial_step, 0)
    sp_back[:, me] = sp_out[me]

    @pl.when(jnp.logical_not(mine_late))
    def _():
        temporal(z_hi)
        temporal(1 - z_hi)


    def await_back(late, count):
        block = sp_back.at[:, 0:count]
        remote(block, block, rt_send.at[0], rt_recv.at[late], partner).wait_recv()

    def combine(ahead, carry):
        of_slab = lax.rem(2 * z_lo + ahead, slabs)
        both = sp_back[:, of_slab].astype(F32) + tmp_out[:, of_slab]
        comb[:, of_slab] = both.astype(BF16)
        return carry

    @pl.when(mine_late)
    def _():
        await_back(0, slabs - 2)

    @pl.when(jnp.logical_not(mine_late))
    def _():
        await_back(0, slabs - 3)

    lax.fori_loop(2, slabs, combine, 0)

    def fill(dst, plane, piece_at):
        def one(at, carry):
            step = lax.div(at, 2)
            block = jnp.where(lax.rem(at, 2) == 0, 2 * stride - 1 - step, step)
            place = lax.rem(2 * plane + 2 * ring - (stride - 1) + block, 2 * ring)
            from_slab = lax.rem(lax.rem(place, slabs) + slabs - 1, slabs)
            dst[at] = comb[lax.div(place, slabs), from_slab]
            return carry

        lax.fori_loop(4 * piece_at, 4 * piece_at + 4, one, 0)

    def head_copy(step, at):
        plane = mod_ring(z + stride * step)
        slot = lax.div(lax.rem(z_lo - lax.rem(plane, half) + half, half), stride)
        rows = pl.ds(4 * at, 4)
        return remote(
            x_send.at[step, rows], x_recv.at[slot, z_hi, rows],
            xs_send.at[step, at], xs_recv.at[slot, z_hi, at], device(plane, core, me),
        )

    def send_heads(step, at):
        fill(x_send.at[step], mod_ring(z + stride * step), at)
        head_copy(step, at).start()

    far = peers // 2
    for at in range(pieces):
        if at < pieces - 1:
            send_heads(far, at)
        for step in range(1, peers):
            if step != far:
                send_heads(step, at)
    for at in range(pieces - 1):
        fill(x_recv.at[0, z_hi], z, at)

    @pl.when(mine_late)
    def _():
        await_back(1, 1)

    @pl.when(jnp.logical_not(mine_late))
    def _():
        await_back(1, 2)

    lax.fori_loop(0, 2, combine, 0)
    send_heads(far, pieces - 1)
    fill(x_recv.at[0, z_hi], z, pieces - 1)
    local_wo.wait()
    take_wo.wait_recv()
    if pairs > 1:
        pair_wo(other).wait_recv()

    to_pair.wait_send()

    @pl.when(own_head)
    def _():
        whole_w.wait_send()
        give_gq.wait_send()
        give_gk.wait_send()

    give_wo.wait_send()
    pass_slab.wait_send()
    pass_slab.wait_recv()
    for at in range(1, pairs):
        plane_piece(at).wait_send()
    if pairs > 1:
        pair_wo(core).wait_send()

        def drain_spread(ahead, carry):
            spread_piece(lax.rem(me + ahead, cols), me).wait_send()
            return carry

        lax.fori_loop(1, cols, drain_spread, 0)
    sent = tokens.at[0 : 2 * ring - 2]
    remote(sent, sent, ag_send.at[0], ag_recv.at[0, 0, 0, 0], partner).wait_send()
    sent = qkv.at[:, 0 : cols - 1]
    remote(sent, sent, aa_send.at[0], aa_recv.at[0], partner).wait_send()
    sent = sp_out.at[0 : cols - 1]
    remote(sent, sent, rt_send.at[0], rt_recv.at[0], partner).wait_send()

    def await_heads(at):
        for step in range(1, peers):
            plane = mod_ring(z + stride * step)
            slot = lax.div(lax.rem(lax.rem(plane, half) - z_lo + half, half), stride)
            hi = lax.div(plane, half)
            rows = pl.ds(4 * at, 4)
            remote(
                x_send.at[step, rows], x_recv.at[slot, hi, rows],
                xs_send.at[step, at], xs_recv.at[slot, hi, at], device(plane, core, me),
            ).wait_recv()

    def final_core(way, step):
        if step < stride - 3:
            return None
        return (step == stride - 3) != (way == 1) and 1 or 0

    def sum_copy(way, step, at):
        mine, theirs, ends = ((r_send, r_recv, r_last), (l_send, l_recv, l_last))[way]
        span_s = slice(at * sum_span, (at + 1) * sum_span)
        dst = theirs.at[step, :, span_s]
        sem = rs_recv.at[way, step, at]
        target = (right, left)[way]
        to_core = final_core(way, step)
        if to_core is not None:
            dst = ends.at[core, :, span_s]
            sem = last_recv.at[way, core, at]
            target = (right_of, left_of)[way][to_core]
        return remote(mine.at[step, :, span_s], dst, rs_send.at[way, step, at], sem, target)

    sum_span = width // SUM_PARTS
    chunk = width // SUM_PIECES
    rows_x = 4 * tok
    for step in range(stride - 1):
        if step % 2 == 0:
            await_heads(step // 2)
            rows = slice(2 * step, 2 * step + 4)
            heads = jnp.concatenate(
                [x_recv[at // 2, at % 2, rows].reshape(rows_x, HEAD_DIM) for at in range(2 * pairs)],
                axis=1,
            )
        for part_at in range(SUM_PARTS):
            span_s = slice(part_at * sum_span, (part_at + 1) * sum_span)
            if step % 2 == 0:
                for at in range(part_at * sum_span, (part_at + 1) * sum_span, chunk):
                    weights = wo[:, :, :, at : at + chunk].reshape(2 * pairs * HEAD_DIM, chunk)
                    product = jnp.dot(heads, weights, preferred_element_type=F32)
                    part[rows, :, at : at + chunk] = product.reshape(4, tok, chunk)
            for way, mine, theirs in ((0, r_send, r_recv), (1, l_send, l_recv)):
                share = part[step * 2 + way, :, span_s]
                if step >= 2:
                    sum_copy(way, step - 2, part_at).wait_recv()
                    share = share + theirs[step - 2, :, span_s].astype(F32)
                mine[step, :, span_s] = share.astype(BF16)
                sum_copy(way, step, part_at).start()

    fin_send[...] = part[2 * stride - 1 - other].astype(BF16)
    give_fin = remote(fin_send, fin_recv, misc_send.at[1], misc_recv.at[1], partner)
    give_fin.start()

    def drain_sum(step):
        for way in (0, 1):
            for at in range(SUM_PARTS):
                sum_copy(way, step, at).wait_send()

    for step in range(1, peers):
        for at in range(pieces):
            head_copy(step, at).wait_send()
    for step in range(stride - 2):
        drain_sum(step)

    def await_last(way, batch):
        ends = (r_last, l_last)[way]
        for at in range(SUM_PARTS):
            dst = ends.at[batch, :, at * sum_span : (at + 1) * sum_span]
            remote(
                dst, dst, rs_send.at[way, 0, at], last_recv.at[way, batch, at], partner
            ).wait_recv()

    def attend(batch, own_share):
        gate = rows_of[2, 2 + batch]
        if stride > 2:
            for way in (0, 1):
                await_last(way, batch)
            sides = r_last[batch].astype(F32) + l_last[batch].astype(F32)
        else:
            for way in (0, 1):

                @pl.when(core == way)
                def _():
                    await_last(way, batch)

            sides = jnp.where(core == 0, r_last[batch].astype(F32), l_last[batch].astype(F32))
        projection = own_share + sides
        out[batch] = (prev[batch].astype(F32) + gate * projection).astype(BF16)

    attend(core, part[2 * stride - 1 - core])
    give_fin.wait_recv()
    attend(other, fin_recv[...].astype(F32))

    give_fin.wait_send()
    drain_sum(stride - 2)


def body(slab_queue, levels, mod_table, w_qkv, q_gain, k_gain, w_out):
    batch, _, tok, width = slab_queue.shape
    ring = lax.axis_size("tm")
    cols = lax.axis_size("space") // 2
    half = ring // 2
    group = 2 if ring > 4 else 1
    stride = half // group
    vmem = pl.BlockSpec(memory_space=pltpu.VMEM)
    hbm = pl.BlockSpec(memory_space=pltpu.HBM)
    dma = pltpu.SemaphoreType.DMA
    block = (tok, width)
    return pl.pallas_call(
        functools.partial(kernel, ring, cols),
        out_shape=pltpu.VMEM((batch, tok, width), BF16),
        in_specs=[hbm] * 7,
        out_specs=vmem,
        scratch_shapes=[
            pltpu.VMEM((batch,) + block, BF16),
            pltpu.SMEM(levels.shape, jnp.int32),
            pltpu.VMEM((3, mod_table.shape[0], width), BF16),
            pltpu.VMEM((3, 4, 1, width), F32),
            pltpu.VMEM(block, BF16),
            pltpu.VMEM((2 * ring,) + block, BF16),
            pltpu.VMEM((width, 3 * HEAD_DIM), BF16),
            pltpu.VMEM((1, HEAD_DIM), F32),
            pltpu.VMEM((1, HEAD_DIM), F32),
            pltpu.VMEM((group, 2, HEAD_DIM, width), BF16),
            pltpu.VMEM((2, ring, tok, 3 * HEAD_DIM), BF16),
            pltpu.VMEM((cols, 2, tok, 3 * HEAD_DIM), BF16),
            pltpu.VMEM((cols, 2, tok, HEAD_DIM), BF16),
            pltpu.VMEM((2, ring, tok, HEAD_DIM), BF16),
            pltpu.VMEM((2, ring, tok, HEAD_DIM), F32),
            pltpu.VMEM((2, ring, tok, HEAD_DIM), BF16),
            pltpu.VMEM((ring // stride, 2 * stride, tok, HEAD_DIM), BF16),
            pltpu.VMEM((group, 2, 2 * stride, tok, HEAD_DIM), BF16),
            pltpu.VMEM((2 * stride,) + block, F32),
            pltpu.VMEM((stride - 1,) + block, BF16),
            pltpu.VMEM((stride - 1,) + block, BF16),
            pltpu.VMEM((stride - 1,) + block, BF16),
            pltpu.VMEM((stride - 1,) + block, BF16),
            pltpu.VMEM((batch,) + block, BF16),
            pltpu.VMEM((batch,) + block, BF16),
            pltpu.VMEM((batch,) + block, BF16),
            pltpu.VMEM(block, BF16),
            pltpu.VMEM(block, BF16),
            dma((7,)),
            dma((5,)),
            dma((5,)),
            dma((1,)),
            dma((2, half + 1, 2, RING_PARTS)),
            dma((1,)),
            dma((1,)),
            dma((1,)),
            dma((2,)),
            dma((ring // stride, stride // 2)),
            dma((group, 2, stride // 2)),
            dma((2, stride - 1, SUM_PARTS)),
            dma((2, stride - 1, SUM_PARTS)),
            dma((2, batch, SUM_PARTS)),
            dma((2,)),
            dma((2,)),
            dma((1,)),
            dma((1,)),
            dma((group,)),
            dma((group,)),
            dma((cols,)),
            dma((cols,)),
            dma((2,)),
        ],
        compiler_params=pltpu.CompilerParams(
            collective_id=0, has_side_effects=True, vmem_limit_bytes=VMEM_BYTES
        ),
        cost_estimate=pl.CostEstimate(
            flops=4 * 10**9, bytes_accessed=8 * 10**6, transcendentals=4 * 10**5
        ),
    )(
        slab_queue.reshape(batch, tok, width), levels, jnp.swapaxes(mod_table, 0, 1),
        w_qkv.reshape(width, 3 * HEAD_DIM), q_gain, k_gain, w_out,
    ).reshape(batch, 1, tok, width)


def solution(mesh):
    placed = (
        P(None, "tm", "space", None),
        P(),
        P(),
        P(None, "tm", None),
        P("tm", None),
        P("tm", None),
        P("tm", None),
    )
    return jax.shard_map(
        body, mesh=mesh, in_specs=placed, out_specs=P(None, "tm", "space", None), check_vma=False
    )
```
